32 devices in a mesh: seq: 4 (over y, x), fsdp: 8 (over z, core).
Axes of the slice: x: 2, y: 2, z: 4, core: 2. Of those that a mesh axis runs over, the one named last changes fastest.
Arguments:
- tokens: bfloat16 [16, 2048, 768], P('fsdp', 'seq'), may hold values from -6 to 6
- segments: int32 [16, 2048], P('fsdp', 'seq'), may hold values from 0 to 31, never falling along the last dimension, each value on 1 to 1024 neighbouring positions
- qkv_weight: bfloat16 [768, 2304], P(('seq', 'fsdp')), may hold values from -0.21875 to 0.21875
- query_bias: bfloat16 [768], P(('seq', 'fsdp')), may hold values from -3 to 3
- value_bias: bfloat16 [768], P(('seq', 'fsdp')), may hold values from -3 to 3
- proj_weight: bfloat16 [768, 768], P(('seq', 'fsdp')), may hold values from -0.875 to 0.875
- proj_bias: bfloat16 [768], P(('seq', 'fsdp')), may hold values from -2 to 2
- attn_gain: bfloat16 [768], P(('seq', 'fsdp')), may hold values from 0.5 to 1.5
- attn_shift: bfloat16 [768], P(('seq', 'fsdp')), may hold values from -2 to 2
- ffn_gain: bfloat16 [768], P(('seq', 'fsdp')), may hold values from 0.5 to 1.5
- ffn_shift: bfloat16 [768], P(('seq', 'fsdp')), may hold values from -2 to 2
- expand_weight: bfloat16 [768, 3072], P(('seq', 'fsdp')), may hold values from -0.21875 to 0.21875
- expand_bias: bfloat16 [3072], P(('seq', 'fsdp')), may hold values from -3 to 3
- contract_weight: bfloat16 [3072, 768], P(('seq', 'fsdp')), may hold values from -0.109375 to 0.109375
- contract_bias: bfloat16 [768], P(('seq', 'fsdp')), may hold values from -2 to 2
- cotangent: bfloat16 [16, 2048, 768], P('fsdp', 'seq'), may hold values from -6 to 6
Outputs:
- outputs: bfloat16 [16, 2048, 768], P('fsdp', 'seq')
- token_grad: bfloat16 [16, 2048, 768], P('fsdp', 'seq')
- qkv_weight_grad: float32 [768, 2304], P(('seq', 'fsdp'))
- query_bias_grad: float32 [768], P(('seq', 'fsdp'))
- value_bias_grad: float32 [768], P(('seq', 'fsdp'))
- proj_weight_grad: float32 [768, 768], P(('seq', 'fsdp'))
- proj_bias_grad: float32 [768], P(('seq', 'fsdp'))
- attn_gain_grad: float32 [768], P(('seq', 'fsdp'))
- attn_shift_grad: float32 [768], P(('seq', 'fsdp'))
- ffn_gain_grad: float32 [768], P(('seq', 'fsdp'))
- ffn_shift_grad: float32 [768], P(('seq', 'fsdp'))
- expand_weight_grad: float32 [768, 3072], P(('seq', 'fsdp'))
- expand_bias_grad: float32 [3072], P(('seq', 'fsdp'))
- contract_weight_grad: float32 [3072, 768], P(('seq', 'fsdp'))
- contract_bias_grad: float32 [768], P(('seq', 'fsdp'))
The draws below stay inside these ranges and needn't reach their ends.
Inputs may be any that keep to these rules, and one draw needn't show every extreme that they name: `segments`: within each packed sequence the document number never falls; every document holds 1 to 1024 tokens and one holds exactly 1024.
All inputs are finite; a program needn't handle non-finite values.
Results may differ from the reference program's by a relative error of at most 0.011.
Values may be sent and summed in bfloat16 or wider, within the bound.
No kernel may reach another device: no remote copies, remote signals or barrier semaphores. Data moves between devices by JAX's collectives and lax.ppermute only.
A program may use at most 192 MiB of HBM per device.

```python
import math
import jax
import jax.numpy as jnp
import numpy as np
from jax import lax

D = 768
HEADS = 12
HD = 64
FF = 3072
SEQ = 2048
SEQS = 16
DOCS = 32
MOST_DOC = 1024


def levels(rng, dims, split, smallest, largest):
    gain = 1.0
    for axis_at, parts in split:
        steps = jax.random.uniform(jax.random.fold_in(jax.random.fold_in(rng, 6), axis_at), (parts,), jnp.float32, smallest / len(split), largest / len(split))
        gain = gain * jnp.repeat(jnp.exp(steps), dims[axis_at] // parts).reshape((-1,) + (1,) * (len(dims) - 1 - axis_at))
    return gain


def split_up(count, total, limit, slope):
    portions = [(1 << 20) // math.isqrt(rank ** slope) + 1 for rank in range(2, count + 1)]
    rest, holding = total - limit - (count - 1), [1] * (count - 1)
    while rest > 0:
        candidates = [i for i in range(count - 1) if holding[i] < limit]
        pool, remaining = sum([portions[i] for i in candidates]), rest
        for i in candidates:
            addition = min(limit - holding[i], max(1, remaining * portions[i] // pool), rest)
            holding[i] = holding[i] + addition
            rest = rest - addition
    return np.array([limit] + holding)


def ragged(stream_key, amount, total, bound, lean):
    if amount == 2:
        one = jax.random.randint(stream_key, (), max(1, total - bound), min(bound, total - 1) + 1)
        return jnp.stack([one, total - one])
    tallies = jnp.asarray(split_up(amount, total, bound, lean), jnp.int32)
    couples = (amount - 1) // 2
    donor, receiver = tallies[1:1 + 2 * couples:2], tallies[2:2 + 2 * couples:2]
    margin = jnp.minimum(donor - 1, bound - receiver)
    passed = jax.random.randint(jax.random.fold_in(stream_key, 1), (couples,), 0, 1 << 20) % (margin + 1)
    tallies = tallies.at[1:1 + 2 * couples:2].set(donor - passed).at[2:2 + 2 * couples:2].set(receiver + passed)
    return tallies[jax.random.permutation(jax.random.fold_in(stream_key, 2), amount)]


def centred(own_key, dims, deviation, reach, split=(), held_as=jnp.bfloat16):
    gain = levels(own_key, dims, split, -0.22, 0.18) if split else 1.0
    values = jax.random.normal(own_key, dims, jnp.float32) * deviation * gain
    return jnp.minimum(jnp.maximum(values, -reach), reach).astype(held_as)


def setup_inputs(seed: int = 0) -> dict:
    splits = jax.random.split(jax.random.key(seed), 17)
    return {
        "tokens": centred(splits[0], (SEQS, SEQ, D), 1.0, 6.0, ((0, 8), (1, 4))),
        "segments": jax.vmap(lambda own: jnp.searchsorted(jnp.cumsum(ragged(own, DOCS, SEQ, MOST_DOC, 2)), jnp.arange(SEQ), side="right"))(jax.random.split(splits[1], SEQS)).reshape((SEQS, SEQ)).astype(jnp.int32),
        "qkv_weight": centred(splits[2], (D, 3 * D), D ** -0.5, 0.21875, ((0, 32),)),
        "query_bias": centred(splits[3], (D,), 0.5, 3.0, ((0, 32),)),
        "value_bias": centred(splits[4], (D,), 0.5, 3.0, ((0, 32),)),
        "proj_weight": centred(splits[5], (D, D), (D // 16) ** -0.5, 0.875, ((0, 32),)),
        "proj_bias": centred(splits[6], (D,), 0.3, 2.0, ((0, 32),)),
        "attn_gain": jnp.clip(1.0 + 0.1 * jax.random.normal(splits[7], (D,), jnp.float32), 0.5, 1.5).astype(jnp.bfloat16),
        "attn_shift": centred(splits[8], (D,), 0.3, 2.0, ((0, 32),)),
        "ffn_gain": jnp.clip(1.0 + 0.1 * jax.random.normal(splits[9], (D,), jnp.float32), 0.5, 1.5).astype(jnp.bfloat16),
        "ffn_shift": centred(splits[10], (D,), 0.3, 2.0, ((0, 32),)),
        "expand_weight": centred(splits[11], (D, FF), D ** -0.5, 0.21875, ((0, 32),)),
        "expand_bias": centred(splits[12], (FF,), 0.5, 3.0, ((0, 32),)),
        "contract_weight": centred(splits[13], (FF, D), FF ** -0.5, 0.109375, ((0, 32),)),
        "contract_bias": centred(splits[14], (D,), 0.3, 2.0, ((0, 32),)),
        "cotangent": centred(splits[15], (SEQS, SEQ, D), 1.0, 6.0, ((0, 8), (1, 4))),
    }


@jax.custom_vjp
def low(v):
    return lax.optimization_barrier(v.astype(jnp.bfloat16)).astype(jnp.float32)

@jax.custom_vjp
def low_back(v):
    return v

def low_keep(v):
    return (low(v), None)

def low_pass(kept, grad):
    return (grad,)

def back_keep(v):
    return (v, None)

def back_low(kept, grad):
    return (low(grad),)
low.defvjp(low_keep, low_pass)
low_back.defvjp(back_keep, back_low)
NORM_EPS = 1e-05
MASKED_SCORE = -1e+30
PRECISE = lax.Precision.HIGHEST

def norm_rows(values_in, norm_gain, norm_shift):
    row_mean = lax.optimization_barrier(jnp.mean(values_in, axis=-1, keepdims=True))
    centered = values_in - row_mean
    row_var = lax.optimization_barrier(jnp.mean(centered * centered, axis=-1, keepdims=True))
    return centered * lax.rsqrt(row_var + NORM_EPS) * norm_gain + norm_shift

def gelu_tanh(values_in):
    return 0.5 * values_in * (1.0 + jnp.tanh(0.7978845608028654 * (values_in + 0.044715 * values_in * values_in * values_in)))

def both_round(values_in):
    return low(low_back(values_in))

def one_sequence(params, token_rows, segment_row):
    qkv_matrix, query_offset, value_offset, proj_matrix, proj_offset, attn_scale, attn_offset, ffn_scale, ffn_offset, expand_matrix, expand_offset, contract_matrix, contract_offset = params
    length = token_rows.shape[0]
    normed_one = low(norm_rows(token_rows, attn_scale, attn_offset))
    mixed_rows = jnp.dot(normed_one, qkv_matrix, precision=PRECISE)
    query_rows = both_round(mixed_rows[:, :D] + query_offset).reshape(length, HEADS, HD)
    key_rows = both_round(mixed_rows[:, D:2 * D]).reshape(length, HEADS, HD)
    value_rows = both_round(mixed_rows[:, 2 * D:] + value_offset).reshape(length, HEADS, HD)
    scores = jnp.einsum('qhd,khd->hqk', query_rows, key_rows, precision=PRECISE) * (1.0 / math.sqrt(HD))
    scores = low_back(scores)
    positions = jnp.arange(length, dtype=jnp.int32)
    allowed = (positions[:, None] >= positions[None, :]) & (segment_row[:, None] == segment_row[None, :])
    scores = jnp.where(allowed[None], scores, MASKED_SCORE)
    probs_low = low(jax.nn.softmax(scores, axis=-1))
    attended = jnp.einsum('hqk,khd->qhd', probs_low, value_rows, precision=PRECISE)
    attended = both_round(attended).reshape(length, D)
    branch = low_back(jnp.dot(attended, proj_matrix, precision=PRECISE) + proj_offset)
    middle = token_rows + branch
    normed_two = low(norm_rows(middle, ffn_scale, ffn_offset))
    hidden = low_back(jnp.dot(normed_two, expand_matrix, precision=PRECISE) + expand_offset)
    active = low(gelu_tanh(hidden))
    output_rows = low_back(jnp.dot(active, contract_matrix, precision=PRECISE) + contract_offset)
    return middle + output_rows

def reference(tokens, segments, qkv_weight, query_bias, value_bias, proj_weight, proj_bias, attn_gain, attn_shift, ffn_gain, ffn_shift, expand_weight, expand_bias, contract_weight, contract_bias, cotangent):
    params = (qkv_weight.astype(jnp.float32), query_bias.astype(jnp.float32), value_bias.astype(jnp.float32), proj_weight.astype(jnp.float32), proj_bias.astype(jnp.float32), attn_gain.astype(jnp.float32), attn_shift.astype(jnp.float32), ffn_gain.astype(jnp.float32), ffn_shift.astype(jnp.float32), expand_weight.astype(jnp.float32), expand_bias.astype(jnp.float32), contract_weight.astype(jnp.float32), contract_bias.astype(jnp.float32))
    inputs = tokens.astype(jnp.float32)

    def forward(param_set, input_set):

        def per_sequence(pair):
            return one_sequence(param_set, pair[0], pair[1])
        return lax.map(jax.checkpoint(per_sequence), (input_set, segments))
    outputs, pullback = jax.vjp(forward, params, inputs)
    grads, input_grad = pullback(cotangent.astype(jnp.float32))
    return (outputs.astype(jnp.bfloat16), input_grad.astype(jnp.bfloat16), grads[0], grads[1], grads[2], grads[3], grads[4], grads[5], grads[6], grads[7], grads[8], grads[9], grads[10], grads[11], grads[12])
```

```python
import functools

import jax
import jax.numpy as jnp
from jax import lax
from jax.experimental import pallas as pl
from jax.experimental.pallas import tpu as pltpu
from jax.sharding import PartitionSpec as P

HD = 64
NORM_EPS = 1e-05
NEG = -1e30
B = 256
MOST_DOC = 1024
ALL = ("seq", "fsdp")
BF = jnp.bfloat16
F32 = jnp.float32
NT = (((1,), (1,)), ((), ()))
NN = (((1,), (0,)), ((), ()))
TN = (((0,), (0,)), ((), ()))


def dg(a, b, dims):
    return lax.dot_general(a, b, dims, preferred_element_type=F32)


def fwd_kernel(lo_ref, start_ref, q_ref, k_ref, v_ref, o_ref, lse_ref, qm, vt, sbuf, mx8, *, heads):
    n = q_ref.shape[0] // B
    lane = lax.broadcasted_iota(jnp.int32, (B, 128), 1)
    kio = lax.broadcasted_iota(jnp.int32, (B, B), 0)
    qio = lax.broadcasted_iota(jnp.int32, (B, B), 1)

    def transpose_block(j, _):
        s = pl.ds(pl.multiple_of(j * B, B), B)
        for p in range(heads // 2):
            vt[128 * p : 128 * p + 128, s] = v_ref[s, 128 * p : 128 * p + 128].T
        return 0

    lax.fori_loop(0, n, transpose_block, 0)

    def qblock(i, _):
        qs = pl.multiple_of(i * B, B)
        for p in range(heads // 2):
            qq = q_ref[pl.ds(qs, B), 128 * p : 128 * p + 128]
            qm[2 * p] = jnp.where(lane < 64, qq, jnp.zeros_like(qq))
            qm[2 * p + 1] = jnp.where(lane >= 64, qq, jnp.zeros_like(qq))
        st_row = start_ref[pl.ds(i, 1), :]

        def scores(j, first):
            ks = pl.multiple_of(j * B, B)
            mask = (kio + ks) >= st_row
            if first:
                mask = mask & (kio <= qio)
            slot = i - j
            for h in range(heads):
                p = h // 2
                k_blk = k_ref[pl.ds(ks, B), 128 * p : 128 * p + 128]
                st = jnp.where(mask, dg(k_blk, qm[h], NT), NEG)
                sbuf[h, slot] = st
                m8 = jnp.max(st.reshape(B // 8, 8, B), axis=0)
                mx8[h] = m8 if first else jnp.maximum(mx8[h], m8)

        scores(i, True)

        def score_step(j, c):
            scores(j, False)
            return c

        lax.fori_loop(lo_ref[i], i, score_step, 0)
        ms = [jnp.max(mx8[h], axis=0, keepdims=True) for h in range(heads)]

        def weigh(j):
            ks = pl.multiple_of(j * B, B)
            slot = i - j
            outs = []
            for h in range(heads):
                p = jnp.exp(sbuf[h, slot] - ms[h])
                l8 = jnp.sum(p.reshape(B // 8, 8, B), axis=0)
                ot = dg(vt[64 * h : 64 * h + 64, pl.ds(ks, B)], p.astype(BF), NN)
                outs.append((ot, l8))
            return outs

        def weigh_step(j, c):
            return [(a[0] + b[0], a[1] + b[1]) for a, b in zip(c, weigh(j))]

        res = lax.fori_loop(lo_ref[i], i, weigh_step, weigh(i))
        for p in range(heads // 2):
            rows = []
            for h in (2 * p, 2 * p + 1):
                total = jnp.sum(res[h][1], axis=0, keepdims=True)
                rows.append(res[h][0] * (1.0 / total))
                lse_ref[h : h + 1, pl.ds(qs, B)] = ms[h] + jnp.log(total)
            pair = jnp.concatenate(rows, axis=0)
            o_ref[pl.ds(qs, B), 128 * p : 128 * p + 128] = pair.T.astype(BF)
        return 0

    lax.fori_loop(0, n, qblock, 0)


def attn_fwd(lo, start, q, k, v):
    n, w = q.shape
    heads = w // HD
    maxb = min(n // B, (MOST_DOC + B - 2) // B + 1)
    return pl.pallas_call(
        functools.partial(fwd_kernel, heads=heads),
        out_shape=(jax.ShapeDtypeStruct((n, w), BF), jax.ShapeDtypeStruct((8, n), F32)),
        in_specs=[pl.BlockSpec(memory_space=pltpu.SMEM)]
        + [pl.BlockSpec(memory_space=pltpu.VMEM)] * 4,
        out_specs=[pl.BlockSpec(memory_space=pltpu.VMEM)] * 2,
        scratch_shapes=[
            pltpu.VMEM((heads, B, 128), BF),
            pltpu.VMEM((w, n), BF),
            pltpu.VMEM((heads, maxb, B, B), F32),
            pltpu.VMEM((heads, 8, B), F32),
        ],
        compiler_params=pltpu.CompilerParams(vmem_limit_bytes=32 * 2**20),
        cost_estimate=pl.CostEstimate(
            flops=20_000_000_000, bytes_accessed=6_000_000, transcendentals=0
        ),
        name="attn_fwd",
    )(lo, start, q, k, v)


def bwd_kernel(
    lo_ref, start_ref, q_ref, k_ref, v_ref, do_ref, o_ref, lse_ref,
    dq_ref, dk_ref, dv_ref, qm, dm, dqa, dka, dva, dd, kt, *, heads,
):
    n = q_ref.shape[0] // B
    lane = lax.broadcasted_iota(jnp.int32, (B, 128), 1)
    kio = lax.broadcasted_iota(jnp.int32, (B, B), 0)
    qio = lax.broadcasted_iota(jnp.int32, (B, B), 1)
    dka[...] = jnp.zeros_like(dka)
    dva[...] = jnp.zeros_like(dva)

    def transpose_block(j, _):
        s = pl.ds(pl.multiple_of(j * B, B), B)
        for p in range(heads // 2):
            kt[128 * p : 128 * p + 128, s] = k_ref[s, 128 * p : 128 * p + 128].T
        return 0

    lax.fori_loop(0, n, transpose_block, 0)

    def qblock(i, _):
        qs = pl.multiple_of(i * B, B)
        for p in range(heads // 2):
            cs = slice(128 * p, 128 * p + 128)
            qq = q_ref[pl.ds(qs, B), cs]
            gg = do_ref[pl.ds(qs, B), cs]
            prod = (o_ref[pl.ds(qs, B), cs].astype(F32) * gg.astype(F32)).T
            dd[2 * p : 2 * p + 1, :] = jnp.sum(prod[:64], axis=0, keepdims=True)
            dd[2 * p + 1 : 2 * p + 2, :] = jnp.sum(prod[64:], axis=0, keepdims=True)
            z = jnp.zeros_like(qq)
            qm[2 * p] = jnp.where(lane < 64, qq, z)
            qm[2 * p + 1] = jnp.where(lane >= 64, qq, z)
            dm[2 * p] = jnp.where(lane < 64, gg, z)
            dm[2 * p + 1] = jnp.where(lane >= 64, gg, z)
        st_row = start_ref[pl.ds(i, 1), :]

        def block(j, first):
            ks = pl.multiple_of(j * B, B)
            mask = (kio + ks) >= st_row
            if first:
                mask = mask & (kio <= qio)
            for p in range(heads // 2):
                cs = slice(128 * p, 128 * p + 128)
                k_blk = k_ref[pl.ds(ks, B), cs]
                v_blk = v_ref[pl.ds(ks, B), cs]
                dvs, dks, dqs = [], [], []
                for h in (2 * p, 2 * p + 1):
                    st = dg(k_blk, qm[h], NT)
                    lse = lse_ref[h : h + 1, pl.ds(qs, B)]
                    pt = jnp.exp(jnp.where(mask, st, NEG) - lse)
                    dp = dg(v_blk, dm[h], NT)
                    ds = pt * (dp - dd[h : h + 1, :])
                    pb = pt.astype(BF)
                    db = ds.astype(BF)
                    dvs.append(dg(pb, dm[h], NN))
                    dks.append(dg(db, qm[h], NN))
                    dqs.append(dg(kt[64 * h : 64 * h + 64, pl.ds(ks, B)], db, NN))
                dva[pl.ds(ks, B), cs] += dvs[0] + dvs[1]
                dka[pl.ds(ks, B), cs] += dks[0] + dks[1]
                dq = jnp.concatenate(dqs, axis=0)
                if first:
                    dqa[cs, :] = dq
                else:
                    dqa[cs, :] += dq

        block(i, True)

        def step(j, c):
            block(j, False)
            return c

        lax.fori_loop(lo_ref[i], i, step, 0)
        for p in range(heads // 2):
            cs = slice(128 * p, 128 * p + 128)
            dq_ref[pl.ds(qs, B), cs] = (dqa[cs, :] * 0.125).T.astype(BF)
        return 0

    lax.fori_loop(0, n, qblock, 0)

    def finish(i, _):
        s = pl.ds(pl.multiple_of(i * B, B), B)
        dk_ref[s, :] = dka[s, :].astype(BF)
        dv_ref[s, :] = dva[s, :].astype(BF)
        return 0

    lax.fori_loop(0, n, finish, 0)


def attn_bwd(lo, start, q, k, v, do, o, lse):
    n, w = q.shape
    heads = w // HD
    s = jax.ShapeDtypeStruct((n, w), BF)
    return pl.pallas_call(
        functools.partial(bwd_kernel, heads=heads),
        out_shape=(s, s, s),
        in_specs=[pl.BlockSpec(memory_space=pltpu.SMEM)]
        + [pl.BlockSpec(memory_space=pltpu.VMEM)] * 7,
        out_specs=[pl.BlockSpec(memory_space=pltpu.VMEM)] * 3,
        scratch_shapes=[
            pltpu.VMEM((heads, B, 128), BF),
            pltpu.VMEM((heads, B, 128), BF),
            pltpu.VMEM((w, B), F32),
            pltpu.VMEM((n, w), F32),
            pltpu.VMEM((n, w), F32),
            pltpu.VMEM((8, B), F32),
            pltpu.VMEM((w, n), BF),
        ],
        compiler_params=pltpu.CompilerParams(vmem_limit_bytes=40 * 2**20),
        cost_estimate=pl.CostEstimate(
            flops=44_000_000_000, bytes_accessed=12_000_000, transcendentals=0
        ),
        name="attn_bwd",
    )(lo, start, q, k, v, do, o, lse)


def pick(array, index, axis=0):
    return lax.dynamic_index_in_dim(array, index, axis, keepdims=False)


def ordered(flag, first, second, axis):
    return jnp.stack(
        [jnp.where(flag == 1, second, first), jnp.where(flag == 1, first, second)], axis
    )


class Net:
    def __init__(self):
        self.nq = lax.axis_size("seq")
        self.nf = lax.axis_size("fsdp")
        self.q = lax.axis_index("seq")
        f = lax.axis_index("fsdp")
        self.z = f // 2
        self.c = f % 2
        self.bits = (self.nf // 2).bit_length() - 1

    def permute(self, value, target):
        pairs = []
        for q in range(self.nq):
            for f in range(self.nf):
                tq, tf = target(q, f)
                pairs.append((q * self.nf + f, tq * self.nf + tf))
        return lax.ppermute(value, ALL, pairs)

    def flip_q(self, value, mask):
        return self.permute(value, lambda q, f: (q ^ mask, f))

    def flip_f(self, value, mask):
        return self.permute(value, lambda q, f: (q, f ^ mask))

    def swap(self, value):
        return self.flip_f(value, 1)

    def _token_target(self, p):
        return lambda q, f: (2 * (f % 2) + (p ^ (q % 2)), (f // 2) * 2 + q // 2)

    def to_chip(self, parts):
        h = self.q % 2
        got = [
            self.permute(jnp.where(h == p, parts[0], parts[1]), self._token_target(p))
            for p in range(2)
        ]
        return jnp.where(h == 0, got[0], got[1]), jnp.where(h == 0, got[1], got[0])

    def from_chip(self, halves):
        h = self.q % 2
        got = []
        for p in range(2):
            forward = self._token_target(p)
            back = {}
            for q in range(self.nq):
                for f in range(self.nf):
                    back[forward(q, f)] = (q, f)
            got.append(
                self.permute(
                    jnp.where(h == p, halves[0], halves[1]), lambda q, f, b=back: b[(q, f)]
                )
            )
        return jnp.stack([jnp.where(h == 0, got[0], got[1]), jnp.where(h == 0, got[1], got[0])])

    def gather_z(self, block):
        out = block[None]
        shape = block.shape
        for level in range(self.bits):
            bit = self.bits - 1 - level
            got = self.flip_f(out, 2 << bit)
            out = ordered((self.z >> bit) & 1, out, got, 1).reshape((-1,) + shape)
        return out

    def scatter_z(self, blocks):
        shape = blocks.shape[1:]
        for bit in range(self.bits):
            parts = blocks.reshape((-1, 2) + shape)
            mine = (self.z >> bit) & 1
            got = self.flip_f(pick(parts, 1 - mine, 1).astype(BF), 2 << bit)
            blocks = pick(parts, mine, 1).astype(F32) + got.astype(F32)
        return blocks[0]

    def gather_q(self, block):
        half = block.shape[0] // 2
        one = self.flip_q(block, 1)
        two = self.flip_q(block, 2)
        three = jnp.concatenate([self.flip_q(one[:half], 2), self.flip_q(two[half:], 1)])
        return [block, one, two, three]

    def absolute(self, blocks):
        shape = blocks[0].shape
        out = jnp.zeros((4,) + shape, blocks[0].dtype)
        for r, block in enumerate(blocks):
            out = lax.dynamic_update_slice(out, block[None], (self.q ^ r,) + (0,) * len(shape))
        return out

    def scatter_q(self, blocks):
        half = blocks.shape[1] // 2
        b1, b2, b3 = (pick(blocks, self.q ^ r).astype(F32) for r in (1, 2, 3))
        far_a = self.flip_q(b3[:half].astype(BF), 2)
        far_b = self.flip_q(b3[half:].astype(BF), 1)
        b1 = jnp.concatenate([b1[:half] + far_a.astype(F32), b1[half:]])
        b2 = jnp.concatenate([b2[:half], b2[half:] + far_b.astype(F32)])
        one = self.flip_q(b1.astype(BF), 1)
        two = self.flip_q(b2.astype(BF), 2)
        return pick(blocks, self.q).astype(F32) + one.astype(F32) + two.astype(F32)


def row_stats(v):
    mean = jnp.mean(v, axis=-1, keepdims=True)
    centered = v - mean
    var = jnp.mean(centered * centered, axis=-1, keepdims=True)
    inv = lax.rsqrt(var + NORM_EPS)
    return centered * inv, inv


def norm_back(xhat, inv, gain, e):
    c = e * gain
    return inv * (
        c
        - jnp.mean(c, axis=-1, keepdims=True)
        - xhat * jnp.mean(c * xhat, axis=-1, keepdims=True)
    )


def body(
    tokens,
    segments,
    qkv_weight,
    query_bias,
    value_bias,
    proj_weight,
    proj_bias,
    attn_gain,
    attn_shift,
    ffn_gain,
    ffn_shift,
    expand_weight,
    expand_bias,
    contract_weight,
    contract_bias,
    cotangent,
):
    net = Net()
    c, z = net.c, net.z
    micro, local, width = tokens.shape
    rows = qkv_weight.shape[0]
    ff = expand_weight.shape[1]
    ff_rows = contract_weight.shape[0]
    ratio = ff // width
    half = width // 2
    nq, nz = net.nq, net.nf // 2
    blk = rows * net.nf
    n = 2 * micro * local
    mine = micro * local

    lanes = width
    seg_rows = jnp.zeros((micro, 8, lanes), BF).at[:, 0, :local].set(segments.astype(BF))
    tok_send = jnp.concatenate([tokens, seg_rows], axis=1)
    t0, t1 = net.to_chip([tok_send[0], tok_send[1]])
    tok = jnp.concatenate([t0[:local], t1[:local]])
    seg_mine = jnp.concatenate([t0[local, :local], t1[local, :local]])

    small = jnp.concatenate(
        [
            query_bias,
            value_bias,
            proj_bias,
            attn_gain,
            attn_shift,
            ffn_gain,
            ffn_shift,
            contract_bias,
            expand_bias,
        ]
    )
    small_len = small.shape[0]
    pad_rows = -(-(3 * rows + 1) // 8) * 8 - 3 * rows
    small_rows = jnp.zeros((pad_rows * half,), BF).at[:small_len].set(small).reshape(pad_rows, half)
    qkv_cut = qkv_weight.reshape(rows, 3, 2, half)
    packs = jnp.stack(
        [
            jnp.concatenate([qkv_cut[:, 0, s], qkv_cut[:, 1, s], qkv_cut[:, 2, s], small_rows])
            for s in range(2)
        ]
    )
    got = net.swap(pick(packs, 1 - c))
    pack = ordered(c, pick(packs, c), got, 0)
    pack = net.gather_z(pack)
    pack = pack.reshape(net.nf * (3 * rows + pad_rows), half)
    pack = net.absolute(net.gather_q(pack)).reshape(nq, net.nf, 3 * rows + pad_rows, half)
    w_qkv = jnp.concatenate(
        [pack[:, :, s * rows : (s + 1) * rows].reshape(width, half) for s in range(3)], axis=1
    )
    vectors = pack[:, :, 3 * rows :].reshape(nq, net.nf, -1)[:, :, :small_len].astype(F32)
    names = []
    for s in range(8):
        names.append(vectors[:, :, s * rows : (s + 1) * rows].reshape(width))
    q_off, v_off, proj_off, a_gain, a_shift, f_gain, f_shift, con_off = names
    exp_off = vectors[:, :, 8 * rows :].reshape(ff)

    proj_cut = proj_weight.reshape(rows, 2, half)
    con_cut = contract_weight.reshape(ff_rows, 2, half)
    exp_cut = expand_weight.reshape(rows, 2, ratio, half)
    packs2 = jnp.stack(
        [
            jnp.concatenate(
                [con_cut[:, s], proj_cut[:, s]] + [exp_cut[:, s, t] for t in range(ratio)]
            )
            for s in range(2)
        ]
    )
    got2 = net.swap(pick(packs2, 1 - c))
    pack2 = ordered(c, pick(packs2, c), got2, 0)
    pack2 = net.gather_z(pack2).reshape(net.nf, -1, half)
    cuts = [ff_rows, ff_rows + rows]
    pieces2 = [pack2[:, : cuts[0]].reshape(-1, half), pack2[:, cuts[0] : cuts[1]].reshape(-1, half)]
    for t in range(ratio):
        pieces2.append(pack2[:, cuts[1] + t * rows : cuts[1] + (t + 1) * rows].reshape(-1, half))
    pack2 = jnp.concatenate(pieces2)
    quarters = net.gather_q(pack2)
    others = [net.swap(x) for x in quarters]
    own_half = net.absolute(quarters)
    other_half = net.absolute(others)
    w_left = jnp.where(c == 0, own_half, other_half)
    w_right = jnp.where(c == 0, other_half, own_half)
    n_con, n_proj = ratio * blk, blk
    w_con = jnp.concatenate(
        [w_left[:, :n_con].reshape(ff, half), w_right[:, :n_con].reshape(ff, half)], axis=1
    )
    w_proj = jnp.concatenate(
        [
            w_left[:, n_con : n_con + n_proj].reshape(width, half),
            w_right[:, n_con : n_con + n_proj].reshape(width, half),
        ],
        axis=1,
    )
    w_exp = jnp.concatenate(
        [
            x[:, n_con + n_proj + t * blk : n_con + n_proj + (t + 1) * blk].reshape(width, half)
            for x in (w_left, w_right)
            for t in range(ratio)
        ],
        axis=1,
    )

    tok32 = tok.astype(F32)
    xhat_one, inv_one = row_stats(tok32)
    normed = (xhat_one * a_gain + a_shift).astype(BF)
    seg_row = jnp.zeros((16, width), BF).at[:2, :local].set(seg_mine.reshape(2, local))
    both = ordered(c, jnp.concatenate([normed, seg_row]), net.swap(jnp.concatenate([normed, seg_row])), 0)
    normed_all = both[:, :mine].reshape(n, width)
    seg = both[:, mine : mine + 2, :local].reshape(n).astype(jnp.int32)
    docs = jnp.arange(32, dtype=jnp.int32)
    before = jnp.sum((seg[None, :] < docs[:, None]).astype(jnp.int32), axis=1)
    start = jnp.sum(jnp.where(seg[None, :] == docs[:, None], before[:, None], 0), axis=0)
    lo = start[::B] // B
    start = start.reshape(n // B, B)
    mixed = dg(normed_all, w_qkv, NN)
    q_half = pick(q_off.reshape(2, half), c)
    v_half = pick(v_off.reshape(2, half), c)
    query = (mixed[:, :half] + q_half).astype(BF) * BF(0.125)
    key = mixed[:, half : 2 * half].astype(BF)
    value = (mixed[:, 2 * half :] + v_half).astype(BF)
    att, lse = attn_fwd(lo, start, query, key, value)

    att_cut = att.reshape(2, mine, half)
    att_own, att_got = pick(att_cut, c), net.swap(pick(att_cut, 1 - c))
    attended = jnp.concatenate(
        [jnp.where(c == 0, att_own, att_got), jnp.where(c == 0, att_got, att_own)], axis=1
    )
    middle = tok32 + (dg(attended, w_proj, NN) + proj_off)
    xhat_two, inv_two = row_stats(middle)
    normed_two = (xhat_two * f_gain + f_shift).astype(BF)
    hidden = dg(normed_two, w_exp, NN) + exp_off
    inner = 0.7978845608028654 * (hidden + 0.044715 * hidden * hidden * hidden)
    th = jnp.tanh(inner)
    active = (0.5 * hidden * (1.0 + th)).astype(BF)
    slope = 0.5 * (1.0 + th) + 0.5 * hidden * (1.0 - th * th) * (
        0.7978845608028654 * (1.0 + 3 * 0.044715 * hidden * hidden)
    )
    out = (middle + (dg(active, w_con, NN) + con_off)).astype(BF)
    result = net.from_chip([out[:local], out[local:]])

    g0, g1 = net.to_chip([cotangent[0], cotangent[1]])
    g = jnp.concatenate([g0, g1])
    g32 = g.astype(F32)
    con_off_grad = jnp.sum(g32, axis=0)
    con_grad = dg(active, g, TN)
    hidden_grad = (dg(g, w_con, NT) * slope).astype(BF)
    exp_off_grad = jnp.sum(hidden_grad.astype(F32), axis=0)
    exp_grad = dg(normed_two, hidden_grad, TN)
    e_two = dg(hidden_grad, w_exp, NT)
    f_gain_grad = jnp.sum(e_two * xhat_two, axis=0)
    f_shift_grad = jnp.sum(e_two, axis=0)
    middle_grad = g32 + norm_back(xhat_two, inv_two, f_gain, e_two)
    branch = middle_grad.astype(BF)
    proj_off_grad = jnp.sum(branch.astype(F32), axis=0)
    proj_grad = dg(attended, branch, TN)
    att_grad = dg(branch, w_proj, NT).astype(BF)
    ag_cut = att_grad.reshape(mine, 2, half)
    ag_own, ag_got = pick(ag_cut, c, 1), net.swap(pick(ag_cut, 1 - c, 1))
    grad_heads = ordered(c, ag_own, ag_got, 0).reshape(n, half)

    con_g = con_grad.reshape(nq, n_con, 2, half)
    proj_g = proj_grad.reshape(nq, n_proj, 2, half)
    exp_g = exp_grad.reshape(nq, blk, 2, ratio, half)

    def half_pack(s):
        return jnp.concatenate(
            [pick(con_g, s, 2), pick(proj_g, s, 2)]
            + [pick(exp_g, s, 2)[:, :, t] for t in range(ratio)],
            axis=1,
        )

    summed = half_pack(c) + net.swap(half_pack(1 - c).astype(BF)).astype(F32)
    summed = net.scatter_q(summed)
    per_f = jnp.concatenate(
        [
            summed[:n_con].reshape(net.nf, ff_rows, half),
            summed[n_con : n_con + n_proj].reshape(net.nf, rows, half),
        ]
        + [
            summed[n_con + n_proj + t * blk : n_con + n_proj + (t + 1) * blk].reshape(
                net.nf, rows, half
            )
            for t in range(ratio)
        ],
        axis=1,
    )
    per_core = net.scatter_z(per_f.reshape(nz, 2, -1, half))
    kept = pick(per_core, c)
    final = ordered(c, kept, net.swap(pick(per_core, 1 - c)), 0)
    con_out = jnp.concatenate([final[0, :ff_rows], final[1, :ff_rows]], axis=1)
    proj_out = jnp.concatenate([final[0, ff_rows : ff_rows + rows], final[1, ff_rows : ff_rows + rows]], axis=1)
    exp_out = jnp.concatenate(
        [
            final[s, ff_rows + rows + t * rows : ff_rows + rows + (t + 1) * rows]
            for s in range(2)
            for t in range(ratio)
        ],
        axis=1,
    )

    dq, dk, dv = attn_bwd(lo, start, query, key, value, grad_heads, att, lse)
    d_mixed = jnp.concatenate([dq, dk, dv], axis=1)
    q_off_half = jnp.sum(dq.astype(F32), axis=0)
    v_off_half = jnp.sum(dv.astype(F32), axis=0)
    qkv_grad = dg(normed_all, d_mixed, TN)
    e_part = dg(d_mixed, w_qkv, NT).reshape(2, mine, width)
    e_one = pick(e_part, c) + net.swap(pick(e_part, 1 - c).astype(BF)).astype(F32)
    a_gain_grad = jnp.sum(e_one * xhat_one, axis=0)
    a_shift_grad = jnp.sum(e_one, axis=0)
    tok_grad = (middle_grad + norm_back(xhat_one, inv_one, a_gain, e_one)).astype(BF)
    token_grad = net.from_chip([tok_grad[:local], tok_grad[local:]])

    qkv_g = jnp.concatenate(
        [qkv_grad[:, s * half : (s + 1) * half].reshape(nq, blk, half) for s in range(3)], axis=1
    )
    qkv_sum = net.scatter_q(qkv_g).reshape(3, net.nf, rows, half).transpose(1, 0, 2, 3)
    qkv_core = net.scatter_z(qkv_sum.reshape(nz, 2, 3 * rows, half))
    qkv_final = ordered(c, pick(qkv_core, c), net.swap(pick(qkv_core, 1 - c)), 0)
    qkv_out = jnp.concatenate(
        [qkv_final[s, t * rows : (t + 1) * rows] for t in range(3) for s in range(2)], axis=1
    )

    zero = jnp.zeros((half,), F32)
    q_off_grad = jnp.where(c == 0, jnp.concatenate([q_off_half, zero]), jnp.concatenate([zero, q_off_half]))
    v_off_grad = jnp.where(c == 0, jnp.concatenate([v_off_half, zero]), jnp.concatenate([zero, v_off_half]))
    parts = [
        x.reshape(nq, net.nf, -1)
        for x in (
            q_off_grad,
            v_off_grad,
            proj_off_grad,
            a_gain_grad,
            a_shift_grad,
            f_gain_grad,
            f_shift_grad,
            con_off_grad,
            exp_off_grad,
        )
    ]
    vec = jnp.concatenate(parts, axis=2)
    for bit in range(2):
        b = (net.q >> bit) & 1
        pairs = vec.reshape(-1, 2, net.nf, small_len)
        vec = pick(pairs, b, 1) + net.flip_q(pick(pairs, 1 - b, 1), 1 << bit)
    vec = vec[0]
    f = 2 * z + c
    for bit in range(net.bits + 1):
        b = (f >> bit) & 1
        pairs = vec.reshape(-1, 2, small_len)
        vec = pick(pairs, b, 1) + net.flip_f(pick(pairs, 1 - b, 1), 1 << bit)
    vec = vec[0]
    outs = [vec[s * rows : (s + 1) * rows] for s in range(8)]
    exp_off_out = vec[8 * rows :]
    return (
        result,
        token_grad,
        qkv_out,
        outs[0],
        outs[1],
        proj_out,
        outs[2],
        outs[3],
        outs[4],
        outs[5],
        outs[6],
        exp_out,
        exp_off_out,
        con_out,
        outs[7],
    )


def solution(mesh):
    act = P("fsdp", "seq", None)
    mat = P(ALL, None)
    vec = P(ALL)
    return jax.shard_map(
        body,
        mesh=mesh,
        in_specs=(
            act, P("fsdp", "seq"), mat, vec, vec, mat, vec, vec, vec, vec, vec, mat, vec, mat, vec, act,
        ),
        out_specs=(act, act, mat, vec, vec, mat, vec, vec, vec, vec, vec, mat, vec, mat, vec),
        check_vma=False,
    )
```

```python
import functools

import jax
import jax.numpy as jnp
from jax import lax
from jax.experimental import pallas as pl
from jax.experimental.pallas import tpu as pltpu
from jax.sharding import PartitionSpec as P

HD = 64
NORM_EPS = 1e-05
NEG = -1e30
B = 256
MOST_DOC = 1024
ALL = ("seq", "fsdp")
BF = jnp.bfloat16
F32 = jnp.float32
NT = (((1,), (1,)), ((), ()))
NN = (((1,), (0,)), ((), ()))
TN = (((0,), (0,)), ((), ()))
TILE = 256
SEG_ROWS = 16
COST = 1.0
ANY = pl.BlockSpec(memory_space=pl.ANY)
VM = pl.BlockSpec(memory_space=pltpu.VMEM)
SM = pl.BlockSpec(memory_space=pltpu.SMEM)


def dg(a, b, dims):
    return lax.dot_general(a, b, dims, preferred_element_type=F32)


def cost(flops):
    return pl.CostEstimate(flops=int(flops * COST), bytes_accessed=1_000_000, transcendentals=0)


def norm_tile(v):
    mean = jnp.mean(v, axis=-1, keepdims=True)
    centered = v - mean
    var = jnp.mean(centered * centered, axis=-1, keepdims=True)
    inv = lax.rsqrt(var + NORM_EPS)
    return centered * inv, inv


def fwd_kernel(lo_ref, start_ref, q_ref, k_ref, v_ref, *refs, heads):
    o_ref, lse_ref, qm, vt, sbuf, mx8 = refs[-6:]
    n = q_ref.shape[0] // B
    lane = lax.broadcasted_iota(jnp.int32, (B, 128), 1)
    kio = lax.broadcasted_iota(jnp.int32, (B, B), 0)
    qio = lax.broadcasted_iota(jnp.int32, (B, B), 1)

    def transpose_block(j, _):
        s = pl.ds(pl.multiple_of(j * B, B), B)
        for p in range(heads // 2):
            vt[128 * p : 128 * p + 128, s] = v_ref[s, 128 * p : 128 * p + 128].T
        return 0

    lax.fori_loop(0, n, transpose_block, 0)

    def qblock(i, _):
        qs = pl.multiple_of(i * B, B)
        for p in range(heads // 2):
            qq = q_ref[pl.ds(qs, B), 128 * p : 128 * p + 128]
            qm[2 * p] = jnp.where(lane < 64, qq, jnp.zeros_like(qq))
            qm[2 * p + 1] = jnp.where(lane >= 64, qq, jnp.zeros_like(qq))
        st_row = start_ref[pl.ds(i, 1), :]

        def scores(j, first):
            ks = pl.multiple_of(j * B, B)
            mask = (kio + ks) >= st_row
            if first:
                mask = mask & (kio <= qio)
            slot = i - j
            for h in range(heads):
                p = h // 2
                k_blk = k_ref[pl.ds(ks, B), 128 * p : 128 * p + 128]
                st = jnp.where(mask, dg(k_blk, qm[h], NT), NEG)
                sbuf[h, slot] = st
                m8 = jnp.max(st.reshape(B // 8, 8, B), axis=0)
                mx8[h] = m8 if first else jnp.maximum(mx8[h], m8)

        scores(i, True)

        def score_step(j, c):
            scores(j, False)
            return c

        lax.fori_loop(lo_ref[i], i, score_step, 0)
        ms = [jnp.max(mx8[h], axis=0, keepdims=True) for h in range(heads)]

        def weigh(j):
            ks = pl.multiple_of(j * B, B)
            slot = i - j
            outs = []
            for h in range(heads):
                p = jnp.exp(sbuf[h, slot] - ms[h])
                l8 = jnp.sum(p.reshape(B // 8, 8, B), axis=0)
                ot = dg(vt[64 * h : 64 * h + 64, pl.ds(ks, B)], p.astype(BF), NN)
                outs.append((ot, l8))
            return outs

        def weigh_step(j, c):
            return [(a[0] + b[0], a[1] + b[1]) for a, b in zip(c, weigh(j))]

        res = lax.fori_loop(lo_ref[i], i, weigh_step, weigh(i))
        for p in range(heads // 2):
            rows = []
            for h in (2 * p, 2 * p + 1):
                total = jnp.sum(res[h][1], axis=0, keepdims=True)
                rows.append(res[h][0] * (1.0 / total))
                lse_ref[h : h + 1, pl.ds(qs, B)] = ms[h] + jnp.log(total)
            pair = jnp.concatenate(rows, axis=0)
            o_ref[pl.ds(qs, B), 128 * p : 128 * p + 128] = pair.T.astype(BF)
        return 0

    lax.fori_loop(0, n, qblock, 0)


def attn_fwd(lo, start, q, k, v, deps):
    n, w = q.shape
    heads = w // HD
    maxb = min(n // B, (MOST_DOC + B - 2) // B + 1)
    return pl.pallas_call(
        functools.partial(fwd_kernel, heads=heads),
        out_shape=(jax.ShapeDtypeStruct((n, w), BF), jax.ShapeDtypeStruct((8, n), F32)),
        in_specs=[SM] + [VM] * 4 + [ANY] * len(deps),
        out_specs=[VM] * 2,
        scratch_shapes=[
            pltpu.VMEM((heads, B, 128), BF),
            pltpu.VMEM((w, n), BF),
            pltpu.VMEM((heads, maxb, B, B), F32),
            pltpu.VMEM((heads, 8, B), F32),
        ],
        compiler_params=pltpu.CompilerParams(vmem_limit_bytes=32 * 2**20),
        cost_estimate=cost(20_000_000_000),
        name="attn_fwd",
    )(lo, start, q, k, v, *deps)


def bwd_kernel(
    place, lo_ref, start_ref, q_ref, k_ref, v_ref, o_ref, lse_ref, own_ref, got_ref, *refs, heads,
):
    out_ref, qm, dm, dqa, dka, dva, dd, kt = refs[-8:]
    n = q_ref.shape[0] // B
    wide = heads * HD
    c = place[1]
    lane = lax.broadcasted_iota(jnp.int32, (B, 128), 1)
    kio = lax.broadcasted_iota(jnp.int32, (B, B), 0)
    qio = lax.broadcasted_iota(jnp.int32, (B, B), 1)
    dka[...] = jnp.zeros_like(dka)
    dva[...] = jnp.zeros_like(dva)

    def transpose_block(j, _):
        s = pl.ds(pl.multiple_of(j * B, B), B)
        for p in range(heads // 2):
            kt[128 * p : 128 * p + 128, s] = k_ref[s, 128 * p : 128 * p + 128].T
        return 0

    lax.fori_loop(0, n, transpose_block, 0)

    def qblock(i, _):
        qs = pl.multiple_of(i * B, B)
        for p in range(heads // 2):
            cs = slice(128 * p, 128 * p + 128)
            qq = q_ref[pl.ds(qs, B), cs]
            gs = pl.ds(pl.multiple_of((i % (n // 2)) * B, B), B)
            gg = jnp.where(i // (n // 2) == c, own_ref[gs, cs], got_ref[gs, cs])
            prod = (o_ref[pl.ds(qs, B), cs].astype(F32) * gg.astype(F32)).T
            dd[2 * p : 2 * p + 1, :] = jnp.sum(prod[:64], axis=0, keepdims=True)
            dd[2 * p + 1 : 2 * p + 2, :] = jnp.sum(prod[64:], axis=0, keepdims=True)
            z = jnp.zeros_like(qq)
            qm[2 * p] = jnp.where(lane < 64, qq, z)
            qm[2 * p + 1] = jnp.where(lane >= 64, qq, z)
            dm[2 * p] = jnp.where(lane < 64, gg, z)
            dm[2 * p + 1] = jnp.where(lane >= 64, gg, z)
        st_row = start_ref[pl.ds(i, 1), :]

        def block(j, first):
            ks = pl.multiple_of(j * B, B)
            mask = (kio + ks) >= st_row
            if first:
                mask = mask & (kio <= qio)
            for p in range(heads // 2):
                cs = slice(128 * p, 128 * p + 128)
                k_blk = k_ref[pl.ds(ks, B), cs]
                v_blk = v_ref[pl.ds(ks, B), cs]
                dvs, dks, dqs = [], [], []
                for h in (2 * p, 2 * p + 1):
                    st = dg(k_blk, qm[h], NT)
                    lse = lse_ref[h : h + 1, pl.ds(qs, B)]
                    pt = jnp.exp(jnp.where(mask, st, NEG) - lse)
                    dp = dg(v_blk, dm[h], NT)
                    ds = pt * (dp - dd[h : h + 1, :])
                    pb = pt.astype(BF)
                    db = ds.astype(BF)
                    dvs.append(dg(pb, dm[h], NN))
                    dks.append(dg(db, qm[h], NN))
                    dqs.append(dg(kt[64 * h : 64 * h + 64, pl.ds(ks, B)], db, NN))
                dva[pl.ds(ks, B), cs] += dvs[0] + dvs[1]
                dka[pl.ds(ks, B), cs] += dks[0] + dks[1]
                dq = jnp.concatenate(dqs, axis=0)
                if first:
                    dqa[cs, :] = dq
                else:
                    dqa[cs, :] += dq

        block(i, True)

        def step(j, c):
            block(j, False)
            return c

        lax.fori_loop(lo_ref[i], i, step, 0)
        for p in range(heads // 2):
            cs = slice(128 * p, 128 * p + 128)
            out_ref[pl.ds(qs, B), cs] = (dqa[cs, :] * 0.125).T.astype(BF)
        return 0

    lax.fori_loop(0, n, qblock, 0)

    def finish(i, _):
        s = pl.ds(pl.multiple_of(i * B, B), B)
        out_ref[s, wide : 2 * wide] = dka[s, :].astype(BF)
        out_ref[s, 2 * wide :] = dva[s, :].astype(BF)
        return 0

    lax.fori_loop(0, n, finish, 0)


def attn_bwd(place, lo, start, q, k, v, o, lse, own, got, deps):
    n, w = q.shape
    heads = w // HD
    return pl.pallas_call(
        functools.partial(bwd_kernel, heads=heads),
        out_shape=jax.ShapeDtypeStruct((n, 3 * w), BF),
        in_specs=[SM] * 2 + [VM] * 8 + [ANY] * len(deps),
        out_specs=VM,
        scratch_shapes=[
            pltpu.VMEM((heads, B, 128), BF),
            pltpu.VMEM((heads, B, 128), BF),
            pltpu.VMEM((w, B), F32),
            pltpu.VMEM((n, w), F32),
            pltpu.VMEM((n, w), F32),
            pltpu.VMEM((8, B), F32),
            pltpu.VMEM((w, n), BF),
        ],
        compiler_params=pltpu.CompilerParams(vmem_limit_bytes=58 * 2**20),
        cost_estimate=cost(42_000_000_000),
        name="attn_bwd",
    )(place, lo, start, q, k, v, o, lse, own, got, *deps)


def qkv_kernel(place, w0, w1, w2, w3a, w3b, own, far, vecs, bias, *refs):
    normed, q_ref, k_ref, v_ref, w, sems = refs[-6:]
    q, c = place[0], place[1]
    blk = w.shape[0] // 4
    half = w.shape[1] // 3
    copies = []

    def add(src, rows, r, offset, part):
        start = pl.multiple_of((q ^ r) * blk + offset, 16)
        size = rows.stop - rows.start
        copies.append(
            pltpu.make_async_copy(
                src.at[rows],
                w.at[pl.ds(start, size), part * half : part * half + half],
                sems.at[len(copies)],
            )
        )

    for r, src in enumerate((w0, w1, w2)):
        for part in range(3):
            add(src, slice(part * blk, part * blk + blk), r, 0, part)
    cut = blk // 2
    add(w3a, slice(0, blk), 3, 0, 0)
    add(w3a, slice(blk, blk + cut), 3, 0, 1)
    add(w3b, slice(0, cut), 3, cut, 1)
    add(w3b, slice(cut, cut + blk), 3, 0, 2)
    for copy in copies:
        copy.start()
    for copy in copies:
        copy.wait()
    count = q_ref.shape[0] // 2
    per = count // TILE // 2

    for k, ref in enumerate((own, far)):
        base = (c if k == 0 else 1 - c) * count

        def tile(m, _, ref=ref, base=base):
            x = ref[m // per, pl.ds(pl.multiple_of((m % per) * TILE, TILE), TILE), :].astype(F32)
            xhat, _inv = norm_tile(x)
            y = (xhat * vecs[0:1, :] + vecs[1:2, :]).astype(BF)
            s = pl.ds(pl.multiple_of(base + m * TILE, TILE), TILE)
            normed[s, :] = y
            mixed = dg(y, w[...], NN) + bias[...]
            q_ref[s, :] = mixed[:, :half].astype(BF) * BF(0.125)
            k_ref[s, :] = mixed[:, half : 2 * half].astype(BF)
            v_ref[s, :] = mixed[:, 2 * half :].astype(BF)
            return 0

        lax.fori_loop(0, 2 * per, tile, 0)


def qkv_apply(place, weights, own, far, vecs, bias, deps):
    width = own.shape[2]
    half = width // 2
    n = 4 * (own.shape[1] - SEG_ROWS)
    part = jax.ShapeDtypeStruct((n, half), BF)
    return pl.pallas_call(
        qkv_kernel,
        out_shape=(
            jax.ShapeDtypeStruct((n, width), BF),
            part,
            part,
            part,
            jax.ShapeDtypeStruct((width, 3 * half), BF),
        ),
        in_specs=[SM] + [ANY] * 5 + [VM] * 4 + [ANY] * len(deps),
        out_specs=[VM] * 5,
        scratch_shapes=[pltpu.SemaphoreType.DMA((13,))],
        compiler_params=pltpu.CompilerParams(vmem_limit_bytes=32 * 2**20),
        cost_estimate=cost(400_000_000),
        name="qkv",
    )(place, *weights, own, far, vecs, bias, *deps)


GELU_A = 0.7978845608028654
GELU_B = 0.7978845608028654 * 0.044715


PIECES = 10


def load_parts(place, pieces, att_refs, w_con, w_exp, w_proj, att, sems):
    q, c = place[0], place[1]
    half = w_proj.shape[1] // 2
    blk = w_proj.shape[0] // 4
    n_con = w_con.shape[0] // 4
    top = n_con + blk

    def start(core):
        for r in range(4):
            src_q = q ^ r
            for k in range(2):
                side = core if k == 0 else 1 - core
                lanes = slice(side * half, side * half + half)
                a_ref = pieces[5 * k + r]
                b_ref, b_at = (a_ref, top) if r < 3 else (pieces[5 * k + 4], 0)
                rows = pl.ds(pl.multiple_of(src_q * blk, blk), blk)
                pltpu.make_async_copy(
                    a_ref.at[n_con:top], w_proj.at[rows, lanes], sems.at[0]
                ).start()
                for b in range(w_exp.shape[0]):
                    pltpu.make_async_copy(
                        b_ref.at[b_at + b * blk : b_at + b * blk + blk],
                        w_exp.at[b, rows, lanes],
                        sems.at[2],
                    ).start()
                pltpu.make_async_copy(
                    a_ref.at[0:n_con],
                    w_con.at[pl.ds(pl.multiple_of(src_q * n_con, n_con), n_con), lanes],
                    sems.at[3],
                ).start()
        count = att.shape[0]
        for k in range(2):
            side = core if k == 0 else 1 - core
            src = att_refs[0].at[core * count : core * count + count] if k == 0 else att_refs[1]
            pltpu.make_async_copy(
                src, att.at[:, side * half : side * half + half], sems.at[1]
            ).start()

    for core in range(2):
        pl.when(c == core)(functools.partial(start, core))


def wait_for(ref, sem):
    pltpu.make_async_copy(ref, ref, sem).wait()


def ffn_fwd_kernel(place, *refs):
    pieces, att_refs, rest = refs[:PIECES], refs[PIECES : PIECES + 2], refs[PIECES + 2 :]
    tok, vecs = rest[:2]
    out, mid, n2, w_con, w_exp, w_proj, att, acc, sems = refs[-9:]
    load_parts(place, pieces, att_refs, w_con, w_exp, w_proj, att, sems)
    wide = w_proj.shape[0]
    tiles = out.shape[0] // TILE
    per = tiles // 2
    wait_for(w_proj, sems.at[0])
    wait_for(att, sems.at[1])

    def first(m, _):
        s = pl.ds(pl.multiple_of(m * TILE, TILE), TILE)
        x = tok[m // per, pl.ds(pl.multiple_of((m % per) * TILE, TILE), TILE), :]
        v = x.astype(F32) + (dg(att[s, :], w_proj[...], NN) + vecs[0:1, :])
        mid[s, :] = v
        xhat, _inv = norm_tile(v)
        n2[s, :] = (xhat * vecs[1:2, :] + vecs[2:3, :]).astype(BF)
        return 0

    lax.fori_loop(0, tiles, first, 0)
    wait_for(w_exp, sems.at[2])
    wait_for(w_con, sems.at[3])

    def second(m, _):
        s = pl.ds(pl.multiple_of(m * TILE, TILE), TILE)
        x = n2[s, :]
        for b in range(w_exp.shape[0]):
            h = dg(x, w_exp[b], NN) + vecs[8 + b : 9 + b, :]
            th = jnp.tanh(h * (GELU_A + GELU_B * (h * h)))
            act = (h * (0.5 + 0.5 * th)).astype(BF)
            part = dg(act, w_con[b * wide : b * wide + wide, :], NN)
            if b == 0:
                acc[...] = part
            else:
                acc[...] += part
        out[s, :] = (mid[s, :] + (acc[...] + vecs[3:4, :])).astype(BF)
        return 0

    lax.fori_loop(0, tiles, second, 0)


def ffn_bwd_kernel(place, *refs):
    pieces, att_refs, rest = refs[:PIECES], refs[PIECES : PIECES + 2], refs[PIECES + 2 :]
    g, mid, n2, vecs = rest[:4]
    (
        keep, send, mgrad, ag_own, ag_send, sums,
        w_con, w_exp, w_proj, att, n2t, act, hg, n2g, dc, de, agr, sems, osems,
    ) = refs[-19:]
    c = place[1]
    load_parts(place, pieces, att_refs, w_con, w_exp, w_proj, att, sems)
    wide = w_proj.shape[0]
    half = wide // 2
    blk = wide // 4
    blocks = w_exp.shape[0]
    tiles = g.shape[0] // TILE
    sums[...] = jnp.zeros_like(sums)

    def flip(m, _):
        s = pl.ds(pl.multiple_of(m * TILE, TILE), TILE)
        n2t[:, s] = n2[s, :].T
        return 0

    lax.fori_loop(0, tiles, flip, 0)
    wait_for(w_exp, sems.at[2])
    wait_for(w_con, sems.at[3])

    def store(k, b, core):
        side = core if k % 2 == 0 else 1 - core
        lanes = slice(side * half, side * half + half)
        if k < 2:
            src, dst = dc.at[:, lanes], (keep, send)[k].at[b, 0:wide]
        else:
            rows = pl.ds(pl.multiple_of(wide + blk + b * blk, blk), blk)
            src, dst = de.at[:, :, lanes], (keep, send)[k - 2].at[:, rows]
        return pltpu.make_async_copy(src, dst, osems.at[k])

    def each(b, which, action):
        for core in range(2):

            @pl.when(c == core)
            def _():
                for k in which:
                    getattr(store(k, b, core), action)()

    def block(b, _):
        con_rows = pl.ds(pl.multiple_of(b * wide, wide), wide)
        bias = vecs[pl.ds(8 + b, 1), :]

        def tile(m, _):
            s = pl.ds(pl.multiple_of(m * TILE, TILE), TILE)
            w_e = w_exp[b]
            h = dg(n2[s, :], w_e, NN) + bias
            h2 = h * h
            t1 = 0.5 + 0.5 * jnp.tanh(h * (GELU_A + GELU_B * h2))
            ac = h * t1
            act[s, :] = ac.astype(BF)
            slope = t1 + ac * (1.0 - t1) * (2 * GELU_A + 6 * GELU_B * h2)
            hid = (dg(g[s, :], w_con[con_rows, :], NT) * slope).astype(BF)
            hg[s, :] = hid
            sums[pl.ds(8 + b, 1), :] += jnp.sum(hid.astype(F32), axis=0, keepdims=True)
            part = dg(hid, w_e, NT)
            n2g[s, :] = jnp.where(b == 0, part, n2g[s, :] + part)
            return 0

        lax.fori_loop(0, tiles, tile, 0)

        @pl.when(b > 0)
        def _():
            each(b - 1, range(4), "wait")

        for t in range(3):
            cols = slice(t * 256, t * 256 + 256)
            dc[:, cols] = dg(act[...], g[:, cols], TN).astype(BF)
        each(b, (0, 1), "start")
        for t in range(3):
            cols = slice(t * 256, t * 256 + 256)
            de[:, :, cols] = dg(n2t[...], hg[:, cols], NN).astype(BF).reshape(4, blk, 256)
        each(b, (2, 3), "start")
        return 0

    lax.fori_loop(0, blocks, block, 0)
    wait_for(w_proj, sems.at[0])
    wait_for(att, sems.at[1])

    def last(m, _):
        s = pl.ds(pl.multiple_of(m * TILE, TILE), TILE)
        xhat, inv = norm_tile(mid[s, :])
        e = n2g[s, :]
        g32 = g[s, :].astype(F32)
        ce = e * vecs[1:2, :]
        mg = g32 + inv * (
            ce
            - jnp.mean(ce, axis=-1, keepdims=True)
            - xhat * jnp.mean(ce * xhat, axis=-1, keepdims=True)
        )
        mgrad[s, :] = mg
        branch = mg.astype(BF)
        hg[s, :] = branch
        sums[0:1, :] += jnp.sum(branch.astype(F32), axis=0, keepdims=True)
        sums[1:2, :] += jnp.sum(e * xhat, axis=0, keepdims=True)
        sums[2:3, :] += jnp.sum(e, axis=0, keepdims=True)
        sums[3:4, :] += jnp.sum(g32, axis=0, keepdims=True)
        agr[s, :] = dg(branch, w_proj[...], NT).astype(BF)
        return 0

    lax.fori_loop(0, tiles, last, 0)
    each(blocks - 1, range(4), "wait")

    def tail(core, action):
        own = slice(core * half, core * half + half)
        far = slice((1 - core) * half, (2 - core) * half)
        for copy in (
            pltpu.make_async_copy(agr.at[:, own], ag_own, osems.at[0]),
            pltpu.make_async_copy(agr.at[:, far], ag_send, osems.at[1]),
        ):
            getattr(copy, action)()

    def tail2(core, action):
        own = slice(core * half, core * half + half)
        far = slice((1 - core) * half, (2 - core) * half)
        for copy in (
            pltpu.make_async_copy(de.at[:, :, own], keep.at[:, wide : wide + blk], osems.at[2]),
            pltpu.make_async_copy(de.at[:, :, far], send.at[:, wide : wide + blk], osems.at[3]),
        ):
            getattr(copy, action)()

    for core in range(2):
        pl.when(c == core)(functools.partial(tail, core, "start"))
    for t in range(3):
        cols = slice(t * 256, t * 256 + 256)
        de[:, :, cols] = dg(att[...], hg[:, cols], TN).astype(BF).reshape(4, blk, 256)
    for core in range(2):

        @pl.when(c == core)
        def _(core=core):
            tail2(core, "start")
            tail(core, "wait")
            tail2(core, "wait")


def ffn_fwd(place, pieces, atts, tok, vecs, deps):
    n, w = atts[1].shape[0], tok.shape[2]
    ff = 4 * pieces[4].shape[0]
    return pl.pallas_call(
        ffn_fwd_kernel,
        out_shape=(
            jax.ShapeDtypeStruct((n, w), BF),
            jax.ShapeDtypeStruct((n, w), F32),
            jax.ShapeDtypeStruct((n, w), BF),
        ),
        in_specs=[SM] + [ANY] * (PIECES + 2) + [VM] * 2 + [ANY] * len(deps),
        out_specs=[VM] * 3,
        scratch_shapes=[
            pltpu.VMEM((ff, w), BF),
            pltpu.VMEM((ff // w, w, w), BF),
            pltpu.VMEM((w, w), BF),
            pltpu.VMEM((n, w), BF),
            pltpu.VMEM((TILE, w), F32),
            pltpu.SemaphoreType.DMA((4,)),
        ],
        compiler_params=pltpu.CompilerParams(vmem_limit_bytes=54 * 2**20),
        cost_estimate=cost(12_000_000_000),
        name="ffn_fwd",
    )(place, *pieces, *atts, tok, vecs, *deps)


def ffn_bwd(place, pieces, atts, g, mid, n2, vecs, deps):
    n, w = g.shape
    half = w // 2
    ff = 4 * pieces[4].shape[0]
    pack = jax.ShapeDtypeStruct((4,) + pieces[0].shape, BF)
    cut = jax.ShapeDtypeStruct((n, half), BF)
    return pl.pallas_call(
        ffn_bwd_kernel,
        out_shape=(
            pack, pack,
            jax.ShapeDtypeStruct((n, w), F32),
            cut, cut,
            jax.ShapeDtypeStruct((16, w), F32),
        ),
        in_specs=[SM] + [ANY] * (PIECES + 2) + [VM] * 4 + [ANY] * len(deps),
        out_specs=[ANY] * 2 + [VM] + [ANY] * 2 + [VM],
        scratch_shapes=[
            pltpu.VMEM((ff, w), BF),
            pltpu.VMEM((ff // w, w, w), BF),
            pltpu.VMEM((w, w), BF),
            pltpu.VMEM((n, w), BF),
            pltpu.VMEM((w, n), BF),
            pltpu.VMEM((n, w), BF),
            pltpu.VMEM((n, w), BF),
            pltpu.VMEM((n, w), F32),
            pltpu.VMEM((w, w), BF),
            pltpu.VMEM((4, w // 4, w), BF),
            pltpu.VMEM((n, w), BF),
            pltpu.SemaphoreType.DMA((4,)),
            pltpu.SemaphoreType.DMA((4,)),
        ],
        compiler_params=pltpu.CompilerParams(vmem_limit_bytes=54 * 2**20),
        cost_estimate=cost(32_000_000_000),
        name="ffn_bwd",
    )(place, *pieces, *atts, g, mid, n2, vecs, *deps)


def pick(array, index, axis=0):
    return lax.dynamic_index_in_dim(array, index, axis, keepdims=False)


def ordered(flag, first, second, axis):
    return jnp.stack(
        [jnp.where(flag == 1, second, first), jnp.where(flag == 1, first, second)], axis
    )


def tie(values, *others):
    return lax.optimization_barrier((values, others))[0]


class Net:
    def __init__(self):
        self.nq = lax.axis_size("seq")
        self.nf = lax.axis_size("fsdp")
        self.q = lax.axis_index("seq")
        f = lax.axis_index("fsdp")
        self.z = f // 2
        self.c = f % 2
        self.bits = (self.nf // 2).bit_length() - 1

    def permute(self, value, target):
        pairs = []
        for q in range(self.nq):
            for f in range(self.nf):
                tq, tf = target(q, f)
                pairs.append((q * self.nf + f, tq * self.nf + tf))
        return lax.ppermute(value, ALL, pairs)

    def flip_q(self, value, mask):
        return self.permute(value, lambda q, f: (q ^ mask, f))

    def flip_f(self, value, mask):
        return self.permute(value, lambda q, f: (q, f ^ mask))

    def swap(self, value):
        return self.flip_f(value, 1)

    def _token_target(self, p):
        return lambda q, f: (2 * (f % 2) + (p ^ (q % 2)), (f // 2) * 2 + q // 2)

    def _route(self, value, target):
        pairs = []
        for q in range(self.nq):
            for f in range(self.nf):
                tq, tf = target(q, f)
                if (tq, tf) != (q, f):
                    pairs.append((q * self.nf + f, tq * self.nf + tf))
        return lax.ppermute(value, ALL, pairs)

    def token_sends(self, parts):
        return [jnp.where(self.q % 2 == p, parts[0], parts[1]) for p in range(2)]

    def to_chip(self, sends):
        return [self._route(sends[p], self._token_target(p)) for p in range(2)]

    def from_chip(self, sends):
        got = []
        for p in range(2):
            forward = self._token_target(p)
            back = {}
            for q in range(self.nq):
                for f in range(self.nf):
                    back[forward(q, f)] = (q, f)
            got.append(self._route(sends[p], lambda q, f, b=back: b[(q, f)]))
        return got

    def settle(self, sends, got):
        first = jnp.where(self.c == self.q // 2, sends[0], got[0])
        return ordered(self.q % 2, first, got[1], 0)

    def gather_z(self, block, levels, gates=()):
        out = block[None]
        shape = block.shape
        for level in range(self.bits):
            if level < len(gates):
                out = tie(out, gates[level])
            levels.append(out)
            bit = self.bits - 1 - level
            got = self.flip_f(out, 2 << bit)
            out = ordered((self.z >> bit) & 1, out, got, 1).reshape((-1,) + shape)
        return out

    def scatter_z(self, blocks, gate=()):
        shape = blocks.shape[1:]
        for bit in range(self.bits):
            parts = blocks.reshape((-1, 2) + shape)
            mine = (self.z >> bit) & 1
            got = self.flip_f(pick(parts, 1 - mine, 1).astype(BF), 2 << bit)
            if bit == 0:
                got = tie(got, gate)
            blocks = pick(parts, mine, 1).astype(F32) + got.astype(F32)
        return blocks[0]

    def absolute(self, r0, r1, r2, r3):
        odd, high = self.q % 2 == 1, self.q // 2 == 1
        x0, x1 = jnp.where(odd, r1, r0), jnp.where(odd, r0, r1)
        x2, x3 = jnp.where(odd, r3, r2), jnp.where(odd, r2, r3)
        return jnp.stack(
            [
                jnp.where(high, x2, x0),
                jnp.where(high, x3, x1),
                jnp.where(high, x0, x2),
                jnp.where(high, x1, x3),
            ]
        )

    def scatter_one(self, term, cut):
        return [
            jnp.concatenate([term(3)[cut:], term(1)[cut:]]).astype(BF),
            jnp.concatenate([term(3)[:cut], term(2)[:cut]]).astype(BF),
        ]

    def scatter_two(self, term, cut, sends):
        got = [self.flip_q(sends[0], 1), self.flip_q(sends[1], 2)]
        rest = sends[0].shape[0] // 2
        more = [
            (term(1)[:cut] + got[1][:cut].astype(F32)).astype(BF),
            (term(2)[cut:] + got[0][:rest].astype(F32)).astype(BF),
        ]
        return got, more

    def scatter_three(self, term, cut, got, more):
        last = [self.flip_q(more[0], 1), self.flip_q(more[1], 2)]
        rest = got[0].shape[0] // 2
        return (
            term(0)[:cut] + got[1][cut:].astype(F32) + last[0].astype(F32),
            term(0)[cut:] + got[0][rest:].astype(F32) + last[1].astype(F32),
        )


def norm_back(xhat, inv, gain, e):
    c = e * gain
    return inv * (
        c
        - jnp.mean(c, axis=-1, keepdims=True)
        - xhat * jnp.mean(c * xhat, axis=-1, keepdims=True)
    )


def body(
    tokens,
    segments,
    qkv_weight,
    query_bias,
    value_bias,
    proj_weight,
    proj_bias,
    attn_gain,
    attn_shift,
    ffn_gain,
    ffn_shift,
    expand_weight,
    expand_bias,
    contract_weight,
    contract_bias,
    cotangent,
):
    net = Net()
    c, z = net.c, net.z
    micro, local, width = tokens.shape
    rows = qkv_weight.shape[0]
    ff = expand_weight.shape[1]
    ff_rows = contract_weight.shape[0]
    ratio = ff // width
    half = width // 2
    nq, nz = net.nq, net.nf // 2
    blk = rows * net.nf
    n = 2 * micro * local
    mine = micro * local

    place = jnp.stack([net.q, c]).astype(jnp.int32)

    seg_rows = jnp.zeros((micro, SEG_ROWS, width), BF).at[:, 0, :local].set(segments.astype(BF))
    tok_send = jnp.concatenate([tokens, seg_rows], axis=1)
    tok_sends = net.token_sends([tok_send[0], tok_send[1]])
    tok_got = net.to_chip(tok_sends)
    tok = net.settle(tok_sends, tok_got)
    tok_far = net.swap(tok)
    seg = ordered(c, tok[:, local, :local], tok_far[:, local, :local], 0).reshape(n)
    seg = seg.astype(jnp.int32)
    docs = jnp.arange(32, dtype=jnp.int32)
    before = jnp.sum((seg[None, :] < docs[:, None]).astype(jnp.int32), axis=1)
    start = jnp.sum(jnp.where(seg[None, :] == docs[:, None], before[:, None], 0), axis=0)
    lo = start[::B] // B
    start = start.reshape(n // B, B)

    qkv_w, con_w, proj_w, exp_w, vector_args = tie(
        (
            qkv_weight,
            contract_weight,
            proj_weight,
            expand_weight,
            (
                query_bias,
                value_bias,
                proj_bias,
                attn_gain,
                attn_shift,
                ffn_gain,
                ffn_shift,
                contract_bias,
                expand_bias,
            ),
        ),
        tok_sends,
    )
    small_len = sum(x.shape[0] for x in vector_args)
    small, at = 0.0, 0
    for x in vector_args:
        small = small + jnp.pad(x.astype(F32), (at, half - at - x.shape[0]))
        at += x.shape[0]
    small = jnp.pad(small.astype(BF)[None], ((0, 7), (0, 0)))

    def columns(matrix, t, s):
        return matrix[:, t * width + s * half : t * width + (s + 1) * half]

    packs = [
        jnp.concatenate(
            [columns(qkv_w, t, s) for t in range(3)]
            + [small, columns(con_w, 0, s), columns(proj_w, 0, s)]
            + [columns(exp_w, t, s) for t in range(ratio)]
        )
        for s in range(2)
    ]
    pack = ordered(
        c,
        jnp.where(c == 0, packs[0], packs[1]),
        net.swap(jnp.where(c == 0, packs[1], packs[0])),
        0,
    )
    n_q = 3 * rows + 8
    q_levels, f_levels = [], []
    pack_q = net.gather_z(pack[:, :n_q], q_levels).reshape(net.nf, n_q, half)
    part_q = jnp.concatenate(
        [pack_q[:, t * rows : (t + 1) * rows].reshape(blk, half) for t in range(3)]
        + [pack_q[:, 3 * rows]]
    )
    part_q = tie(part_q, tok_got)
    cut = 3 * blk // 2
    q1, q2 = net.flip_q(part_q, 1), net.flip_q(part_q, 2)
    q3_sends = q1[:cut], q2[cut:]
    q3a, q3b = net.flip_q(q3_sends[0], 2), net.flip_q(q3_sends[1], 1)
    n_con, n_proj = ratio * blk, blk
    top = n_con + n_proj
    pack_f = net.gather_z(pack[:, n_q:], f_levels, (q_levels[-1], part_q))
    pack_f = pack_f.reshape(net.nf, -1, half)
    part_f = jnp.concatenate(
        [pack_f[:, :ff_rows].reshape(-1, half), pack_f[:, ff_rows : ff_rows + rows].reshape(-1, half)]
        + [
            pack_f[:, ff_rows + t * rows : ff_rows + (t + 1) * rows].reshape(-1, half)
            for t in range(1, ratio + 1)
        ]
    )
    part_f = tie(part_f, q3_sends)
    f1, f2 = net.flip_q(part_f, 1), net.flip_q(part_f, 2)
    f3_sends = f1[:top], f2[top:]

    vectors = net.absolute(part_q[3 * blk :], q1[3 * blk :], q2[3 * blk :], q3b[3 * blk - cut :])
    vectors = vectors.reshape(nq * net.nf, half).astype(F32)
    eight = [vectors[:, s * rows : (s + 1) * rows].reshape(width) for s in range(8)]
    q_off, v_off, proj_off, a_gain, a_shift, f_gain, f_shift, con_off = eight
    exp_off = vectors[:, 8 * rows : small_len].reshape(ff)
    vecs = jnp.concatenate(
        [
            jnp.stack([proj_off, f_gain, f_shift, con_off]),
            jnp.zeros((4, width), F32),
            exp_off.reshape(ratio, width),
            jnp.zeros((8 - ratio, width), F32),
        ]
    )

    bias = jnp.concatenate(
        [pick(q_off.reshape(2, half), c), jnp.zeros((half,), F32), pick(v_off.reshape(2, half), c)]
    )[None]
    normed_all, query, key, value, w_qkv = qkv_apply(
        place,
        (part_q, q1, q2, q3a, q3b),
        tok,
        tok_far,
        jnp.stack([a_gain, a_shift]),
        bias,
        [part_f],
    )
    att, lse = attn_fwd(lo, start, query, key, value, f3_sends)
    att_got = net.swap(pick(att.reshape(2, mine, half), 1 - c))
    f3a, f3b = net.flip_q(f3_sends[0], 2), net.flip_q(f3_sends[1], 1)
    cot_sends = net.token_sends(tie((cotangent[0], cotangent[1]), f3a, f3b))
    pieces = [part_f, f1, f2, f3a, f3b]
    pieces = pieces + [net.swap(x) for x in pieces]
    atts = (att, att_got)

    out, middle, normed_two = ffn_fwd(place, pieces, atts, tok, vecs, cot_sends)
    out_sends = net.token_sends([out[:local], out[local:]])
    out_got = net.from_chip(out_sends)

    g = net.settle(cot_sends, net.to_chip(cot_sends)).reshape(mine, width)
    keep, send, middle_grad, ag_own, ag_send, sums = ffn_bwd(
        place, pieces, atts, g, middle, normed_two, vecs, out_sends
    )
    ag_send, send, out_got = tie((ag_send, send, out_got))
    result = net.settle(out_sends, out_got)
    ag_got = net.swap(ag_send)
    proj_off_grad, f_gain_grad, f_shift_grad, con_off_grad = (sums[s] for s in range(4))
    exp_off_grad = sums[8 : 8 + ratio].reshape(ff)

    got = net.swap(send)

    def term(r):
        return pick(keep, net.q ^ r).astype(F32) + pick(got, net.q ^ r).astype(F32)

    f_sends = net.scatter_one(term, top)
    d_mixed = attn_bwd(
        place, lo, start, query, key, value, att, lse, ag_own, ag_got, f_sends
    )
    f_got, f_more = net.scatter_two(term, top, f_sends)
    d_mixed, f_more = tie((d_mixed, f_more))

    e_send = dg(pick(d_mixed.reshape(2, mine, 3 * half), 1 - c), w_qkv, NT).astype(BF)
    d_mixed, e_send = tie((d_mixed, e_send))
    e_got = net.swap(e_send)
    qkv_grad = dg(normed_all, d_mixed, TN).reshape(nq, blk, 3 * half)
    d_sum = jnp.sum(d_mixed.astype(F32), axis=0)
    q_off_half = d_sum[:half]
    v_off_half = d_sum[2 * half :]
    sum_a, sum_b = net.scatter_three(term, top, f_got, f_more)
    per_f = jnp.concatenate(
        [
            sum_a[:n_con].reshape(net.nf, ff_rows, half),
            sum_a[n_con:].reshape(net.nf, rows, half),
        ]
        + [sum_b[t * blk : (t + 1) * blk].reshape(net.nf, rows, half) for t in range(ratio)],
        axis=1,
    )
    d_mixed, qkv_grad, per_f = tie((d_mixed, qkv_grad, per_f))
    e_one = dg(pick(d_mixed.reshape(2, mine, 3 * half), c), w_qkv, NT) + e_got.astype(F32)
    xhat_one, inv_one = norm_tile(tok[:, :local].reshape(mine, width).astype(F32))
    a_gain_grad = jnp.sum(e_one * xhat_one, axis=0)
    a_shift_grad = jnp.sum(e_one, axis=0)
    tok_grad = (middle_grad + norm_back(xhat_one, inv_one, a_gain, e_one)).astype(BF)
    tg_sends = net.token_sends([tok_grad[:local], tok_grad[local:]])

    zero = jnp.zeros((half,), F32)
    q_off_grad = jnp.where(c == 0, jnp.concatenate([q_off_half, zero]), jnp.concatenate([zero, q_off_half]))
    v_off_grad = jnp.where(c == 0, jnp.concatenate([v_off_half, zero]), jnp.concatenate([zero, v_off_half]))
    vec = jnp.concatenate(
        [
            x.reshape(nq, net.nf, -1)
            for x in (
                q_off_grad,
                v_off_grad,
                proj_off_grad,
                a_gain_grad,
                a_shift_grad,
                f_gain_grad,
                f_shift_grad,
                con_off_grad,
                exp_off_grad,
            )
        ],
        axis=2,
    )
    vec_rows = net.nf * small_len // (3 * half)
    vec = jnp.pad(vec.reshape(nq, vec_rows, 3 * half), ((0, 0), (0, 16 - vec_rows), (0, 0)))

    def q_term(r):
        return jnp.concatenate([pick(qkv_grad, net.q ^ r), pick(vec, net.q ^ r)])

    q_cut = (blk + 16) // 2
    q_sends, tg_sends = tie((net.scatter_one(q_term, q_cut), tg_sends))
    q_got, q_more = net.scatter_two(q_term, q_cut, q_sends)
    tg_sends = tie(tg_sends, q_more)
    token_grad = net.settle(tg_sends, net.from_chip(tg_sends))
    q_sum = jnp.concatenate(net.scatter_three(q_term, q_cut, q_got, q_more))
    vec = q_sum[blk : blk + vec_rows].reshape(net.nf, 1, small_len)
    vec = jnp.pad(vec, ((0, 0), (0, 7), (0, 3 * half - small_len)))
    q_sum = jnp.concatenate([q_sum[:blk].reshape(net.nf, rows, 3 * half), vec], axis=1)

    per_core = net.scatter_z(per_f.reshape(nz, 2, -1, half), q_sends)
    final = ordered(c, pick(per_core, c), net.swap(pick(per_core, 1 - c)), 0)
    con_out = jnp.concatenate([final[0, :ff_rows], final[1, :ff_rows]], axis=1)
    proj_out = jnp.concatenate(
        [final[0, ff_rows : ff_rows + rows], final[1, ff_rows : ff_rows + rows]], axis=1
    )
    exp_out = jnp.concatenate(
        [
            final[s, ff_rows + rows + t * rows : ff_rows + rows + (t + 1) * rows]
            for t in range(ratio)
            for s in range(2)
        ],
        axis=1,
    )
    q_core = net.scatter_z(q_sum.reshape(nz, 2, rows + 8, 3 * half))
    q_kept, q_far = pick(q_core, c), net.swap(pick(q_core, 1 - c))
    vec = (q_kept + q_far)[rows, :small_len]
    final = ordered(c, q_kept, q_far, 0)
    qkv_out = jnp.concatenate(
        [final[s, :rows, t * half : (t + 1) * half] for t in range(3) for s in range(2)], axis=1
    )
    outs = [vec[s * rows : (s + 1) * rows] for s in range(8)]
    exp_off_out = vec[8 * rows :]
    return (
        result,
        token_grad,
        qkv_out,
        outs[0],
        outs[1],
        proj_out,
        outs[2],
        outs[3],
        outs[4],
        outs[5],
        outs[6],
        exp_out,
        exp_off_out,
        con_out,
        outs[7],
    )


def solution(mesh):
    act = P("fsdp", "seq", None)
    mat = P(ALL, None)
    vec = P(ALL)
    return jax.shard_map(
        body,
        mesh=mesh,
        in_specs=(
            act, P("fsdp", "seq"), mat, vec, vec, mat, vec, vec, vec, vec, vec, mat, vec, mat, vec, act,
        ),
        out_specs=(act, act, mat, vec, vec, mat, vec, vec, vec, vec, vec, mat, vec, mat, vec),
        check_vma=False,
    )
```

```python
import functools

import jax
import jax.numpy as jnp
from jax import lax
from jax.experimental import pallas as pl
from jax.experimental.pallas import tpu as pltpu
from jax.sharding import PartitionSpec as P

HD = 64
NORM_EPS = 1e-05
NEG = -1e30
B = 256
MOST_DOC = 1024
ALL = ("seq", "fsdp")
BF = jnp.bfloat16
F32 = jnp.float32
NT = (((1,), (1,)), ((), ()))
NN = (((1,), (0,)), ((), ()))
TN = (((0,), (0,)), ((), ()))
TILE = 512
SEG_ROWS = 16
COST = 1.0
ANY = pl.BlockSpec(memory_space=pl.ANY)
VM = pl.BlockSpec(memory_space=pltpu.VMEM)
SM = pl.BlockSpec(memory_space=pltpu.SMEM)


def dg(a, b, dims):
    return lax.dot_general(a, b, dims, preferred_element_type=F32)


def cost(flops):
    return pl.CostEstimate(flops=int(flops * COST), bytes_accessed=1_000_000, transcendentals=0)


def norm_tile(v):
    mean = jnp.mean(v, axis=-1, keepdims=True)
    centered = v - mean
    var = jnp.mean(centered * centered, axis=-1, keepdims=True)
    inv = lax.rsqrt(var + NORM_EPS)
    return centered * inv, inv


def fwd_kernel(lo_ref, start_ref, q_ref, k_ref, v_ref, *refs, heads, base):
    o_ref, lse_ref, qm, vt, sbuf, mx8 = refs[-6:]
    end = base + o_ref.shape[0] // B
    lane = lax.broadcasted_iota(jnp.int32, (B, 128), 1)
    kio = lax.broadcasted_iota(jnp.int32, (B, B), 0)
    qio = lax.broadcasted_iota(jnp.int32, (B, B), 1)

    def transpose_block(j, _):
        s = pl.ds(pl.multiple_of(j * B, B), B)
        for p in range(heads // 2):
            vt[128 * p : 128 * p + 128, s] = v_ref[s, 128 * p : 128 * p + 128].T
        return 0

    lax.fori_loop(lo_ref[base], end, transpose_block, 0)

    def qblock(i, _):
        qs = pl.multiple_of(i * B, B)
        rows_out = pl.ds(pl.multiple_of((i - base) * B, B), B)
        for p in range(heads // 2):
            qq = q_ref[pl.ds(qs, B), 128 * p : 128 * p + 128]
            qm[2 * p] = jnp.where(lane < 64, qq, jnp.zeros_like(qq))
            qm[2 * p + 1] = jnp.where(lane >= 64, qq, jnp.zeros_like(qq))
        st_row = start_ref[pl.ds(i, 1), :]

        def scores(j, first):
            ks = pl.multiple_of(j * B, B)
            mask = (kio + ks) >= st_row
            if first:
                mask = mask & (kio <= qio)
            slot = i - j
            for h in range(heads):
                p = h // 2
                k_blk = k_ref[pl.ds(ks, B), 128 * p : 128 * p + 128]
                st = jnp.where(mask, dg(k_blk, qm[h], NT), NEG)
                sbuf[h, slot] = st
                m8 = jnp.max(st.reshape(B // 8, 8, B), axis=0)
                mx8[h] = m8 if first else jnp.maximum(mx8[h], m8)

        scores(i, True)

        def score_step(j, c):
            scores(j, False)
            return c

        lax.fori_loop(lo_ref[i], i, score_step, 0)
        ms = [jnp.max(mx8[h], axis=0, keepdims=True) for h in range(heads)]

        def weigh(j):
            ks = pl.multiple_of(j * B, B)
            slot = i - j
            outs = []
            for h in range(heads):
                p = jnp.exp(sbuf[h, slot] - ms[h])
                l8 = jnp.sum(p.reshape(B // 8, 8, B), axis=0)
                ot = dg(vt[64 * h : 64 * h + 64, pl.ds(ks, B)], p.astype(BF), NN)
                outs.append((ot, l8))
            return outs

        def weigh_step(j, c):
            return [(a[0] + b[0], a[1] + b[1]) for a, b in zip(c, weigh(j))]

        res = lax.fori_loop(lo_ref[i], i, weigh_step, weigh(i))
        for p in range(heads // 2):
            rows = []
            for h in (2 * p, 2 * p + 1):
                total = jnp.sum(res[h][1], axis=0, keepdims=True)
                rows.append(res[h][0] * (1.0 / total))
                lse_ref[h : h + 1, rows_out] = ms[h] + jnp.log(total)
            pair = jnp.concatenate(rows, axis=0)
            o_ref[rows_out, 128 * p : 128 * p + 128] = pair.T.astype(BF)
        return 0

    lax.fori_loop(base, end, qblock, 0)


def attn_fwd(lo, start, q, k, v, part, deps):
    n, w = q.shape
    heads = w // HD
    maxb = min(n // B, (MOST_DOC + B - 2) // B + 1)
    return pl.pallas_call(
        functools.partial(fwd_kernel, heads=heads, base=part * (n // 2 // B)),
        out_shape=(
            jax.ShapeDtypeStruct((n // 2, w), BF),
            jax.ShapeDtypeStruct((8, n // 2), F32),
        ),
        in_specs=[SM] + [VM] * 4 + [ANY] * len(deps),
        out_specs=[VM] * 2,
        scratch_shapes=[
            pltpu.VMEM((heads, B, 128), BF),
            pltpu.VMEM((w, n), BF),
            pltpu.VMEM((heads, maxb, B, B), F32),
            pltpu.VMEM((heads, 8, B), F32),
        ],
        compiler_params=pltpu.CompilerParams(vmem_limit_bytes=32 * 2**20),
        cost_estimate=cost(10_000_000_000),
        name="attn_fwd",
    )(lo, start, q, k, v, *deps)


def bwd_kernel(
    place, lo_ref, start_ref, q_ref, k_ref, v_ref, o0_ref, o1_ref, lse0_ref, lse1_ref, own_ref, got_ref, *refs, heads,
):
    out_ref, qm, dm, dqa, dka, dva, dd, kt = refs[-8:]
    n = q_ref.shape[0] // B
    wide = heads * HD
    c = place[1]
    lane = lax.broadcasted_iota(jnp.int32, (B, 128), 1)
    kio = lax.broadcasted_iota(jnp.int32, (B, B), 0)
    qio = lax.broadcasted_iota(jnp.int32, (B, B), 1)
    dka[...] = jnp.zeros_like(dka)
    dva[...] = jnp.zeros_like(dva)

    def transpose_block(j, _):
        s = pl.ds(pl.multiple_of(j * B, B), B)
        for p in range(heads // 2):
            kt[128 * p : 128 * p + 128, s] = k_ref[s, 128 * p : 128 * p + 128].T
        return 0

    lax.fori_loop(0, n, transpose_block, 0)

    def qblock(i, _):
        qs = pl.multiple_of(i * B, B)
        for p in range(heads // 2):
            cs = slice(128 * p, 128 * p + 128)
            qq = q_ref[pl.ds(qs, B), cs]
            gs = pl.ds(pl.multiple_of((i % (n // 2)) * B, B), B)
            gg = jnp.where(i // (n // 2) == c, own_ref[gs, cs], got_ref[gs, cs])
            oo = jnp.where(i < n // 2, o0_ref[gs, cs], o1_ref[gs, cs])
            prod = (oo.astype(F32) * gg.astype(F32)).T
            dd[2 * p : 2 * p + 1, :] = jnp.sum(prod[:64], axis=0, keepdims=True)
            dd[2 * p + 1 : 2 * p + 2, :] = jnp.sum(prod[64:], axis=0, keepdims=True)
            z = jnp.zeros_like(qq)
            qm[2 * p] = jnp.where(lane < 64, qq, z)
            qm[2 * p + 1] = jnp.where(lane >= 64, qq, z)
            dm[2 * p] = jnp.where(lane < 64, gg, z)
            dm[2 * p + 1] = jnp.where(lane >= 64, gg, z)
        st_row = start_ref[pl.ds(i, 1), :]
        gs = pl.ds(pl.multiple_of((i % (n // 2)) * B, B), B)

        def block(j, first):
            ks = pl.multiple_of(j * B, B)
            mask = (kio + ks) >= st_row
            if first:
                mask = mask & (kio <= qio)
            for p in range(heads // 2):
                cs = slice(128 * p, 128 * p + 128)
                k_blk = k_ref[pl.ds(ks, B), cs]
                v_blk = v_ref[pl.ds(ks, B), cs]
                dvs, dks, dqs = [], [], []
                for h in (2 * p, 2 * p + 1):
                    st = dg(k_blk, qm[h], NT)
                    lse = jnp.where(i < n // 2, lse0_ref[h : h + 1, gs], lse1_ref[h : h + 1, gs])
                    pt = jnp.exp(jnp.where(mask, st, NEG) - lse)
                    dp = dg(v_blk, dm[h], NT)
                    ds = pt * (dp - dd[h : h + 1, :])
                    pb = pt.astype(BF)
                    db = ds.astype(BF)
                    dvs.append(dg(pb, dm[h], NN))
                    dks.append(dg(db, qm[h], NN))
                    dqs.append(dg(kt[64 * h : 64 * h + 64, pl.ds(ks, B)], db, NN))
                dva[pl.ds(ks, B), cs] += dvs[0] + dvs[1]
                dka[pl.ds(ks, B), cs] += dks[0] + dks[1]
                dq = jnp.concatenate(dqs, axis=0)
                if first:
                    dqa[cs, :] = dq
                else:
                    dqa[cs, :] += dq

        block(i, True)

        def step(j, c):
            block(j, False)
            return c

        lax.fori_loop(lo_ref[i], i, step, 0)
        for p in range(heads // 2):
            cs = slice(128 * p, 128 * p + 128)
            out_ref[pl.ds(qs, B), cs] = (dqa[cs, :] * 0.125).T.astype(BF)
        return 0

    lax.fori_loop(0, n, qblock, 0)

    def finish(i, _):
        s = pl.ds(pl.multiple_of(i * B, B), B)
        out_ref[s, wide : 2 * wide] = dka[s, :].astype(BF)
        out_ref[s, 2 * wide :] = dva[s, :].astype(BF)
        return 0

    lax.fori_loop(0, n, finish, 0)


def attn_bwd(place, lo, start, q, k, v, atts, lses, own, got, deps):
    n, w = q.shape
    heads = w // HD
    return pl.pallas_call(
        functools.partial(bwd_kernel, heads=heads),
        out_shape=jax.ShapeDtypeStruct((n, 3 * w), BF),
        in_specs=[SM] * 2 + [VM] * 10 + [ANY] * len(deps),
        out_specs=VM,
        scratch_shapes=[
            pltpu.VMEM((heads, B, 128), BF),
            pltpu.VMEM((heads, B, 128), BF),
            pltpu.VMEM((w, B), F32),
            pltpu.VMEM((n, w), F32),
            pltpu.VMEM((n, w), F32),
            pltpu.VMEM((8, B), F32),
            pltpu.VMEM((w, n), BF),
        ],
        compiler_params=pltpu.CompilerParams(vmem_limit_bytes=56 * 2**20),
        cost_estimate=cost(42_000_000_000),
        name="attn_bwd",
    )(place, lo, start, q, k, v, *atts, *lses, own, got, *deps)


def qkv_bwd_kernel(place, mixed, normed, w_ref, *refs):
    e_own, e_send, qg, sums = refs[-4:]
    c = place[1]
    count = e_own.shape[0]
    wide = sums.shape[1]
    step = min(512, count)
    sums[...] = jnp.zeros_like(sums)

    def push(m, _):
        s = pl.ds(pl.multiple_of(m * step, step), step)
        far = pl.ds(pl.multiple_of((1 - c) * count + m * step, step), step)
        own = pl.ds(pl.multiple_of(c * count + m * step, step), step)
        for rows in (far, own):
            sums[0:1, :] += jnp.sum(mixed[rows, :wide].astype(F32), axis=0, keepdims=True)
            sums[1:2, :] += jnp.sum(mixed[rows, 2 * wide :].astype(F32), axis=0, keepdims=True)
        e_send[s, :] = dg(mixed[far, :], w_ref[...], NT).astype(BF)
        e_own[s, :] = dg(mixed[own, :], w_ref[...], NT)
        return 0

    lax.fori_loop(0, count // step, push, 0)
    for at in range(0, 3 * wide, 256):
        cols = slice(at, min(at + 256, 3 * wide))
        grad = dg(normed[...], mixed[:, cols], TN).astype(BF)
        qg[:, :, cols] = grad.reshape(qg.shape[0], qg.shape[1], -1)


def qkv_bwd(place, mixed, normed, w_qkv, deps):
    n, d = normed.shape
    w = mixed.shape[1] // 3
    return pl.pallas_call(
        qkv_bwd_kernel,
        out_shape=(
            jax.ShapeDtypeStruct((n // 2, d), F32),
            jax.ShapeDtypeStruct((n // 2, d), BF),
            jax.ShapeDtypeStruct((4, d // 4, 3 * w), BF),
            jax.ShapeDtypeStruct((8, w), F32),
        ),
        in_specs=[SM] + [VM] * 3 + [ANY] * len(deps),
        out_specs=[VM] * 4,
        compiler_params=pltpu.CompilerParams(vmem_limit_bytes=40 * 2**20),
        cost_estimate=cost(1_000_000_000),
        name="qkv_bwd",
    )(place, mixed, normed, w_qkv, *deps)


def last_kernel(place, e_own, e_got, x_ref, mg_ref, vecs, f_sums, d_sums, out, vec, sums):
    step = pl.program_id(0)

    @pl.when(step == 0)
    def _():
        sums[...] = jnp.zeros_like(sums)
        vec[...] = jnp.zeros_like(vec)

    e = e_own[...] + e_got[...].astype(F32)
    xhat, inv = norm_tile(x_ref[0].astype(F32))
    ce = e * vecs[0:1, :]
    grad = mg_ref[...] + inv * (
        ce
        - jnp.mean(ce, axis=-1, keepdims=True)
        - xhat * jnp.mean(ce * xhat, axis=-1, keepdims=True)
    )
    out[0] = grad.astype(BF)
    sums[3:4, :] += jnp.sum(e * xhat, axis=0, keepdims=True)
    sums[4:5, :] += jnp.sum(e, axis=0, keepdims=True)

    @pl.when(step == pl.num_programs(0) - 1)
    def _():
        half = d_sums.shape[1]
        for core in range(2):

            @pl.when(place[1] == core)
            def _(core=core):
                sums[0:2, core * half : core * half + half] = d_sums[0:2, :]

        sums[2:3, :] = f_sums[0:1, :]
        sums[5:8, :] = f_sums[1:4, :]
        parts = vec.shape[0]
        blk = sums.shape[1] // parts
        for p in range(parts):
            vec[p, 0:8, 0:blk] = sums[:, p * blk : p * blk + blk]
            for t in range(parts):
                vec[p, 8 + t : 9 + t, 0:blk] = f_sums[8 + p : 9 + p, t * blk : t * blk + blk]


def last_norm(place, e_own, e_got, tok, mg, vecs, f_sums, d_sums, lanes):
    n, w = e_own.shape
    count = n // 2
    step = 256
    per = count // step
    flat = pl.BlockSpec((step, w), lambda i: (i, 0))
    block = pl.BlockSpec((1, step, w), lambda i: (i // per, i % per, 0))
    return pl.pallas_call(
        last_kernel,
        grid=(n // step,),
        out_shape=(
            jax.ShapeDtypeStruct((2, count, w), BF),
            jax.ShapeDtypeStruct((4, 16, lanes), F32),
        ),
        in_specs=[SM, flat, flat, block, flat]
        + [pl.BlockSpec(x.shape, lambda i: (0, 0)) for x in (vecs, f_sums, d_sums)],
        out_specs=[block, pl.BlockSpec((4, 16, lanes), lambda i: (0, 0, 0))],
        scratch_shapes=[pltpu.VMEM((8, w), F32)],
        compiler_params=pltpu.CompilerParams(vmem_limit_bytes=16 * 2**20),
        cost_estimate=cost(400_000_000),
        name="last_norm",
    )(place, e_own, e_got, tok, mg, vecs, f_sums, d_sums)


def add_kernel(place, keep, got, out_x, out_y):
    step = pl.program_id(0)
    total = (keep[...].astype(F32) + got[...].astype(F32)).astype(BF)

    @pl.when(step < 2)
    def _():
        out_x[...] = total

    @pl.when(step >= 2)
    def _():
        out_y[...] = total


def first_messages(place, keep, got):
    _, rows, w = keep.shape
    half = rows // 2

    def at(i, p):
        r = jnp.where(i % 2 == 0, 3, jnp.where(i < 2, 1, 2))
        return (p[0] ^ r, jnp.where(i < 2, 1, 0), 0)

    pack = pl.BlockSpec((None, half, w), at)
    message = jax.ShapeDtypeStruct((rows, w), BF)
    return pl.pallas_call(
        add_kernel,
        grid_spec=pltpu.PrefetchScalarGridSpec(
            num_scalar_prefetch=1,
            grid=(4,),
            in_specs=[pack, pack],
            out_specs=[
                pl.BlockSpec((half, w), lambda i, p: (jnp.minimum(i, 1), 0)),
                pl.BlockSpec((half, w), lambda i, p: (jnp.maximum(i - 2, 0), 0)),
            ],
        ),
        out_shape=(message, message),
        compiler_params=pltpu.CompilerParams(vmem_limit_bytes=56 * 2**20),
        cost_estimate=cost(400_000_000),
        name="first_messages",
    )(place, keep, got)


def qkv_kernel(place, w0, w1, w2, w3a, w3b, own, far, vecs, bias, *refs):
    normed, q_ref, k_ref, v_ref, w, sems = refs[-6:]
    q, c = place[0], place[1]
    blk = w.shape[0] // 4
    half = w.shape[1] // 3
    copies = []

    def add(src, rows, r, offset, part):
        start = pl.multiple_of((q ^ r) * blk + offset, 16)
        size = rows.stop - rows.start
        copies.append(
            pltpu.make_async_copy(
                src.at[rows],
                w.at[pl.ds(start, size), part * half : part * half + half],
                sems.at[len(copies)],
            )
        )

    for r, src in enumerate((w0, w1, w2)):
        for part in range(3):
            add(src, slice(part * blk, part * blk + blk), r, 0, part)
    cut = blk // 2
    add(w3a, slice(0, blk), 3, 0, 0)
    add(w3a, slice(blk, blk + cut), 3, 0, 1)
    add(w3b, slice(0, cut), 3, cut, 1)
    add(w3b, slice(cut, cut + blk), 3, 0, 2)
    for copy in copies:
        copy.start()
    for copy in copies:
        copy.wait()
    count = q_ref.shape[0] // 2
    per = count // TILE // 2

    for k, ref in enumerate((own, far)):
        base = (c if k == 0 else 1 - c) * count

        def tile(m, _, ref=ref, base=base):
            x = ref[m // per, pl.ds(pl.multiple_of((m % per) * TILE, TILE), TILE), :].astype(F32)
            xhat, _inv = norm_tile(x)
            y = (xhat * vecs[0:1, :] + vecs[1:2, :]).astype(BF)
            s = pl.ds(pl.multiple_of(base + m * TILE, TILE), TILE)
            normed[s, :] = y
            mixed = dg(y, w[...], NN) + bias[...]
            q_ref[s, :] = mixed[:, :half].astype(BF) * BF(0.125)
            k_ref[s, :] = mixed[:, half : 2 * half].astype(BF)
            v_ref[s, :] = mixed[:, 2 * half :].astype(BF)
            return 0

        lax.fori_loop(0, 2 * per, tile, 0)


def qkv_apply(place, weights, own, far, vecs, bias, deps):
    width = own.shape[2]
    half = width // 2
    n = 4 * (own.shape[1] - SEG_ROWS)
    part = jax.ShapeDtypeStruct((n, half), BF)
    return pl.pallas_call(
        qkv_kernel,
        out_shape=(
            jax.ShapeDtypeStruct((n, width), BF),
            part,
            part,
            part,
            jax.ShapeDtypeStruct((width, 3 * half), BF),
        ),
        in_specs=[SM] + [ANY] * 5 + [VM] * 4 + [ANY] * len(deps),
        out_specs=[VM] * 5,
        scratch_shapes=[pltpu.SemaphoreType.DMA((13,))],
        compiler_params=pltpu.CompilerParams(vmem_limit_bytes=56 * 2**20),
        cost_estimate=cost(400_000_000),
        name="qkv",
    )(place, *weights, own, far, vecs, bias, *deps)


GELU_A = 0.7978845608028654
GELU_B = 0.7978845608028654 * 0.044715


PIECES = 10


def load_parts(place, pieces, att_refs, w_con, w_exp, w_proj, att, sems):
    q, c = place[0], place[1]
    blk = w_proj.shape[1] // 4
    n_con = w_con.shape[1] // 4
    top = n_con + blk
    for core in range(2):

        @pl.when(c == core)
        def _(core=core):
            pltpu.make_async_copy(att_refs[core], att.at[core], sems.at[1]).start()
            pltpu.make_async_copy(att_refs[2], att.at[1 - core], sems.at[1]).start()


    def each(action):
        for r in range(4):
            rows = pl.ds(pl.multiple_of((q ^ r) * blk, blk), blk)
            con_rows = pl.ds(pl.multiple_of((q ^ r) * n_con, n_con), n_con)
            for k in range(2):
                a_ref = pieces[5 * k + r]
                b_ref, b_at = (a_ref, top) if r < 3 else (pieces[5 * k + 4], 0)
                action(c if k == 0 else 1 - c, a_ref, b_ref, b_at, rows, con_rows)

    def proj(side, a_ref, b_ref, b_at, rows, con_rows):
        pltpu.make_async_copy(a_ref.at[n_con:top], w_proj.at[side, rows], sems.at[0]).start()

    def expand(b, side, a_ref, b_ref, b_at, rows, con_rows):
        src = b_ref.at[b_at + b * blk : b_at + b * blk + blk]
        pltpu.make_async_copy(src, w_exp.at[b, side, rows], sems.at[2]).start()

    def contract(side, a_ref, b_ref, b_at, rows, con_rows):
        pltpu.make_async_copy(a_ref.at[0:n_con], w_con.at[side, con_rows], sems.at[3]).start()

    each(proj)
    for b in range(w_exp.shape[0]):
        each(functools.partial(expand, b))
    each(contract)


def pair(ref, *at):
    return jnp.concatenate([ref[(*at[:-1], 0, at[-1])], ref[(*at[:-1], 1, at[-1])]], axis=1)


def wait_for(ref, sem):
    pltpu.make_async_copy(ref, ref, sem).wait()


def ffn_fwd_kernel(place, *refs):
    pieces, att_refs, rest = refs[:PIECES], refs[PIECES : PIECES + 3], refs[PIECES + 3 :]
    tok, vecs = rest[:2]
    out, mid, n2, w_con, w_exp, w_proj, att, acc, sems = refs[-9:]
    load_parts(place, pieces, att_refs, w_con, w_exp, w_proj, att, sems)
    wide = w_proj.shape[1]
    tiles = out.shape[0] // TILE
    per = tiles // 2
    wait_for(w_proj, sems.at[0])
    wait_for(att, sems.at[1])

    def first(m, _):
        s = pl.ds(pl.multiple_of(m * TILE, TILE), TILE)
        x = tok[m // per, pl.ds(pl.multiple_of((m % per) * TILE, TILE), TILE), :]
        v = x.astype(F32) + (dg(pair(att, s), pair(w_proj, slice(None)), NN) + vecs[0:1, :])
        mid[s, :] = v
        xhat, _inv = norm_tile(v)
        n2[s, :] = (xhat * vecs[1:2, :] + vecs[2:3, :]).astype(BF)
        return 0

    lax.fori_loop(0, tiles, first, 0)
    wait_for(w_exp, sems.at[2])
    wait_for(w_con, sems.at[3])

    def second(m, _):
        s = pl.ds(pl.multiple_of(m * TILE, TILE), TILE)
        x = n2[s, :]
        for b in range(w_exp.shape[0]):
            h = dg(x, pair(w_exp, b, slice(None)), NN) + vecs[8 + b : 9 + b, :]
            th = jnp.tanh(h * (GELU_A + GELU_B * (h * h)))
            act = (h * (0.5 + 0.5 * th)).astype(BF)
            part = dg(act, pair(w_con, slice(b * wide, b * wide + wide)), NN)
            if b == 0:
                acc[...] = part
            else:
                acc[...] += part
        out[s, :] = (mid[s, :] + (acc[...] + vecs[3:4, :])).astype(BF)
        return 0

    lax.fori_loop(0, tiles, second, 0)


def ffn_bwd_kernel(place, *refs):
    pieces, att_refs, rest = refs[:PIECES], refs[PIECES : PIECES + 3], refs[PIECES + 3 :]
    g, mid, n2, vecs = rest[:4]
    (
        keep, send, mgrad, ag_own, ag_send, sums,
        w_con, w_exp, w_proj, att, n2t, act, hg, n2g, dc, de, agr, sems, osems,
    ) = refs[-19:]
    c = place[1]
    load_parts(place, pieces, att_refs, w_con, w_exp, w_proj, att, sems)
    wide = w_proj.shape[1]
    half = wide // 2
    blk = wide // 4
    blocks = w_exp.shape[0]
    tiles = g.shape[0] // TILE
    sums[...] = jnp.zeros_like(sums)

    def flip(m, _):
        s = pl.ds(pl.multiple_of(m * TILE, TILE), TILE)
        n2t[:, s] = n2[s, :].T
        return 0

    lax.fori_loop(0, tiles, flip, 0)
    wait_for(w_exp, sems.at[2])
    wait_for(w_con, sems.at[3])

    def store(k, b):
        side = c if k % 2 == 0 else 1 - c
        if k < 2:
            src, dst = dc.at[side], (keep, send)[k].at[b, 0:wide]
        else:
            rows = pl.ds(pl.multiple_of(wide + blk + b * blk, blk), blk)
            src, dst = de.at[side], (keep, send)[k - 2].at[:, rows]
        return pltpu.make_async_copy(src, dst, osems.at[k])

    def put(ref, t, value):
        value = value.astype(BF).reshape(ref.shape[1:-1] + (256,))
        at = t * 256
        if at < half:
            ref[0, ..., at : min(at + 256, half)] = value[..., : half - at]
        if at + 256 > half:
            ref[1, ..., max(at - half, 0) : at + 256 - half] = value[..., max(half - at, 0) :]

    def block(b, _):
        con_rows = pl.ds(pl.multiple_of(b * wide, wide), wide)
        bias = vecs[pl.ds(8 + b, 1), :]

        def tile(m, _):
            s = pl.ds(pl.multiple_of(m * TILE, TILE), TILE)
            w_e = pair(w_exp, b, slice(None))
            h = dg(n2[s, :], w_e, NN) + bias
            h2 = h * h
            t1 = 0.5 + 0.5 * jnp.tanh(h * (GELU_A + GELU_B * h2))
            ac = h * t1
            act[s, :] = ac.astype(BF)
            slope = t1 + ac * (1.0 - t1) * (2 * GELU_A + 6 * GELU_B * h2)
            hid = (dg(g[s, :], pair(w_con, con_rows), NT) * slope).astype(BF)
            hg[s, :] = hid
            sums[pl.ds(8 + b, 1), :] += jnp.sum(hid.astype(F32), axis=0, keepdims=True)
            part = dg(hid, w_e, NT)
            n2g[s, :] = jnp.where(b == 0, part, n2g[s, :] + part)
            return 0

        lax.fori_loop(0, tiles, tile, 0)

        @pl.when(b > 0)
        def _():
            for k in range(4):
                store(k, b - 1).wait()

        for t in range(3):
            cols = slice(t * 256, t * 256 + 256)
            put(dc, t, dg(act[...], g[:, cols], TN))
        for k in range(2):
            store(k, b).start()
        for t in range(3):
            cols = slice(t * 256, t * 256 + 256)
            put(de, t, dg(n2t[...], hg[:, cols], NN))
        for k in range(2, 4):
            store(k, b).start()
        return 0

    lax.fori_loop(0, blocks, block, 0)
    wait_for(w_proj, sems.at[0])
    wait_for(att, sems.at[1])

    def last(m, _):
        s = pl.ds(pl.multiple_of(m * TILE, TILE), TILE)
        xhat, inv = norm_tile(mid[s, :])
        e = n2g[s, :]
        g32 = g[s, :].astype(F32)
        ce = e * vecs[1:2, :]
        mg = g32 + inv * (
            ce
            - jnp.mean(ce, axis=-1, keepdims=True)
            - xhat * jnp.mean(ce * xhat, axis=-1, keepdims=True)
        )
        mgrad[s, :] = mg
        branch = mg.astype(BF)
        hg[s, :] = branch
        sums[0:1, :] += jnp.sum(branch.astype(F32), axis=0, keepdims=True)
        sums[1:2, :] += jnp.sum(e * xhat, axis=0, keepdims=True)
        sums[2:3, :] += jnp.sum(e, axis=0, keepdims=True)
        sums[3:4, :] += jnp.sum(g32, axis=0, keepdims=True)
        grad = dg(branch, pair(w_proj, slice(None)), NT).astype(BF)
        agr[0, s, :] = grad[:, :half]
        agr[1, s, :] = grad[:, half:]
        return 0

    lax.fori_loop(0, tiles, last, 0)
    for k in range(4):
        store(k, blocks - 1).wait()
    ends = [
        pltpu.make_async_copy(agr.at[c], ag_own, osems.at[0]),
        pltpu.make_async_copy(agr.at[1 - c], ag_send, osems.at[1]),
        pltpu.make_async_copy(de.at[c], keep.at[:, wide : wide + blk], osems.at[2]),
        pltpu.make_async_copy(de.at[1 - c], send.at[:, wide : wide + blk], osems.at[3]),
    ]
    for copy in ends[:2]:
        copy.start()
    for t in range(3):
        cols = slice(t * 256, t * 256 + 256)
        put(de, t, dg(pair(att, slice(None)), hg[:, cols], TN))
    for copy in ends[2:]:
        copy.start()
    for copy in ends:
        copy.wait()


def ffn_fwd(place, pieces, atts, tok, vecs, deps):
    n, w = atts[2].shape[0], tok.shape[2]
    ff = 4 * pieces[4].shape[0]
    return pl.pallas_call(
        ffn_fwd_kernel,
        out_shape=(
            jax.ShapeDtypeStruct((n, w), BF),
            jax.ShapeDtypeStruct((n, w), F32),
            jax.ShapeDtypeStruct((n, w), BF),
        ),
        in_specs=[SM] + [ANY] * (PIECES + 3) + [VM] * 2 + [ANY] * len(deps),
        out_specs=[VM] * 3,
        scratch_shapes=[
            pltpu.VMEM((2, ff, w // 2), BF),
            pltpu.VMEM((ff // w, 2, w, w // 2), BF),
            pltpu.VMEM((2, w, w // 2), BF),
            pltpu.VMEM((2, n, w // 2), BF),
            pltpu.VMEM((TILE, w), F32),
            pltpu.SemaphoreType.DMA((4,)),
        ],
        compiler_params=pltpu.CompilerParams(vmem_limit_bytes=54 * 2**20),
        cost_estimate=cost(12_000_000_000),
        name="ffn_fwd",
    )(place, *pieces, *atts, tok, vecs, *deps)


def ffn_bwd(place, pieces, atts, g, mid, n2, vecs, deps):
    n, w = g.shape
    half = w // 2
    ff = 4 * pieces[4].shape[0]
    pack = jax.ShapeDtypeStruct((4,) + pieces[0].shape, BF)
    cut = jax.ShapeDtypeStruct((n, half), BF)
    return pl.pallas_call(
        ffn_bwd_kernel,
        out_shape=(
            pack, pack,
            jax.ShapeDtypeStruct((n, w), F32),
            cut, cut,
            jax.ShapeDtypeStruct((16, w), F32),
        ),
        in_specs=[SM] + [ANY] * (PIECES + 3) + [VM] * 4 + [ANY] * len(deps),
        out_specs=[ANY] * 2 + [VM] + [ANY] * 2 + [VM],
        scratch_shapes=[
            pltpu.VMEM((2, ff, w // 2), BF),
            pltpu.VMEM((ff // w, 2, w, w // 2), BF),
            pltpu.VMEM((2, w, w // 2), BF),
            pltpu.VMEM((2, n, w // 2), BF),
            pltpu.VMEM((w, n), BF),
            pltpu.VMEM((n, w), BF),
            pltpu.VMEM((n, w), BF),
            pltpu.VMEM((n, w), F32),
            pltpu.VMEM((2, w, half), BF),
            pltpu.VMEM((2, 4, w // 4, half), BF),
            pltpu.VMEM((2, n, half), BF),
            pltpu.SemaphoreType.DMA((4,)),
            pltpu.SemaphoreType.DMA((4,)),
        ],
        compiler_params=pltpu.CompilerParams(vmem_limit_bytes=54 * 2**20),
        cost_estimate=cost(32_000_000_000),
        name="ffn_bwd",
    )(place, *pieces, *atts, g, mid, n2, vecs, *deps)


def pick(array, index, axis=0):
    return lax.dynamic_index_in_dim(array, index, axis, keepdims=False)


def ordered(flag, first, second, axis):
    return jnp.stack(
        [jnp.where(flag == 1, second, first), jnp.where(flag == 1, first, second)], axis
    )


def tie(values, *others):
    return lax.optimization_barrier((values, others))[0]


class Net:
    def __init__(self):
        self.nq = lax.axis_size("seq")
        self.nf = lax.axis_size("fsdp")
        self.q = lax.axis_index("seq")
        f = lax.axis_index("fsdp")
        self.z = f // 2
        self.c = f % 2
        self.bits = (self.nf // 2).bit_length() - 1

    def permute(self, value, target):
        pairs = []
        for q in range(self.nq):
            for f in range(self.nf):
                tq, tf = target(q, f)
                pairs.append((q * self.nf + f, tq * self.nf + tf))
        return lax.ppermute(value, ALL, pairs)

    def flip_q(self, value, mask):
        return self.permute(value, lambda q, f: (q ^ mask, f))

    def flip_f(self, value, mask):
        return self.permute(value, lambda q, f: (q, f ^ mask))

    def swap(self, value):
        return self.flip_f(value, 1)

    def _token_target(self, p):
        return lambda q, f: (2 * (f % 2) + (p ^ (q % 2)), (f // 2) * 2 + q // 2)

    def _route(self, value, target):
        pairs = []
        for q in range(self.nq):
            for f in range(self.nf):
                tq, tf = target(q, f)
                if (tq, tf) != (q, f):
                    pairs.append((q * self.nf + f, tq * self.nf + tf))
        return lax.ppermute(value, ALL, pairs)

    def token_sends(self, parts):
        return [jnp.where(self.q % 2 == p, parts[0], parts[1]) for p in range(2)]

    def to_chip(self, sends):
        return [self._route(sends[p], self._token_target(p)) for p in range(2)]

    def from_chip(self, sends):
        got = []
        for p in range(2):
            forward = self._token_target(p)
            back = {}
            for q in range(self.nq):
                for f in range(self.nf):
                    back[forward(q, f)] = (q, f)
            got.append(self._route(sends[p], lambda q, f, b=back: b[(q, f)]))
        return got

    def settle(self, sends, got):
        first = jnp.where(self.c == self.q // 2, sends[0], got[0])
        return ordered(self.q % 2, first, got[1], 0)

    def gather_z(self, block):
        return [block] + [self.flip_f(block, 2 * m) for m in range(1, self.nf // 2)]

    def by_z(self, blocks):
        for bit in range(self.bits):
            flag = (self.z >> bit) & 1 == 1
            blocks = [jnp.where(flag, blocks[i ^ (1 << bit)], x) for i, x in enumerate(blocks)]
        return jnp.stack(blocks)

    def scatter_z(self, blocks, gate=()):
        shape = blocks.shape[1:]
        for bit in range(self.bits):
            parts = blocks.reshape((-1, 2) + shape)
            mine = (self.z >> bit) & 1
            got = self.flip_f(pick(parts, 1 - mine, 1).astype(BF), 2 << bit)
            if bit == 0:
                got = tie(got, gate)
            blocks = pick(parts, mine, 1).astype(F32) + got.astype(F32)
        return blocks[0]

    def absolute(self, r0, r1, r2, r3):
        odd, high = self.q % 2 == 1, self.q // 2 == 1
        x0, x1 = jnp.where(odd, r1, r0), jnp.where(odd, r0, r1)
        x2, x3 = jnp.where(odd, r3, r2), jnp.where(odd, r2, r3)
        return jnp.stack(
            [
                jnp.where(high, x2, x0),
                jnp.where(high, x3, x1),
                jnp.where(high, x0, x2),
                jnp.where(high, x1, x3),
            ]
        )

    def scatter_one(self, term, cut):
        return [
            jnp.concatenate([term(3)[cut:], term(1)[cut:]]).astype(BF),
            jnp.concatenate([term(3)[:cut], term(2)[:cut]]).astype(BF),
        ]

    def scatter_two(self, term, cut, sends, gate):
        got = tie([self.flip_q(sends[0], 1), self.flip_q(sends[1], 2)], gate)
        rest = sends[0].shape[0] // 2
        more = [
            (term(1)[:cut] + got[1][:cut].astype(F32)).astype(BF),
            (term(2)[cut:] + got[0][:rest].astype(F32)).astype(BF),
        ]
        return got, more

    def scatter_three(self, term, cut, got, more):
        last = [self.flip_q(more[0], 1), self.flip_q(more[1], 2)]
        rest = got[0].shape[0] // 2
        return (
            term(0)[:cut] + got[1][cut:].astype(F32) + last[0].astype(F32),
            term(0)[cut:] + got[0][rest:].astype(F32) + last[1].astype(F32),
        )


def body(
    tokens,
    segments,
    qkv_weight,
    query_bias,
    value_bias,
    proj_weight,
    proj_bias,
    attn_gain,
    attn_shift,
    ffn_gain,
    ffn_shift,
    expand_weight,
    expand_bias,
    contract_weight,
    contract_bias,
    cotangent,
):
    net = Net()
    c, z = net.c, net.z
    micro, local, width = tokens.shape
    rows = qkv_weight.shape[0]
    ff = expand_weight.shape[1]
    ff_rows = contract_weight.shape[0]
    ratio = ff // width
    half = width // 2
    nq, nz = net.nq, net.nf // 2
    blk = rows * net.nf
    n = 2 * micro * local
    mine = micro * local

    place = jnp.stack([net.q, c]).astype(jnp.int32)

    seg_rows = jnp.zeros((micro, SEG_ROWS, width), BF).at[:, 0, :local].set(segments.astype(BF))
    tok_send = jnp.concatenate([tokens, seg_rows], axis=1)
    tok_sends = net.token_sends([tok_send[0], tok_send[1]])
    tok_got = net.to_chip(tok_sends)
    tok = net.settle(tok_sends, tok_got)
    tok_far = net.swap(tok)
    seg = ordered(c, tok[:, local, :local], tok_far[:, local, :local], 0).reshape(n)
    seg = seg.astype(jnp.int32)
    docs = jnp.arange(32, dtype=jnp.int32)
    before = jnp.sum((seg[None, :] < docs[:, None]).astype(jnp.int32), axis=1)
    start = jnp.sum(jnp.where(seg[None, :] == docs[:, None], before[:, None], 0), axis=0)
    lo = start[::B] // B
    start = start.reshape(n // B, B)

    qkv_w, con_w, proj_w, exp_w, vector_args = tie(
        (
            qkv_weight,
            contract_weight,
            proj_weight,
            expand_weight,
            (
                query_bias,
                value_bias,
                proj_bias,
                attn_gain,
                attn_shift,
                ffn_gain,
                ffn_shift,
                contract_bias,
                expand_bias,
            ),
        ),
        tok_sends,
    )
    small_len = sum(x.shape[0] for x in vector_args)
    small, at = 0.0, 0
    for x in vector_args:
        small = small + jnp.pad(x.astype(F32), (at, half - at - x.shape[0]))
        at += x.shape[0]
    small = jnp.pad(small.astype(BF)[None], ((0, 7), (0, 0)))

    def columns(matrix, t, s):
        return matrix[:, t * width + s * half : t * width + (s + 1) * half]

    packs = [
        jnp.concatenate(
            [columns(qkv_w, t, s) for t in range(3)]
            + [small, columns(con_w, 0, s), columns(proj_w, 0, s)]
            + [columns(exp_w, t, s) for t in range(ratio)]
        )
        for s in range(2)
    ]
    pack = ordered(
        c,
        jnp.where(c == 0, packs[0], packs[1]),
        net.swap(jnp.where(c == 0, packs[1], packs[0])),
        0,
    )
    n_q = 3 * rows + 8
    pack_qs = net.gather_z(pack[:, :n_q])
    pack_q = net.by_z(tie(pack_qs, tok_got)).reshape(net.nf, n_q, half)
    part_q = jnp.concatenate(
        [pack_q[:, t * rows : (t + 1) * rows].reshape(blk, half) for t in range(3)]
        + [pack_q[:, 3 * rows]]
    )
    cut = 3 * blk // 2
    q1, q2 = net.flip_q(part_q, 1), net.flip_q(part_q, 2)
    q3_sends = q1[:cut], q2[cut:]
    q3a, q3b = net.flip_q(q3_sends[0], 2), net.flip_q(q3_sends[1], 1)
    n_con, n_proj = ratio * blk, blk
    top = n_con + n_proj
    pack_fs = net.gather_z(tie(pack[:, n_q:], pack_qs[1]))
    pack_f = net.by_z(tie(pack_fs, q3_sends))
    pack_f = pack_f.reshape(net.nf, -1, half)
    part_f = jnp.concatenate(
        [pack_f[:, :ff_rows].reshape(-1, half), pack_f[:, ff_rows : ff_rows + rows].reshape(-1, half)]
        + [
            pack_f[:, ff_rows + t * rows : ff_rows + (t + 1) * rows].reshape(-1, half)
            for t in range(1, ratio + 1)
        ]
    )
    part_f = tie(part_f, q3a, q3b)
    f1, f2 = net.flip_q(part_f, 1), net.flip_q(part_f, 2)
    f3_sends = f1[:top], f2[top:]

    vectors = net.absolute(part_q[3 * blk :], q1[3 * blk :], q2[3 * blk :], q3b[3 * blk - cut :])
    vectors = vectors.reshape(nq * net.nf, half).astype(F32)
    eight = [vectors[:, s * rows : (s + 1) * rows].reshape(width) for s in range(8)]
    q_off, v_off, proj_off, a_gain, a_shift, f_gain, f_shift, con_off = eight
    exp_off = vectors[:, 8 * rows : small_len].reshape(ff)
    vecs = jnp.concatenate(
        [
            jnp.stack([proj_off, f_gain, f_shift, con_off]),
            jnp.zeros((4, width), F32),
            exp_off.reshape(ratio, width),
            jnp.zeros((8 - ratio, width), F32),
        ]
    )

    bias = jnp.concatenate(
        [pick(q_off.reshape(2, half), c), jnp.zeros((half,), F32), pick(v_off.reshape(2, half), c)]
    )[None]
    normed_all, query, key, value, w_qkv = qkv_apply(
        place,
        (part_q, q1, q2, q3a, q3b),
        tok,
        tok_far,
        jnp.stack([a_gain, a_shift]),
        bias,
        [part_f],
    )
    att0, lse0 = attn_fwd(lo, start, query, key, value, 0, [])
    att1, lse1 = attn_fwd(lo, start, query, key, value, 1, [*f3_sends, lse0])
    att_got = net.swap(jnp.where(c == 0, att1, att0))
    f3a, f3b = net.flip_q(f3_sends[0], 2), net.flip_q(f3_sends[1], 1)
    cot_sends = net.token_sends(tie((cotangent[0], cotangent[1]), f3a, f3b))
    pieces = [part_f, f1, f2, f3a, f3b]
    pieces = pieces + [net.swap(x) for x in pieces]
    atts = (att0, att1, att_got)

    out, middle, normed_two = ffn_fwd(place, pieces, atts, tok, vecs, cot_sends)
    out_sends = net.token_sends([out[:local], out[local:]])
    out_got = net.from_chip(out_sends)

    g = net.settle(cot_sends, net.to_chip(cot_sends)).reshape(mine, width)
    keep, send, middle_grad, ag_own, ag_send, sums = ffn_bwd(
        place, pieces, atts, g, middle, normed_two, vecs, out_sends
    )
    ag_send, send, out_got = tie((ag_send, send, out_got))
    result = net.settle(out_sends, out_got)
    ag_got = net.swap(ag_send)

    got = net.swap(send)
    packs = (keep, got)
    f_sends = first_messages(place, keep, got)
    d_mixed = attn_bwd(
        place, lo, start, query, key, value, atts[:2], (lse0, lse1), ag_own, ag_got, f_sends
    )
    f_x, f_y = net.flip_q(f_sends[0], 1), net.flip_q(f_sends[1], 2)
    cut_f = keep.shape[1] // 2

    def term(r, half_row):
        rows_of = slice(half_row * cut_f, half_row * cut_f + cut_f)
        return sum(pick(x, net.q ^ r)[rows_of].astype(F32) for x in packs)

    f_more = (
        (term(1, 0) + f_y[:cut_f].astype(F32)).astype(BF),
        (term(2, 1) + f_x[:cut_f].astype(F32)).astype(BF),
    )
    e_own, e_send, qkv_grad, d_sum = qkv_bwd(place, d_mixed, normed_all, w_qkv, f_more)

    e_got = net.swap(e_send)
    f_last = net.flip_q(f_more[0], 1), net.flip_q(f_more[1], 2)
    f_sum = jnp.concatenate(
        [
            term(0, 0) + f_y[cut_f:].astype(F32) + f_last[0].astype(F32),
            term(0, 1) + f_x[cut_f:].astype(F32) + f_last[1].astype(F32),
        ]
    )
    per_f = jnp.concatenate(
        [
            f_sum[:n_con].reshape(net.nf, ff_rows, half),
            f_sum[n_con:top].reshape(net.nf, rows, half),
        ]
        + [
            f_sum[top + t * blk : top + (t + 1) * blk].reshape(net.nf, rows, half)
            for t in range(ratio)
        ],
        axis=1,
    )
    e_own, per_f = tie((e_own, per_f))
    tok_grad, vec = last_norm(
        place, e_own, e_got, tok, middle_grad, jnp.stack([a_gain, a_shift]), sums, d_sum, 3 * half
    )
    tg_sends = net.token_sends([tok_grad[0], tok_grad[1]])
    def q_term(r):
        return jnp.concatenate([pick(qkv_grad, net.q ^ r).astype(F32), pick(vec, net.q ^ r)])

    q_cut = (blk + 16) // 2
    q_sends = tie(net.scatter_one(q_term, q_cut), tg_sends)

    q_got, q_more = net.scatter_two(q_term, q_cut, q_sends, tg_sends)
    tg_sends = tie(tg_sends, q_more)
    token_grad = net.settle(tg_sends, net.from_chip(tg_sends))
    q_sum = jnp.concatenate(net.scatter_three(q_term, q_cut, q_got, q_more))
    per_core = net.scatter_z(per_f.reshape(nz, 2, -1, half), q_got)
    final = ordered(c, pick(per_core, c), net.swap(pick(per_core, 1 - c)), 0)
    con_out = jnp.concatenate([final[0, :ff_rows], final[1, :ff_rows]], axis=1)
    proj_out = jnp.concatenate(
        [final[0, ff_rows : ff_rows + rows], final[1, ff_rows : ff_rows + rows]], axis=1
    )
    exp_out = jnp.concatenate(
        [
            final[s, ff_rows + rows + t * rows : ff_rows + rows + (t + 1) * rows]
            for t in range(ratio)
            for s in range(2)
        ],
        axis=1,
    )
    q_rows, vec = q_sum[:blk].reshape(nz, 2 * rows, 3 * half), q_sum[blk:]
    for bit in range(net.bits):
        parts = q_rows.reshape(-1, 2, 2 * rows, 3 * half)
        side = (z >> bit) & 1
        away = pick(parts, 1 - side, 1)
        count = away.shape[0] * 2 * rows
        moved = net.flip_f(
            jnp.concatenate([away.reshape(count, 3 * half), vec]).astype(BF), 2 << bit
        ).astype(F32)
        q_rows = pick(parts, side, 1) + moved[:count].reshape(away.shape)
        vec = vec + moved[count:]
    q_core = q_rows.reshape(2, rows, 3 * half)
    moved = net.swap(jnp.concatenate([pick(q_core, 1 - c), vec]))
    vec = vec[:, :blk] + moved[rows:, :blk]
    final = ordered(c, pick(q_core, c), moved[:rows], 0)
    qkv_out = jnp.concatenate(
        [final[s, :, t * half : (t + 1) * half] for t in range(3) for s in range(2)], axis=1
    )
    f = 2 * z + c
    outs = lax.dynamic_slice(vec, (0, f * rows), (8, rows))
    exp_off_out = lax.dynamic_slice(vec[8 : 8 + ratio].reshape(-1), (f * ff_rows,), (ff_rows,))
    return (
        result,
        token_grad,
        qkv_out,
        outs[0],
        outs[1],
        proj_out,
        outs[2],
        outs[3],
        outs[4],
        outs[5],
        outs[6],
        exp_out,
        exp_off_out,
        con_out,
        outs[7],
    )


def solution(mesh):
    act = P("fsdp", "seq", None)
    mat = P(ALL, None)
    vec = P(ALL)
    return jax.shard_map(
        body,
        mesh=mesh,
        in_specs=(
            act, P("fsdp", "seq"), mat, vec, vec, mat, vec, vec, vec, vec, vec, mat, vec, mat, vec, act,
        ),
        out_specs=(act, act, mat, vec, vec, mat, vec, vec, vec, vec, vec, mat, vec, mat, vec),
        check_vma=False,
    )
```

```python
import functools

import jax
import jax.numpy as jnp
import numpy as np
from jax import lax
from jax.experimental import pallas as pl
from jax.experimental.pallas import tpu as pltpu
from jax.sharding import PartitionSpec as P

HD = 64
NORM_EPS = 1e-05
NEG = -1e30
B = 256
MOST_DOC = 1024
ALL = ("seq", "fsdp")
BF = jnp.bfloat16
F32 = jnp.float32
NT = (((1,), (1,)), ((), ()))
NN = (((1,), (0,)), ((), ()))
TN = (((0,), (0,)), ((), ()))
TILE = 512
SEG_ROWS = 16
COST = 1.0
ANY = pl.BlockSpec(memory_space=pl.ANY)
VM = pl.BlockSpec(memory_space=pltpu.VMEM)
SM = pl.BlockSpec(memory_space=pltpu.SMEM)


def dg(a, b, dims):
    return lax.dot_general(a, b, dims, preferred_element_type=F32)


def cost(flops):
    return pl.CostEstimate(flops=int(flops * COST), bytes_accessed=1_000_000, transcendentals=0)


def norm_tile(v):
    mean = jnp.mean(v, axis=-1, keepdims=True)
    centered = v - mean
    var = jnp.mean(centered * centered, axis=-1, keepdims=True)
    inv = lax.rsqrt(var + NORM_EPS)
    return centered * inv, inv


def fwd_kernel(lo_ref, start_ref, q_ref, k_ref, v_ref, *refs, heads, base):
    o_ref, lse_ref, qm, vt, sbuf, mx8 = refs[-6:]
    end = base + o_ref.shape[0] // B
    lane = lax.broadcasted_iota(jnp.int32, (B, 128), 1)
    kio = lax.broadcasted_iota(jnp.int32, (B, B), 0)
    qio = lax.broadcasted_iota(jnp.int32, (B, B), 1)

    def transpose_block(j, _):
        s = pl.ds(pl.multiple_of(j * B, B), B)
        for p in range(heads // 2):
            vt[128 * p : 128 * p + 128, s] = v_ref[s, 128 * p : 128 * p + 128].T
        return 0

    lax.fori_loop(lo_ref[base], end, transpose_block, 0)

    def qblock(i, _):
        qs = pl.multiple_of(i * B, B)
        rows_out = pl.ds(pl.multiple_of((i - base) * B, B), B)
        for p in range(heads // 2):
            qq = q_ref[pl.ds(qs, B), 128 * p : 128 * p + 128]
            qm[2 * p] = jnp.where(lane < 64, qq, jnp.zeros_like(qq))
            qm[2 * p + 1] = jnp.where(lane >= 64, qq, jnp.zeros_like(qq))
        st_row = start_ref[pl.ds(i, 1), :]

        def scores(j, first):
            ks = pl.multiple_of(j * B, B)
            mask = (kio + ks) >= st_row
            if first:
                mask = mask & (kio <= qio)
            slot = i - j
            for h in range(heads):
                p = h // 2
                k_blk = k_ref[pl.ds(ks, B), 128 * p : 128 * p + 128]
                st = jnp.where(mask, dg(k_blk, qm[h], NT), NEG)
                sbuf[h, slot] = st
                m8 = jnp.max(st.reshape(B // 8, 8, B), axis=0)
                mx8[h] = m8 if first else jnp.maximum(mx8[h], m8)

        scores(i, True)

        def score_step(j, c):
            scores(j, False)
            return c

        lax.fori_loop(lo_ref[i], i, score_step, 0)
        ms = [jnp.max(mx8[h], axis=0, keepdims=True) for h in range(heads)]

        def weigh(j):
            ks = pl.multiple_of(j * B, B)
            slot = i - j
            outs = []
            for h in range(heads):
                p = jnp.exp(sbuf[h, slot] - ms[h])
                l8 = jnp.sum(p.reshape(B // 8, 8, B), axis=0)
                ot = dg(vt[64 * h : 64 * h + 64, pl.ds(ks, B)], p.astype(BF), NN)
                outs.append((ot, l8))
            return outs

        def weigh_step(j, c):
            return [(a[0] + b[0], a[1] + b[1]) for a, b in zip(c, weigh(j))]

        res = lax.fori_loop(lo_ref[i], i, weigh_step, weigh(i))
        for p in range(heads // 2):
            rows = []
            for h in (2 * p, 2 * p + 1):
                total = jnp.sum(res[h][1], axis=0, keepdims=True)
                rows.append(res[h][0] * (1.0 / total))
                lse_ref[h : h + 1, rows_out] = ms[h] + jnp.log(total)
            pair = jnp.concatenate(rows, axis=0)
            o_ref[rows_out, 128 * p : 128 * p + 128] = pair.T.astype(BF)
        return 0

    lax.fori_loop(base, end, qblock, 0)


def attn_fwd(lo, start, q, k, v, part, deps):
    n, w = q.shape
    heads = w // HD
    maxb = min(n // B, (MOST_DOC + B - 2) // B + 1)
    return pl.pallas_call(
        functools.partial(fwd_kernel, heads=heads, base=part * (n // 2 // B)),
        out_shape=(
            jax.ShapeDtypeStruct((n // 2, w), BF),
            jax.ShapeDtypeStruct((8, n // 2), F32),
        ),
        in_specs=[SM] + [VM] * 4 + [ANY] * len(deps),
        out_specs=[VM] * 2,
        scratch_shapes=[
            pltpu.VMEM((heads, B, 128), BF),
            pltpu.VMEM((w, n), BF),
            pltpu.VMEM((heads, maxb, B, B), F32),
            pltpu.VMEM((heads, 8, B), F32),
        ],
        compiler_params=pltpu.CompilerParams(vmem_limit_bytes=32 * 2**20),
        cost_estimate=cost(10_000_000_000),
        name="attn_fwd",
    )(lo, start, q, k, v, *deps)


def bwd_kernel(
    place, lo_ref, start_ref, q_ref, k_ref, v_ref, o0_ref, o1_ref, lse0_ref, lse1_ref, own_ref, got_ref, *refs, heads,
):
    out_ref, qm, dm, dqa, dka, dva, dd, kt = refs[-8:]
    n = q_ref.shape[0] // B
    wide = heads * HD
    c = place[1]
    lane = lax.broadcasted_iota(jnp.int32, (B, 128), 1)
    kio = lax.broadcasted_iota(jnp.int32, (B, B), 0)
    qio = lax.broadcasted_iota(jnp.int32, (B, B), 1)
    dka[...] = jnp.zeros_like(dka)
    dva[...] = jnp.zeros_like(dva)

    def transpose_block(j, _):
        s = pl.ds(pl.multiple_of(j * B, B), B)
        for p in range(heads // 2):
            kt[128 * p : 128 * p + 128, s] = k_ref[s, 128 * p : 128 * p + 128].T
        return 0

    lax.fori_loop(0, n, transpose_block, 0)

    def qblock(i, _):
        qs = pl.multiple_of(i * B, B)
        for p in range(heads // 2):
            cs = slice(128 * p, 128 * p + 128)
            qq = q_ref[pl.ds(qs, B), cs]
            gs = pl.ds(pl.multiple_of((i % (n // 2)) * B, B), B)
            gg = jnp.where(i // (n // 2) == c, own_ref[gs, cs], got_ref[gs, cs])
            oo = jnp.where(i < n // 2, o0_ref[gs, cs], o1_ref[gs, cs])
            prod = (oo.astype(F32) * gg.astype(F32)).T
            dd[2 * p : 2 * p + 1, :] = jnp.sum(prod[:64], axis=0, keepdims=True)
            dd[2 * p + 1 : 2 * p + 2, :] = jnp.sum(prod[64:], axis=0, keepdims=True)
            z = jnp.zeros_like(qq)
            qm[2 * p] = jnp.where(lane < 64, qq, z)
            qm[2 * p + 1] = jnp.where(lane >= 64, qq, z)
            dm[2 * p] = jnp.where(lane < 64, gg, z)
            dm[2 * p + 1] = jnp.where(lane >= 64, gg, z)
        st_row = start_ref[pl.ds(i, 1), :]
        gs = pl.ds(pl.multiple_of((i % (n // 2)) * B, B), B)

        def block(j, first):
            ks = pl.multiple_of(j * B, B)
            mask = (kio + ks) >= st_row
            if first:
                mask = mask & (kio <= qio)
            for p in range(heads // 2):
                cs = slice(128 * p, 128 * p + 128)
                k_blk = k_ref[pl.ds(ks, B), cs]
                v_blk = v_ref[pl.ds(ks, B), cs]
                dvs, dks, dqs = [], [], []
                for h in (2 * p, 2 * p + 1):
                    st = dg(k_blk, qm[h], NT)
                    lse = jnp.where(i < n // 2, lse0_ref[h : h + 1, gs], lse1_ref[h : h + 1, gs])
                    pt = jnp.exp(jnp.where(mask, st, NEG) - lse)
                    dp = dg(v_blk, dm[h], NT)
                    ds = pt * (dp - dd[h : h + 1, :])
                    pb = pt.astype(BF)
                    db = ds.astype(BF)
                    dvs.append(dg(pb, dm[h], NN))
                    dks.append(dg(db, qm[h], NN))
                    dqs.append(dg(kt[64 * h : 64 * h + 64, pl.ds(ks, B)], db, NN))
                dva[pl.ds(ks, B), cs] += dvs[0] + dvs[1]
                dka[pl.ds(ks, B), cs] += dks[0] + dks[1]
                dq = jnp.concatenate(dqs, axis=0)
                if first:
                    dqa[cs, :] = dq
                else:
                    dqa[cs, :] += dq

        block(i, True)

        def step(j, c):
            block(j, False)
            return c

        lax.fori_loop(lo_ref[i], i, step, 0)
        for p in range(heads // 2):
            cs = slice(128 * p, 128 * p + 128)
            out_ref[pl.ds(qs, B), cs] = (dqa[cs, :] * 0.125).T.astype(BF)
        return 0

    lax.fori_loop(0, n, qblock, 0)

    def finish(i, _):
        s = pl.ds(pl.multiple_of(i * B, B), B)
        out_ref[s, wide : 2 * wide] = dka[s, :].astype(BF)
        out_ref[s, 2 * wide :] = dva[s, :].astype(BF)
        return 0

    lax.fori_loop(0, n, finish, 0)


def attn_bwd(place, lo, start, q, k, v, atts, lses, own, got, deps):
    n, w = q.shape
    heads = w // HD
    return pl.pallas_call(
        functools.partial(bwd_kernel, heads=heads),
        out_shape=jax.ShapeDtypeStruct((n, 3 * w), BF),
        in_specs=[SM] * 2 + [VM] * 10 + [ANY] * len(deps),
        out_specs=VM,
        scratch_shapes=[
            pltpu.VMEM((heads, B, 128), BF),
            pltpu.VMEM((heads, B, 128), BF),
            pltpu.VMEM((w, B), F32),
            pltpu.VMEM((n, w), F32),
            pltpu.VMEM((n, w), F32),
            pltpu.VMEM((8, B), F32),
            pltpu.VMEM((w, n), BF),
        ],
        compiler_params=pltpu.CompilerParams(vmem_limit_bytes=56 * 2**20),
        cost_estimate=cost(42_000_000_000),
        name="attn_bwd",
    )(place, lo, start, q, k, v, *atts, *lses, own, got, *deps)


def qkv_bwd_kernel(place, mixed, normed, w_ref, *refs):
    e_own, e_send, qg, sums = refs[-4:]
    c = place[1]
    count = e_own.shape[0]
    wide = sums.shape[1]
    step = min(512, count)
    sums[...] = jnp.zeros_like(sums)

    def push(m, _):
        s = pl.ds(pl.multiple_of(m * step, step), step)
        far = pl.ds(pl.multiple_of((1 - c) * count + m * step, step), step)
        own = pl.ds(pl.multiple_of(c * count + m * step, step), step)
        for rows in (far, own):
            sums[0:1, :] += jnp.sum(mixed[rows, :wide].astype(F32), axis=0, keepdims=True)
            sums[1:2, :] += jnp.sum(mixed[rows, 2 * wide :].astype(F32), axis=0, keepdims=True)
        e_send[s, :] = dg(mixed[far, :], w_ref[...], NT).astype(BF)
        e_own[s, :] = dg(mixed[own, :], w_ref[...], NT)
        return 0

    lax.fori_loop(0, count // step, push, 0)
    for at in range(0, 3 * wide, 256):
        cols = slice(at, min(at + 256, 3 * wide))
        grad = dg(normed[...], mixed[:, cols], TN).astype(BF)
        qg[:, :, cols] = grad.reshape(qg.shape[0], qg.shape[1], -1)


def qkv_bwd(place, mixed, normed, w_qkv, deps):
    n, d = normed.shape
    w = mixed.shape[1] // 3
    return pl.pallas_call(
        qkv_bwd_kernel,
        out_shape=(
            jax.ShapeDtypeStruct((n // 2, d), F32),
            jax.ShapeDtypeStruct((n // 2, d), BF),
            jax.ShapeDtypeStruct((4, d // 4, 3 * w), BF),
            jax.ShapeDtypeStruct((8, w), F32),
        ),
        in_specs=[SM] + [VM] * 3 + [ANY] * len(deps),
        out_specs=[VM] * 4,
        compiler_params=pltpu.CompilerParams(vmem_limit_bytes=40 * 2**20),
        cost_estimate=cost(1_000_000_000),
        name="qkv_bwd",
    )(place, mixed, normed, w_qkv, *deps)


def last_kernel(place, e_own, e_got, x_ref, mg_ref, vecs, f_sums, d_sums, out, vec, sums):
    step = pl.program_id(0)

    @pl.when(step == 0)
    def _():
        sums[...] = jnp.zeros_like(sums)
        vec[...] = jnp.zeros_like(vec)

    e = e_own[...] + e_got[...].astype(F32)
    xhat, inv = norm_tile(x_ref[0].astype(F32))
    ce = e * vecs[2:3, :]
    grad = mg_ref[...] + inv * (
        ce
        - jnp.mean(ce, axis=-1, keepdims=True)
        - xhat * jnp.mean(ce * xhat, axis=-1, keepdims=True)
    )
    out[0] = grad.astype(BF)
    sums[3:4, :] += jnp.sum(e * xhat, axis=0, keepdims=True)
    sums[4:5, :] += jnp.sum(e, axis=0, keepdims=True)

    @pl.when(step == pl.num_programs(0) - 1)
    def _():
        half = d_sums.shape[1]
        for core in range(2):

            @pl.when(place[1] == core)
            def _(core=core):
                sums[0:2, core * half : core * half + half] = d_sums[0:2, :]

        sums[2:3, :] = f_sums[0:1, :]
        sums[5:8, :] = f_sums[1:4, :]
        parts = vec.shape[0]
        blk = sums.shape[1] // parts
        for p in range(parts):
            vec[p, 0:8, 0:blk] = sums[:, p * blk : p * blk + blk]
            for t in range(parts):
                vec[p, 8 + t : 9 + t, 0:blk] = f_sums[8 + p : 9 + p, t * blk : t * blk + blk]


def last_norm(place, e_own, e_got, tok, mg, vecs, f_sums, d_sums, lanes):
    n, w = e_own.shape
    count = n // 2
    step = 256
    per = count // step
    flat = pl.BlockSpec((step, w), lambda i: (i, 0))
    block = pl.BlockSpec((1, step, w), lambda i: (i // per, i % per, 0))
    return pl.pallas_call(
        last_kernel,
        grid=(n // step,),
        out_shape=(
            jax.ShapeDtypeStruct((2, count, w), BF),
            jax.ShapeDtypeStruct((4, 16, lanes), F32),
        ),
        in_specs=[SM, flat, flat, block, flat]
        + [pl.BlockSpec(x.shape, lambda i: (0, 0)) for x in (vecs, f_sums, d_sums)],
        out_specs=[block, pl.BlockSpec((4, 16, lanes), lambda i: (0, 0, 0))],
        scratch_shapes=[pltpu.VMEM((8, w), F32)],
        compiler_params=pltpu.CompilerParams(vmem_limit_bytes=16 * 2**20),
        cost_estimate=cost(400_000_000),
        name="last_norm",
    )(place, e_own, e_got, tok, mg, vecs, f_sums, d_sums)


def add_kernel(place, keep, got, out_x, out_y):
    step = pl.program_id(0)
    total = (keep[...].astype(F32) + got[...].astype(F32)).astype(BF)

    @pl.when(step < 2)
    def _():
        out_x[...] = total

    @pl.when(step >= 2)
    def _():
        out_y[...] = total


def first_messages(place, keep, got):
    _, rows, w = keep.shape
    half = rows // 2

    def at(i, p):
        r = jnp.where(i % 2 == 0, 3, jnp.where(i < 2, 1, 2))
        return (p[0] ^ r, jnp.where(i < 2, 1, 0), 0)

    pack = pl.BlockSpec((None, half, w), at)
    message = jax.ShapeDtypeStruct((rows, w), BF)
    return pl.pallas_call(
        add_kernel,
        grid_spec=pltpu.PrefetchScalarGridSpec(
            num_scalar_prefetch=1,
            grid=(4,),
            in_specs=[pack, pack],
            out_specs=[
                pl.BlockSpec((half, w), lambda i, p: (jnp.minimum(i, 1), 0)),
                pl.BlockSpec((half, w), lambda i, p: (jnp.maximum(i - 2, 0), 0)),
            ],
        ),
        out_shape=(message, message),
        compiler_params=pltpu.CompilerParams(vmem_limit_bytes=56 * 2**20),
        cost_estimate=cost(400_000_000),
        name="first_messages",
    )(place, keep, got)


def vector_kernel(rows_ref, lane_at, row_at, out):
    count, lanes = rows_ref.shape
    width = out.shape[1]
    lane = lax.broadcasted_iota(jnp.int32, (lanes, width), 0)
    row = lax.broadcasted_iota(jnp.int32, (count, width), 0)
    for k in range(out.shape[0]):
        choose = jnp.where(lane == lane_at[k : k + 1, :], 1.0, 0.0).astype(BF)
        spread = dg(rows_ref[...], choose, NN)
        kept = jnp.where(row == row_at[k : k + 1, :], spread, 0.0)
        out[k : k + 1, :] = jnp.sum(kept, axis=0, keepdims=True)


def vector_rows(spread, rows, ff_rows, which, width):
    n = np.arange(width)
    lane_at, row_at = np.full((8, width), -1), np.full((8, width), -1)
    for i, k in enumerate(which):
        size, at = (rows, n) if k < 8 else (ff_rows, n + (k - 8) * width)
        lane_at[i] = (k if k < 8 else 8) * rows + at % size
        row_at[i] = at // size
    return pl.pallas_call(
        vector_kernel,
        out_shape=jax.ShapeDtypeStruct((8, width), F32),
        in_specs=[VM] * 3,
        out_specs=VM,
        compiler_params=pltpu.CompilerParams(vmem_limit_bytes=16 * 2**20),
        cost_estimate=cost(400_000_000),
        name="vectors",
    )(spread, jnp.asarray(lane_at, jnp.int32), jnp.asarray(row_at, jnp.int32))


def qkv_kernel(place, w0, w1, w2, w3a, w3b, own, far, vecs, *refs):
    normed, q_ref, k_ref, v_ref, w, sems = refs[-6:]
    q, c = place[0], place[1]
    blk = w.shape[0] // 4
    half = w.shape[1] // 3
    copies = []

    def add(src, rows, r, offset, part):
        start = pl.multiple_of((q ^ r) * blk + offset, 16)
        size = rows.stop - rows.start
        copies.append(
            pltpu.make_async_copy(
                src.at[rows],
                w.at[pl.ds(start, size), part * half : part * half + half],
                sems.at[len(copies)],
            )
        )

    for r, src in enumerate((w0, w1, w2)):
        for part in range(3):
            add(src, slice(part * blk, part * blk + blk), r, 0, part)
    cut = blk // 2
    add(w3a, slice(0, blk), 3, 0, 0)
    add(w3a, slice(blk, blk + cut), 3, 0, 1)
    add(w3b, slice(0, cut), 3, cut, 1)
    add(w3b, slice(cut, cut + blk), 3, 0, 2)
    for copy in copies:
        copy.start()
    for copy in copies:
        copy.wait()
    count = q_ref.shape[0] // 2
    per = count // TILE // 2
    q_bias = jnp.where(c == 0, vecs[0:1, :half], vecs[0:1, half:])
    v_bias = jnp.where(c == 0, vecs[1:2, :half], vecs[1:2, half:])

    for k, ref in enumerate((own, far)):
        base = (c if k == 0 else 1 - c) * count

        def tile(m, _, ref=ref, base=base):
            x = ref[m // per, pl.ds(pl.multiple_of((m % per) * TILE, TILE), TILE), :].astype(F32)
            xhat, _inv = norm_tile(x)
            y = (xhat * vecs[2:3, :] + vecs[3:4, :]).astype(BF)
            s = pl.ds(pl.multiple_of(base + m * TILE, TILE), TILE)
            normed[s, :] = y
            mixed = dg(y, w[...], NN)
            q_ref[s, :] = (mixed[:, :half] + q_bias).astype(BF) * BF(0.125)
            k_ref[s, :] = mixed[:, half : 2 * half].astype(BF)
            v_ref[s, :] = (mixed[:, 2 * half :] + v_bias).astype(BF)
            return 0

        lax.fori_loop(0, 2 * per, tile, 0)


def qkv_apply(place, weights, own, far, vecs, deps):
    width = own.shape[2]
    half = width // 2
    n = 4 * (own.shape[1] - SEG_ROWS)
    part = jax.ShapeDtypeStruct((n, half), BF)
    return pl.pallas_call(
        qkv_kernel,
        out_shape=(
            jax.ShapeDtypeStruct((n, width), BF),
            part,
            part,
            part,
            jax.ShapeDtypeStruct((width, 3 * half), BF),
        ),
        in_specs=[SM] + [ANY] * 5 + [VM] * 3 + [ANY] * len(deps),
        out_specs=[VM] * 5,
        scratch_shapes=[pltpu.SemaphoreType.DMA((13,))],
        compiler_params=pltpu.CompilerParams(vmem_limit_bytes=32 * 2**20),
        cost_estimate=cost(400_000_000),
        name="qkv",
    )(place, *weights, own, far, vecs, *deps)


GELU_A = 0.7978845608028654
GELU_B = 0.7978845608028654 * 0.044715


PIECES = 10


def load_parts(place, pieces, att_refs, w_con, w_exp, w_proj, att, sems):
    q, c = place[0], place[1]
    blk = w_proj.shape[1] // 4
    n_con = w_con.shape[1] // 4
    top = n_con + blk
    for core in range(2):

        @pl.when(c == core)
        def _(core=core):
            pltpu.make_async_copy(att_refs[core], att.at[core], sems.at[1]).start()
            pltpu.make_async_copy(att_refs[2], att.at[1 - core], sems.at[1]).start()

    def each(action):
        for r in range(4):
            rows = pl.ds(pl.multiple_of((q ^ r) * blk, blk), blk)
            con_rows = pl.ds(pl.multiple_of((q ^ r) * n_con, n_con), n_con)
            for k in range(2):
                a_ref = pieces[5 * k + r]
                b_ref, b_at = (a_ref, top) if r < 3 else (pieces[5 * k + 4], 0)
                action(q ^ r, c if k == 0 else 1 - c, a_ref, b_ref, b_at, rows, con_rows)

    def proj(src_q, side, a_ref, b_ref, b_at, rows, con_rows):
        pltpu.make_async_copy(a_ref.at[n_con:top], w_proj.at[side, rows], sems.at[0]).start()

    def expand(b, src_q, side, a_ref, b_ref, b_at, rows, con_rows):
        src = b_ref.at[b_at + b * blk : b_at + b * blk + blk]
        pltpu.make_async_copy(src, w_exp.at[b, side, rows], sems.at[2 + b]).start()

    def contract(src_q, side, a_ref, b_ref, b_at, rows, con_rows):
        dst = w_con.at[side, con_rows]
        pltpu.make_async_copy(a_ref.at[0:n_con], dst, sems.at[6 + src_q]).start()

    each(proj)
    each(functools.partial(expand, 0))
    each(contract)
    for b in range(1, w_exp.shape[0]):
        each(functools.partial(expand, b))


def pair(ref, *at):
    return jnp.concatenate([ref[(*at[:-1], 0, at[-1])], ref[(*at[:-1], 1, at[-1])]], axis=1)


def wait_for(ref, sem):
    pltpu.make_async_copy(ref, ref, sem).wait()


def ffn_fwd_kernel(place, *refs):
    pieces, att_refs, rest = refs[:PIECES], refs[PIECES : PIECES + 3], refs[PIECES + 3 :]
    tok, vecs = rest[:2]
    *outs, mid_out, n2_out, w_con, w_exp, w_proj, att, acc, mid, n2, res, sems, osem = refs[-14:]
    load_parts(place, pieces, att_refs, w_con, w_exp, w_proj, att, sems)
    wide = w_proj.shape[1]
    tiles = mid.shape[0] // TILE
    per = tiles // 2
    wait_for(w_proj, sems.at[0])
    wait_for(att, sems.at[1])

    def first(m, _):
        s = pl.ds(pl.multiple_of(m * TILE, TILE), TILE)
        x = tok[m // per, pl.ds(pl.multiple_of((m % per) * TILE, TILE), TILE), :]
        v = x.astype(F32) + (dg(pair(att, s), pair(w_proj, slice(None)), NN) + vecs[0:1, :])
        mid[s, :] = v
        xhat, _inv = norm_tile(v)
        n2[s, :] = (xhat * vecs[1:2, :] + vecs[2:3, :]).astype(BF)
        pltpu.make_async_copy(mid.at[s], mid_out.at[s], osem.at[0]).start()
        pltpu.make_async_copy(n2.at[s], n2_out.at[s], osem.at[1]).start()
        return 0

    lax.fori_loop(0, tiles, first, 0)
    for b in range(4):
        wait_for(w_exp.at[b], sems.at[2 + b])
        wait_for(w_con.at[:, b * wide : b * wide + wide], sems.at[6 + b])

    def second(m, _):
        s = pl.ds(pl.multiple_of(m * TILE, TILE), TILE)
        x = n2[s, :]
        for b in range(w_exp.shape[0]):
            h = dg(x, pair(w_exp, b, slice(None)), NN) + vecs[4 + b : 5 + b, :]
            th = jnp.tanh(h * (GELU_A + GELU_B * (h * h)))
            act = (h * (0.5 + 0.5 * th)).astype(BF)
            part = dg(act, pair(w_con, slice(b * wide, b * wide + wide)), NN)
            if b == 0:
                acc[...] = part
            else:
                acc[...] += part
        res[s, :] = (mid[s, :] + (acc[...] + vecs[3:4, :])).astype(BF)
        rows = pl.ds(pl.multiple_of((m % per) * TILE, TILE), TILE)
        for p in range(2):

            @pl.when((m // per) ^ (place[0] % 2) == p)
            def _(p=p):
                pltpu.make_async_copy(res.at[s], outs[p].at[rows], osem.at[2]).start()

        return 0

    lax.fori_loop(0, tiles, second, 0)
    wait_for(mid, osem.at[0])
    wait_for(n2, osem.at[1])
    wait_for(res, osem.at[2])


def ffn_bwd_kernel(place, *refs):
    pieces, att_refs, rest = refs[:PIECES], refs[PIECES : PIECES + 3], refs[PIECES + 3 :]
    g_send, g_got0, g_got1, mid_ref, n2, vecs = rest[:6]
    (
        keep, send, mgrad, ag_own, ag_send, sums,
        w_con, w_exp, w_proj, att, g, mid, act, hg, n2g, dc, de, agr, sems, osems,
    ) = refs[-20:]
    c = place[1]
    load_parts(place, pieces, att_refs, w_con, w_exp, w_proj, att, sems)
    wide = w_proj.shape[1]
    half = wide // 2
    blk = wide // 4
    blocks = w_exp.shape[0]
    tiles = n2.shape[0] // TILE
    sums[...] = jnp.zeros_like(sums)
    odd = place[0] % 2
    count = g_got0.shape[0]

    def fetch(ref, block):
        dst = g.at[pl.ds(pl.multiple_of(block * count, count), count)]
        pltpu.make_async_copy(ref, dst, sems.at[10]).start()

    pl.when(c == place[0] // 2)(functools.partial(fetch, g_send, odd))
    pl.when(c != place[0] // 2)(functools.partial(fetch, g_got0, odd))
    fetch(g_got1, 1 - odd)
    pltpu.make_async_copy(mid_ref, mid, sems.at[11]).start()
    wait_for(g, sems.at[10])

    def store(k, b):
        side = c if k % 2 == 0 else 1 - c
        if k < 2:
            src, dst = dc.at[side], (keep, send)[k].at[b, 0:wide]
        else:
            rows = pl.ds(pl.multiple_of(wide + blk + b * blk, blk), blk)
            src, dst = de.at[side], (keep, send)[k - 2].at[:, rows]
        return pltpu.make_async_copy(src, dst, osems.at[k])

    def put(ref, t, value):
        value = value.astype(BF).reshape(ref.shape[1:-1] + (256,))
        at = t * 256
        if at < half:
            ref[0, ..., at : min(at + 256, half)] = value[..., : half - at]
        if at + 256 > half:
            ref[1, ..., max(at - half, 0) : at + 256 - half] = value[..., max(half - at, 0) :]

    def block(b, _):
        con_rows = pl.ds(pl.multiple_of(b * wide, wide), wide)
        wait_for(w_exp.at[b], sems.at[2 + b])
        wait_for(w_con.at[:, con_rows], sems.at[6 + b])
        bias = vecs[pl.ds(4 + b, 1), :]

        def tile(m, _):
            s = pl.ds(pl.multiple_of(m * TILE, TILE), TILE)
            w_e = pair(w_exp, b, slice(None))
            h = dg(n2[s, :], w_e, NN) + bias
            h2 = h * h
            t1 = 0.5 + 0.5 * jnp.tanh(h * (GELU_A + GELU_B * h2))
            ac = h * t1
            act[s, :] = ac.astype(BF)
            slope = t1 + ac * (1.0 - t1) * (2 * GELU_A + 6 * GELU_B * h2)
            hid = (dg(g[s, :], pair(w_con, con_rows), NT) * slope).astype(BF)
            hg[s, :] = hid
            sums[pl.ds(8 + b, 1), :] += jnp.sum(hid.astype(F32), axis=0, keepdims=True)
            part = dg(hid, w_e, NT)
            n2g[s, :] = jnp.where(b == 0, part, n2g[s, :] + part)
            return 0

        lax.fori_loop(0, tiles, tile, 0)

        @pl.when(b > 0)
        def _():
            for k in range(4):
                store(k, b - 1).wait()

        for t in range(3):
            cols = slice(t * 256, t * 256 + 256)
            put(dc, t, dg(act[...], g[:, cols], TN))
        for k in range(2):
            store(k, b).start()
        for t in range(3):
            cols = slice(t * 256, t * 256 + 256)
            put(de, t, dg(n2[...], hg[:, cols], TN))
        for k in range(2, 4):
            store(k, b).start()
        return 0

    lax.fori_loop(0, blocks, block, 0)
    wait_for(w_proj, sems.at[0])
    wait_for(att, sems.at[1])
    wait_for(mid, sems.at[11])

    def last(m, _):
        s = pl.ds(pl.multiple_of(m * TILE, TILE), TILE)
        xhat, inv = norm_tile(mid[s, :])
        e = n2g[s, :]
        g32 = g[s, :].astype(F32)
        ce = e * vecs[1:2, :]
        mg = g32 + inv * (
            ce
            - jnp.mean(ce, axis=-1, keepdims=True)
            - xhat * jnp.mean(ce * xhat, axis=-1, keepdims=True)
        )
        mid[s, :] = mg
        pltpu.make_async_copy(mid.at[s], mgrad.at[s], osems.at[4]).start()
        branch = mg.astype(BF)
        hg[s, :] = branch
        sums[0:1, :] += jnp.sum(branch.astype(F32), axis=0, keepdims=True)
        sums[1:2, :] += jnp.sum(e * xhat, axis=0, keepdims=True)
        sums[2:3, :] += jnp.sum(e, axis=0, keepdims=True)
        sums[3:4, :] += jnp.sum(g32, axis=0, keepdims=True)
        grad = dg(branch, pair(w_proj, slice(None)), NT).astype(BF)
        agr[0, s, :] = grad[:, :half]
        agr[1, s, :] = grad[:, half:]
        return 0

    lax.fori_loop(0, tiles, last, 0)
    for k in range(4):
        store(k, blocks - 1).wait()
    ends = [
        pltpu.make_async_copy(agr.at[c], ag_own, osems.at[0]),
        pltpu.make_async_copy(agr.at[1 - c], ag_send, osems.at[1]),
        pltpu.make_async_copy(de.at[c], keep.at[:, wide : wide + blk], osems.at[2]),
        pltpu.make_async_copy(de.at[1 - c], send.at[:, wide : wide + blk], osems.at[3]),
    ]
    for copy in ends[:2]:
        copy.start()
    for t in range(3):
        cols = slice(t * 256, t * 256 + 256)
        put(de, t, dg(pair(att, slice(None)), hg[:, cols], TN))
    for copy in ends[2:]:
        copy.start()
    for copy in ends:
        copy.wait()
    wait_for(mid, osems.at[4])


def ffn_fwd(place, pieces, atts, tok, vecs, deps):
    n, w = atts[2].shape[0], tok.shape[2]
    ff = 4 * pieces[4].shape[0]
    return pl.pallas_call(
        ffn_fwd_kernel,
        out_shape=(
            jax.ShapeDtypeStruct((n // 2, w), BF),
            jax.ShapeDtypeStruct((n // 2, w), BF),
            jax.ShapeDtypeStruct((n, w), F32),
            jax.ShapeDtypeStruct((n, w), BF),
        ),
        in_specs=[SM] + [ANY] * (PIECES + 3) + [VM] * 2 + [ANY] * len(deps),
        out_specs=[ANY] * 4,
        scratch_shapes=[
            pltpu.VMEM((2, ff, w // 2), BF),
            pltpu.VMEM((ff // w, 2, w, w // 2), BF),
            pltpu.VMEM((2, w, w // 2), BF),
            pltpu.VMEM((2, n, w // 2), BF),
            pltpu.VMEM((TILE, w), F32),
            pltpu.VMEM((n, w), F32),
            pltpu.VMEM((n, w), BF),
            pltpu.VMEM((n, w), BF),
            pltpu.SemaphoreType.DMA((10,)),
            pltpu.SemaphoreType.DMA((3,)),
        ],
        compiler_params=pltpu.CompilerParams(vmem_limit_bytes=60 * 2**20),
        cost_estimate=cost(12_000_000_000),
        name="ffn_fwd",
    )(place, *pieces, *atts, tok, vecs, *deps)


def ffn_bwd(place, pieces, atts, cots, mid, n2, vecs, deps):
    n, w = n2.shape
    half = w // 2
    ff = 4 * pieces[4].shape[0]
    pack = jax.ShapeDtypeStruct((4,) + pieces[0].shape, BF)
    cut = jax.ShapeDtypeStruct((n, half), BF)
    return pl.pallas_call(
        ffn_bwd_kernel,
        out_shape=(
            pack, pack,
            jax.ShapeDtypeStruct((n, w), F32),
            cut, cut,
            jax.ShapeDtypeStruct((16, w), F32),
        ),
        in_specs=[SM] + [ANY] * (PIECES + 3 + 4) + [VM] * 2 + [ANY] * len(deps),
        out_specs=[ANY] * 5 + [VM],
        scratch_shapes=[
            pltpu.VMEM((2, ff, w // 2), BF),
            pltpu.VMEM((ff // w, 2, w, w // 2), BF),
            pltpu.VMEM((2, w, w // 2), BF),
            pltpu.VMEM((2, n, w // 2), BF),
            pltpu.VMEM((n, w), BF),
            pltpu.VMEM((n, w), F32),
            pltpu.VMEM((n, w), BF),
            pltpu.VMEM((n, w), BF),
            pltpu.VMEM((n, w), F32),
            pltpu.VMEM((2, w, half), BF),
            pltpu.VMEM((2, 4, w // 4, half), BF),
            pltpu.VMEM((2, n, half), BF),
            pltpu.SemaphoreType.DMA((12,)),
            pltpu.SemaphoreType.DMA((5,)),
        ],
        compiler_params=pltpu.CompilerParams(vmem_limit_bytes=60 * 2**20),
        cost_estimate=cost(32_000_000_000),
        name="ffn_bwd",
    )(place, *pieces, *atts, *cots, mid, n2, vecs, *deps)


def pick(array, index, axis=0):
    return lax.dynamic_index_in_dim(array, index, axis, keepdims=False)


def ordered(flag, first, second, axis):
    return jnp.stack(
        [jnp.where(flag == 1, second, first), jnp.where(flag == 1, first, second)], axis
    )


def tie(values, *others):
    return lax.optimization_barrier((values, others))[0]


class Net:
    def __init__(self):
        self.nq = lax.axis_size("seq")
        self.nf = lax.axis_size("fsdp")
        self.q = lax.axis_index("seq")
        f = lax.axis_index("fsdp")
        self.z = f // 2
        self.c = f % 2
        self.bits = (self.nf // 2).bit_length() - 1

    def permute(self, value, target):
        pairs = []
        for q in range(self.nq):
            for f in range(self.nf):
                tq, tf = target(q, f)
                pairs.append((q * self.nf + f, tq * self.nf + tf))
        return lax.ppermute(value, ALL, pairs)

    def flip_q(self, value, mask):
        return self.permute(value, lambda q, f: (q ^ mask, f))

    def flip_f(self, value, mask):
        return self.permute(value, lambda q, f: (q, f ^ mask))

    def swap(self, value):
        return self.flip_f(value, 1)

    def _token_target(self, p):
        return lambda q, f: (2 * (f % 2) + (p ^ (q % 2)), (f // 2) * 2 + q // 2)

    def _route(self, value, target):
        pairs = []
        for q in range(self.nq):
            for f in range(self.nf):
                tq, tf = target(q, f)
                if (tq, tf) != (q, f):
                    pairs.append((q * self.nf + f, tq * self.nf + tf))
        return lax.ppermute(value, ALL, pairs)

    def token_sends(self, parts):
        return [jnp.where(self.q % 2 == p, parts[0], parts[1]) for p in range(2)]

    def to_chip(self, sends):
        return [self._route(sends[p], self._token_target(p)) for p in range(2)]

    def from_chip(self, sends):
        got = []
        for p in range(2):
            forward = self._token_target(p)
            back = {}
            for q in range(self.nq):
                for f in range(self.nf):
                    back[forward(q, f)] = (q, f)
            got.append(self._route(sends[p], lambda q, f, b=back: b[(q, f)]))
        return got

    def settle(self, sends, got):
        first = jnp.where(self.c == self.q // 2, sends[0], got[0])
        return ordered(self.q % 2, first, got[1], 0)

    def gather_z(self, block):
        return [block] + [self.flip_f(block, 2 * m) for m in range(1, self.nf // 2)]

    def by_z(self, blocks):
        for bit in range(self.bits):
            flag = (self.z >> bit) & 1 == 1
            blocks = [jnp.where(flag, blocks[i ^ (1 << bit)], x) for i, x in enumerate(blocks)]
        return jnp.stack(blocks)

    def scatter_z(self, blocks, gate=()):
        shape = blocks.shape[1:]
        for bit in range(self.bits):
            parts = blocks.reshape((-1, 2) + shape)
            mine = (self.z >> bit) & 1
            got = self.flip_f(pick(parts, 1 - mine, 1).astype(BF), 2 << bit)
            if bit == 0:
                got = tie(got, gate)
            blocks = pick(parts, mine, 1).astype(F32) + got.astype(F32)
        return blocks[0]

    def absolute(self, r0, r1, r2, r3):
        odd, high = self.q % 2 == 1, self.q // 2 == 1
        x0, x1 = jnp.where(odd, r1, r0), jnp.where(odd, r0, r1)
        x2, x3 = jnp.where(odd, r3, r2), jnp.where(odd, r2, r3)
        return jnp.stack(
            [
                jnp.where(high, x2, x0),
                jnp.where(high, x3, x1),
                jnp.where(high, x0, x2),
                jnp.where(high, x1, x3),
            ]
        )

    def scatter_one(self, term, cut):
        return [
            jnp.concatenate([term(3)[cut:], term(1)[cut:]]).astype(BF),
            jnp.concatenate([term(3)[:cut], term(2)[:cut]]).astype(BF),
        ]

    def scatter_two(self, term, cut, sends, gate):
        got = tie([self.flip_q(sends[0], 1), self.flip_q(sends[1], 2)], gate)
        rest = sends[0].shape[0] // 2
        more = [
            (term(1)[:cut] + got[1][:cut].astype(F32)).astype(BF),
            (term(2)[cut:] + got[0][:rest].astype(F32)).astype(BF),
        ]
        return got, more

    def scatter_three(self, term, cut, got, more):
        last = [self.flip_q(more[0], 1), self.flip_q(more[1], 2)]
        rest = got[0].shape[0] // 2
        return (
            term(0)[:cut] + got[1][cut:].astype(F32) + last[0].astype(F32),
            term(0)[cut:] + got[0][rest:].astype(F32) + last[1].astype(F32),
        )


def body(
    tokens,
    segments,
    qkv_weight,
    query_bias,
    value_bias,
    proj_weight,
    proj_bias,
    attn_gain,
    attn_shift,
    ffn_gain,
    ffn_shift,
    expand_weight,
    expand_bias,
    contract_weight,
    contract_bias,
    cotangent,
):
    net = Net()
    c, z = net.c, net.z
    micro, local, width = tokens.shape
    rows = qkv_weight.shape[0]
    ff = expand_weight.shape[1]
    ff_rows = contract_weight.shape[0]
    ratio = ff // width
    half = width // 2
    nq, nz = net.nq, net.nf // 2
    blk = rows * net.nf
    n = 2 * micro * local
    mine = micro * local

    place = jnp.stack([net.q, c]).astype(jnp.int32)

    seg_rows = jnp.zeros((micro, SEG_ROWS, width), BF).at[:, 0, :local].set(segments.astype(BF))
    tok_send = jnp.concatenate([tokens, seg_rows], axis=1)
    tok_sends = net.token_sends([tok_send[0], tok_send[1]])
    tok_got = net.to_chip(tok_sends)
    tok = net.settle(tok_sends, tok_got)
    tok_far = net.swap(tok)
    seg = ordered(c, tok[:, local, :local], tok_far[:, local, :local], 0).reshape(n)
    seg = seg.astype(jnp.int32)
    docs = jnp.arange(32, dtype=jnp.int32)
    before = jnp.sum((seg[None, :] < docs[:, None]).astype(jnp.int32), axis=1)
    start = jnp.sum(jnp.where(seg[None, :] == docs[:, None], before[:, None], 0), axis=0)
    lo = start[::B] // B
    start = start.reshape(n // B, B)

    qkv_w, con_w, proj_w, exp_w, vector_args = tie(
        (
            qkv_weight,
            contract_weight,
            proj_weight,
            expand_weight,
            (
                query_bias,
                value_bias,
                proj_bias,
                attn_gain,
                attn_shift,
                ffn_gain,
                ffn_shift,
                contract_bias,
                expand_bias,
            ),
        ),
        tok_sends,
    )
    small_len = sum(x.shape[0] for x in vector_args)
    small, at = 0.0, 0
    for x in vector_args:
        small = small + jnp.pad(x.astype(F32), (at, half - at - x.shape[0]))
        at += x.shape[0]
    small = jnp.pad(small.astype(BF)[None], ((0, 7), (0, 0)))

    def columns(matrix, t, s):
        return matrix[:, t * width + s * half : t * width + (s + 1) * half]

    packs = [
        jnp.concatenate(
            [columns(qkv_w, t, s) for t in range(3)]
            + [small, columns(con_w, 0, s), columns(proj_w, 0, s)]
            + [columns(exp_w, t, s) for t in range(ratio)]
        )
        for s in range(2)
    ]
    pack = ordered(
        c,
        jnp.where(c == 0, packs[0], packs[1]),
        net.swap(jnp.where(c == 0, packs[1], packs[0])),
        0,
    )
    n_q = 3 * rows + 8
    pack_qs = net.gather_z(pack[:, :n_q])
    pack_q = net.by_z(tie(pack_qs, tok_got)).reshape(net.nf, n_q, half)
    part_q = jnp.concatenate(
        [pack_q[:, t * rows : (t + 1) * rows].reshape(blk, half) for t in range(3)]
        + [pack_q[:, 3 * rows]]
    )
    cut = 3 * blk // 2
    q1, q2 = net.flip_q(part_q, 1), net.flip_q(part_q, 2)
    q3_sends = q1[:cut], q2[cut:]
    q3a, q3b = net.flip_q(q3_sends[0], 2), net.flip_q(q3_sends[1], 1)
    n_con, n_proj = ratio * blk, blk
    top = n_con + n_proj
    pack_fs = net.gather_z(tie(pack[:, n_q:], pack_qs[1]))
    pack_f = net.by_z(tie(pack_fs, q3_sends))
    pack_f = pack_f.reshape(net.nf, -1, half)
    part_f = jnp.concatenate(
        [pack_f[:, :ff_rows].reshape(-1, half), pack_f[:, ff_rows : ff_rows + rows].reshape(-1, half)]
        + [
            pack_f[:, ff_rows + t * rows : ff_rows + (t + 1) * rows].reshape(-1, half)
            for t in range(1, ratio + 1)
        ]
    )
    part_f = tie(part_f, q3a, q3b)
    f1, f2 = net.flip_q(part_f, 1), net.flip_q(part_f, 2)
    f3_sends = f1[:top], f2[top:]

    spread = net.absolute(part_q[3 * blk :], q1[3 * blk :], q2[3 * blk :], q3b[3 * blk - cut :])
    spread = spread.reshape(nq * net.nf, half)
    norm_vecs = vector_rows(spread, rows, ff_rows, (0, 1, 3, 4), width)
    vecs = vector_rows(spread, rows, ff_rows, (2, 5, 6, 7, 8, 9, 10, 11), width)

    normed_all, query, key, value, w_qkv = qkv_apply(
        place,
        (part_q, q1, q2, q3a, q3b),
        tok,
        tok_far,
        norm_vecs,
        [part_f],
    )
    att0, lse0 = attn_fwd(lo, start, query, key, value, 0, [])
    att1, lse1 = attn_fwd(lo, start, query, key, value, 1, [*f3_sends, lse0])
    att_got = net.swap(jnp.where(c == 0, att1, att0))
    f3a, f3b = net.flip_q(f3_sends[0], 2), net.flip_q(f3_sends[1], 1)
    cot_sends = net.token_sends(tie((cotangent[0], cotangent[1]), f3a, f3b))
    pieces = [part_f, f1, f2, f3a, f3b]
    pieces = pieces + [net.swap(x) for x in pieces]
    atts = (att0, att1, att_got)

    *out_sends, middle, normed_two = ffn_fwd(place, pieces, atts, tok, vecs, cot_sends)
    out_got = net.from_chip(out_sends)

    cots = (cot_sends[0], *net.to_chip(cot_sends))
    keep, send, middle_grad, ag_own, ag_send, sums = ffn_bwd(
        place, pieces, atts, cots, middle, normed_two, vecs, out_sends
    )
    ag_send, send, out_got = tie((ag_send, send, out_got))
    result = net.settle(out_sends, out_got)
    ag_got = net.swap(ag_send)

    got = net.swap(send)
    packs = (keep, got)
    f_sends = first_messages(place, keep, got)
    d_mixed = attn_bwd(
        place, lo, start, query, key, value, atts[:2], (lse0, lse1), ag_own, ag_got, f_sends
    )
    f_x, f_y = tie((net.flip_q(f_sends[0], 1), net.flip_q(f_sends[1], 2)), d_mixed)
    cut_f = keep.shape[1] // 2

    def term(r, half_row):
        rows_of = slice(half_row * cut_f, half_row * cut_f + cut_f)
        return sum(pick(x, net.q ^ r)[rows_of].astype(F32) for x in packs)

    f_more = (
        (term(1, 0) + f_y[:cut_f].astype(F32)).astype(BF),
        (term(2, 1) + f_x[:cut_f].astype(F32)).astype(BF),
    )
    e_own, e_send, qkv_grad, d_sum = qkv_bwd(place, d_mixed, normed_all, w_qkv, f_more)

    e_got = net.swap(e_send)
    f_last = net.flip_q(f_more[0], 1), net.flip_q(f_more[1], 2)
    f_sum = jnp.concatenate(
        [
            term(0, 0) + f_y[cut_f:].astype(F32) + f_last[0].astype(F32),
            term(0, 1) + f_x[cut_f:].astype(F32) + f_last[1].astype(F32),
        ]
    )
    per_f = jnp.concatenate(
        [
            f_sum[:n_con].reshape(net.nf, ff_rows, half),
            f_sum[n_con:top].reshape(net.nf, rows, half),
        ]
        + [
            f_sum[top + t * blk : top + (t + 1) * blk].reshape(net.nf, rows, half)
            for t in range(ratio)
        ],
        axis=1,
    )
    e_own, per_f = tie((e_own, per_f))
    tok_grad, vec = last_norm(
        place, e_own, e_got, tok, middle_grad, norm_vecs, sums, d_sum, 3 * half
    )
    tg_sends = net.token_sends([tok_grad[0], tok_grad[1]])
    def q_term(r):
        return jnp.concatenate([pick(qkv_grad, net.q ^ r).astype(F32), pick(vec, net.q ^ r)])

    q_cut = (blk + 16) // 2
    q_sends = tie(net.scatter_one(q_term, q_cut), tg_sends)

    q_got, q_more = net.scatter_two(q_term, q_cut, q_sends, tg_sends)
    tg_sends = tie(tg_sends, q_more)
    token_grad = net.settle(tg_sends, net.from_chip(tg_sends))
    q_sum = jnp.concatenate(net.scatter_three(q_term, q_cut, q_got, q_more))
    per_core = net.scatter_z(per_f.reshape(nz, 2, -1, half), q_got)
    final = ordered(c, pick(per_core, c), net.swap(pick(per_core, 1 - c)), 0)
    con_out = jnp.concatenate([final[0, :ff_rows], final[1, :ff_rows]], axis=1)
    proj_out = jnp.concatenate(
        [final[0, ff_rows : ff_rows + rows], final[1, ff_rows : ff_rows + rows]], axis=1
    )
    exp_out = jnp.concatenate(
        [
            final[s, ff_rows + rows + t * rows : ff_rows + rows + (t + 1) * rows]
            for t in range(ratio)
            for s in range(2)
        ],
        axis=1,
    )
    q_rows, vec = q_sum[:blk].reshape(nz, 2 * rows, 3 * half), q_sum[blk:]
    for bit in range(net.bits):
        parts = q_rows.reshape(-1, 2, 2 * rows, 3 * half)
        side = (z >> bit) & 1
        away = pick(parts, 1 - side, 1)
        count = away.shape[0] * 2 * rows
        moved = net.flip_f(
            jnp.concatenate([away.reshape(count, 3 * half), vec]).astype(BF), 2 << bit
        ).astype(F32)
        q_rows = pick(parts, side, 1) + moved[:count].reshape(away.shape)
        vec = vec + moved[count:]
    q_core = q_rows.reshape(2, rows, 3 * half)
    moved = net.swap(jnp.concatenate([pick(q_core, 1 - c), vec]))
    vec = vec[:, :blk] + moved[rows:, :blk]
    final = ordered(c, pick(q_core, c), moved[:rows], 0)
    qkv_out = jnp.concatenate(
        [final[s, :, t * half : (t + 1) * half] for t in range(3) for s in range(2)], axis=1
    )
    f = 2 * z + c
    outs = lax.dynamic_slice(vec, (0, f * rows), (8, rows))
    exp_off_out = lax.dynamic_slice(vec[8 : 8 + ratio].reshape(-1), (f * ff_rows,), (ff_rows,))
    return (
        result,
        token_grad,
        qkv_out,
        outs[0],
        outs[1],
        proj_out,
        outs[2],
        outs[3],
        outs[4],
        outs[5],
        outs[6],
        exp_out,
        exp_off_out,
        con_out,
        outs[7],
    )


def solution(mesh):
    act = P("fsdp", "seq", None)
    mat = P(ALL, None)
    vec = P(ALL)
    return jax.shard_map(
        body,
        mesh=mesh,
        in_specs=(
            act, P("fsdp", "seq"), mat, vec, vec, mat, vec, vec, vec, vec, vec, mat, vec, mat, vec, act,
        ),
        out_specs=(act, act, mat, vec, vec, mat, vec, vec, vec, vec, vec, mat, vec, mat, vec),
        check_vma=False,
    )
```

```python
import functools

import jax
import jax.numpy as jnp
import numpy as np
from jax import lax
from jax.experimental import pallas as pl
from jax.experimental.pallas import tpu as pltpu
from jax.sharding import PartitionSpec as P

HD = 64
NORM_EPS = 1e-05
NEG = -1e30
B = 256
MOST_DOC = 1024
ALL = ("seq", "fsdp")
BF = jnp.bfloat16
F32 = jnp.float32
NT = (((1,), (1,)), ((), ()))
NN = (((1,), (0,)), ((), ()))
TN = (((0,), (0,)), ((), ()))
TILE = 512
SEG_ROWS = 16
COST = 1.0
ANY = pl.BlockSpec(memory_space=pl.ANY)
VM = pl.BlockSpec(memory_space=pltpu.VMEM)
SM = pl.BlockSpec(memory_space=pltpu.SMEM)


def dg(a, b, dims):
    return lax.dot_general(a, b, dims, preferred_element_type=F32)


def cost(flops):
    return pl.CostEstimate(flops=int(flops * COST), bytes_accessed=1_000_000, transcendentals=0)


def norm_tile(v):
    mean = jnp.mean(v, axis=-1, keepdims=True)
    centered = v - mean
    var = jnp.mean(centered * centered, axis=-1, keepdims=True)
    inv = lax.rsqrt(var + NORM_EPS)
    return centered * inv, inv


def fwd_kernel(lo_ref, start_ref, q_ref, k_ref, v_ref, *refs, heads, base):
    o_ref, lse_ref, qm, vt, sbuf, mx8, acc, sum8 = refs[-8:]
    end = base + o_ref.shape[0] // B
    lane = lax.broadcasted_iota(jnp.int32, (B, 128), 1)

    def transpose_block(j, _):
        s = pl.ds(pl.multiple_of(j * B, B), B)
        for p in range(heads // 2):
            vt[128 * p : 128 * p + 128, s] = v_ref[s, 128 * p : 128 * p + 128].T
        return 0

    lax.fori_loop(lo_ref[base], end, transpose_block, 0)

    def qblock(i, _):
        qs = pl.multiple_of(i * B, B)
        rows_out = pl.ds(pl.multiple_of((i - base) * B, B), B)
        for p in range(heads // 2):
            qq = q_ref[pl.ds(qs, B), 128 * p : 128 * p + 128]
            qm[2 * p] = jnp.where(lane < 64, qq, jnp.zeros_like(qq))
            qm[2 * p + 1] = jnp.where(lane >= 64, qq, jnp.zeros_like(qq))
        st_row = start_ref[pl.ds(i, 1), :]

        low = lo_ref[i]
        rest = jnp.maximum(i - low - 1, 0)

        def each(body):
            pl.when(low < i)(lambda: body(i - 1, 2, True))
            pl.when(low == i)(lambda: body(i, 1, True))

            def step(t, c):
                body(low + 2 * t, 2, False)
                return c

            lax.fori_loop(0, rest // 2, step, 0)
            pl.when(rest % 2 == 1)(lambda: body(i - 2, 1, False))

        def scores(j, count, first):
            ks = pl.multiple_of(j * B, B)
            held = pl.ds(pl.multiple_of((j - low) * B, B), count * B)
            kpos = lax.broadcasted_iota(jnp.int32, (count * B, B), 0) + ks
            mask = kpos >= st_row
            if first:
                mask = mask & (kpos - qs <= lax.broadcasted_iota(jnp.int32, (count * B, B), 1))
            for h in range(heads):
                p = h // 2
                k_blk = k_ref[pl.ds(ks, count * B), 128 * p : 128 * p + 128]
                st = jnp.where(mask, dg(k_blk, qm[h], NT), NEG)
                sbuf[h, held, :] = st
                m8 = jnp.max(st.reshape(count * B // 8, 8, B), axis=0)
                mx8[h] = m8 if first else jnp.maximum(mx8[h], m8)

        each(scores)
        ms = [jnp.max(mx8[h], axis=0, keepdims=True) for h in range(heads)]

        def weigh(j, count, first):
            ks = pl.multiple_of(j * B, B)
            held = pl.ds(pl.multiple_of((j - low) * B, B), count * B)
            for h in range(heads):
                p = jnp.exp(sbuf[h, held, :] - ms[h])
                l8 = jnp.sum(p.reshape(count * B // 8, 8, B), axis=0)
                ot = dg(vt[64 * h : 64 * h + 64, pl.ds(ks, count * B)], p.astype(BF), NN)
                acc[h] = ot if first else acc[h] + ot
                sum8[h] = l8 if first else sum8[h] + l8

        each(weigh)
        for p in range(heads // 2):
            rows = []
            for h in (2 * p, 2 * p + 1):
                total = jnp.sum(sum8[h], axis=0, keepdims=True)
                rows.append(acc[h] * (1.0 / total))
                lse_ref[h : h + 1, rows_out] = ms[h] + jnp.log(total)
            pair = jnp.concatenate(rows, axis=0)
            o_ref[rows_out, 128 * p : 128 * p + 128] = pair.T.astype(BF)
        return 0

    lax.fori_loop(base, end, qblock, 0)


def attn_fwd(lo, start, q, k, v, part, deps):
    n, w = q.shape
    heads = w // HD
    maxb = min(n // B, (MOST_DOC + B - 2) // B + 1)
    return pl.pallas_call(
        functools.partial(fwd_kernel, heads=heads, base=part * (n // 2 // B)),
        out_shape=(
            jax.ShapeDtypeStruct((n // 2, w), BF),
            jax.ShapeDtypeStruct((8, n // 2), F32),
        ),
        in_specs=[SM] + [VM] * 4 + [ANY] * len(deps),
        out_specs=[VM] * 2,
        scratch_shapes=[
            pltpu.VMEM((heads, B, 128), BF),
            pltpu.VMEM((w, n), BF),
            pltpu.VMEM((heads, maxb * B, B), F32),
            pltpu.VMEM((heads, 8, B), F32),
            pltpu.VMEM((heads, HD, B), F32),
            pltpu.VMEM((heads, 8, B), F32),
        ],
        compiler_params=pltpu.CompilerParams(vmem_limit_bytes=32 * 2**20),
        cost_estimate=cost(10_000_000_000),
        name="attn_fwd",
    )(lo, start, q, k, v, *deps)


def bwd_kernel(
    place, lo_ref, start_ref, q_ref, k_ref, v_ref, o0_ref, o1_ref, lse0_ref, lse1_ref, own_ref, got_ref, *refs, heads,
):
    out_ref, qm, dm, dqa, dka, dva, dd, kt = refs[-8:]
    n = q_ref.shape[0] // B
    wide = heads * HD
    c = place[1]
    lane = lax.broadcasted_iota(jnp.int32, (B, 128), 1)
    dka[...] = jnp.zeros_like(dka)
    dva[...] = jnp.zeros_like(dva)

    def transpose_block(j, _):
        s = pl.ds(pl.multiple_of(j * B, B), B)
        for p in range(heads // 2):
            kt[128 * p : 128 * p + 128, s] = k_ref[s, 128 * p : 128 * p + 128].T
        return 0

    lax.fori_loop(0, n, transpose_block, 0)

    def qblock(i, _):
        qs = pl.multiple_of(i * B, B)
        for p in range(heads // 2):
            cs = slice(128 * p, 128 * p + 128)
            qq = q_ref[pl.ds(qs, B), cs]
            gs = pl.ds(pl.multiple_of((i % (n // 2)) * B, B), B)
            gg = jnp.where(i // (n // 2) == c, own_ref[gs, cs], got_ref[gs, cs])
            oo = jnp.where(i < n // 2, o0_ref[gs, cs], o1_ref[gs, cs])
            prod = (oo.astype(F32) * gg.astype(F32)).T
            dd[2 * p : 2 * p + 1, :] = jnp.sum(prod[:64], axis=0, keepdims=True)
            dd[2 * p + 1 : 2 * p + 2, :] = jnp.sum(prod[64:], axis=0, keepdims=True)
            z = jnp.zeros_like(qq)
            qm[2 * p] = jnp.where(lane < 64, qq, z)
            qm[2 * p + 1] = jnp.where(lane >= 64, qq, z)
            dm[2 * p] = jnp.where(lane < 64, gg, z)
            dm[2 * p + 1] = jnp.where(lane >= 64, gg, z)
        st_row = start_ref[pl.ds(i, 1), :]
        gs = pl.ds(pl.multiple_of((i % (n // 2)) * B, B), B)

        def block(j, count, first):
            ks = pl.multiple_of(j * B, B)
            rows = pl.ds(ks, count * B)
            kpos = lax.broadcasted_iota(jnp.int32, (count * B, B), 0) + ks
            mask = kpos >= st_row
            if first:
                mask = mask & (kpos - qs <= lax.broadcasted_iota(jnp.int32, (count * B, B), 1))
            for p in range(heads // 2):
                cs = slice(128 * p, 128 * p + 128)
                k_blk = k_ref[rows, cs]
                v_blk = v_ref[rows, cs]
                dvs, dks, dqs = [], [], []
                for h in (2 * p, 2 * p + 1):
                    st = dg(k_blk, qm[h], NT)
                    lse = jnp.where(i < n // 2, lse0_ref[h : h + 1, gs], lse1_ref[h : h + 1, gs])
                    pt = jnp.exp(jnp.where(mask, st, NEG) - lse)
                    dp = dg(v_blk, dm[h], NT)
                    ds = pt * (dp - dd[h : h + 1, :])
                    pb = pt.astype(BF)
                    db = ds.astype(BF)
                    dvs.append(dg(pb, dm[h], NN))
                    dks.append(dg(db, qm[h], NN))
                    dqs.append(dg(kt[64 * h : 64 * h + 64, rows], db, NN))
                dva[rows, cs] += dvs[0] + dvs[1]
                dka[rows, cs] += dks[0] + dks[1]
                dq = jnp.concatenate(dqs, axis=0)
                if first:
                    dqa[cs, :] = dq
                else:
                    dqa[cs, :] += dq

        low = lo_ref[i]
        rest = jnp.maximum(i - low - 1, 0)
        pl.when(low < i)(lambda: block(i - 1, 2, True))
        pl.when(low == i)(lambda: block(i, 1, True))

        def step(t, c):
            block(low + 2 * t, 2, False)
            return c

        lax.fori_loop(0, rest // 2, step, 0)
        pl.when(rest % 2 == 1)(lambda: block(i - 2, 1, False))
        for p in range(heads // 2):
            cs = slice(128 * p, 128 * p + 128)
            out_ref[pl.ds(qs, B), cs] = (dqa[cs, :] * 0.125).T.astype(BF)
        return 0

    lax.fori_loop(0, n, qblock, 0)

    def finish(i, _):
        s = pl.ds(pl.multiple_of(i * B, B), B)
        out_ref[s, wide : 2 * wide] = dka[s, :].astype(BF)
        out_ref[s, 2 * wide :] = dva[s, :].astype(BF)
        return 0

    lax.fori_loop(0, n, finish, 0)


def attn_bwd(place, lo, start, q, k, v, atts, lses, own, got, deps):
    n, w = q.shape
    heads = w // HD
    return pl.pallas_call(
        functools.partial(bwd_kernel, heads=heads),
        out_shape=jax.ShapeDtypeStruct((n, 3 * w), BF),
        in_specs=[SM] * 2 + [VM] * 10 + [ANY] * len(deps),
        out_specs=VM,
        scratch_shapes=[
            pltpu.VMEM((heads, B, 128), BF),
            pltpu.VMEM((heads, B, 128), BF),
            pltpu.VMEM((w, B), F32),
            pltpu.VMEM((n, w), F32),
            pltpu.VMEM((n, w), F32),
            pltpu.VMEM((8, B), F32),
            pltpu.VMEM((w, n), BF),
        ],
        compiler_params=pltpu.CompilerParams(vmem_limit_bytes=56 * 2**20),
        cost_estimate=cost(42_000_000_000),
        name="attn_bwd",
    )(place, lo, start, q, k, v, *atts, *lses, own, got, *deps)


def qkv_bwd_kernel(place, mixed, normed, w_ref, *refs):
    e_own, e_send, qg, sums = refs[-4:]
    c = place[1]
    count = e_own.shape[0]
    wide = sums.shape[1]
    step = min(512, count)
    sums[...] = jnp.zeros_like(sums)

    def push(m, _):
        s = pl.ds(pl.multiple_of(m * step, step), step)
        far = pl.ds(pl.multiple_of((1 - c) * count + m * step, step), step)
        own = pl.ds(pl.multiple_of(c * count + m * step, step), step)
        for rows in (far, own):
            sums[0:1, :] += jnp.sum(mixed[rows, :wide].astype(F32), axis=0, keepdims=True)
            sums[1:2, :] += jnp.sum(mixed[rows, 2 * wide :].astype(F32), axis=0, keepdims=True)
        e_send[s, :] = dg(mixed[far, :], w_ref[...], NT).astype(BF)
        e_own[s, :] = dg(mixed[own, :], w_ref[...], NT)
        return 0

    lax.fori_loop(0, count // step, push, 0)
    for at in range(0, 3 * wide, 256):
        cols = slice(at, min(at + 256, 3 * wide))
        grad = dg(normed[...], mixed[:, cols], TN).astype(BF)
        qg[:, :, cols] = grad.reshape(qg.shape[0], qg.shape[1], -1)


def qkv_bwd(place, mixed, normed, w_qkv, deps):
    n, d = normed.shape
    w = mixed.shape[1] // 3
    return pl.pallas_call(
        qkv_bwd_kernel,
        out_shape=(
            jax.ShapeDtypeStruct((n // 2, d), F32),
            jax.ShapeDtypeStruct((n // 2, d), BF),
            jax.ShapeDtypeStruct((4, d // 4, 3 * w), BF),
            jax.ShapeDtypeStruct((8, w), F32),
        ),
        in_specs=[SM] + [VM] * 3 + [ANY] * len(deps),
        out_specs=[VM] * 4,
        compiler_params=pltpu.CompilerParams(vmem_limit_bytes=40 * 2**20),
        cost_estimate=cost(1_000_000_000),
        name="qkv_bwd",
    )(place, mixed, normed, w_qkv, *deps)


def last_kernel(place, e_own, e_got, x_ref, mg_ref, vecs, f_sums, d_sums, out, vec, sums):
    step = pl.program_id(0)

    @pl.when(step == 0)
    def _():
        sums[...] = jnp.zeros_like(sums)
        vec[...] = jnp.zeros_like(vec)

    e = e_own[...] + e_got[...].astype(F32)
    xhat, inv = norm_tile(x_ref[0].astype(F32))
    ce = e * vecs[2:3, :]
    grad = mg_ref[...] + inv * (
        ce
        - jnp.mean(ce, axis=-1, keepdims=True)
        - xhat * jnp.mean(ce * xhat, axis=-1, keepdims=True)
    )
    out[0] = grad.astype(BF)
    sums[3:4, :] += jnp.sum(e * xhat, axis=0, keepdims=True)
    sums[4:5, :] += jnp.sum(e, axis=0, keepdims=True)

    @pl.when(step == pl.num_programs(0) - 1)
    def _():
        half = d_sums.shape[1]
        for core in range(2):

            @pl.when(place[1] == core)
            def _(core=core):
                sums[0:2, core * half : core * half + half] = d_sums[0:2, :]

        sums[2:3, :] = f_sums[0:1, :]
        sums[5:8, :] = f_sums[1:4, :]
        parts = vec.shape[0]
        blk = sums.shape[1] // parts
        for p in range(parts):
            vec[p, 0:8, 0:blk] = sums[:, p * blk : p * blk + blk]
            for t in range(parts):
                vec[p, 8 + t : 9 + t, 0:blk] = f_sums[8 + p : 9 + p, t * blk : t * blk + blk]


def last_norm(place, e_own, e_got, tok, mg, vecs, f_sums, d_sums, lanes):
    n, w = e_own.shape
    count = n // 2
    step = 256
    per = count // step
    flat = pl.BlockSpec((step, w), lambda i: (i, 0))
    block = pl.BlockSpec((1, step, w), lambda i: (i // per, i % per, 0))
    return pl.pallas_call(
        last_kernel,
        grid=(n // step,),
        out_shape=(
            jax.ShapeDtypeStruct((2, count, w), BF),
            jax.ShapeDtypeStruct((4, 16, lanes), F32),
        ),
        in_specs=[SM, flat, flat, block, flat]
        + [pl.BlockSpec(x.shape, lambda i: (0, 0)) for x in (vecs, f_sums, d_sums)],
        out_specs=[block, pl.BlockSpec((4, 16, lanes), lambda i: (0, 0, 0))],
        scratch_shapes=[pltpu.VMEM((8, w), F32)],
        compiler_params=pltpu.CompilerParams(vmem_limit_bytes=16 * 2**20),
        cost_estimate=cost(400_000_000),
        name="last_norm",
    )(place, e_own, e_got, tok, mg, vecs, f_sums, d_sums)


def add_kernel(place, keep, got, out_x, out_y):
    step = pl.program_id(0)
    total = (keep[...].astype(F32) + got[...].astype(F32)).astype(BF)

    @pl.when(step < 2)
    def _():
        out_x[...] = total

    @pl.when(step >= 2)
    def _():
        out_y[...] = total


def first_messages(place, keep, got):
    _, rows, w = keep.shape
    half = rows // 2

    def at(i, p):
        r = jnp.where(i % 2 == 0, 3, jnp.where(i < 2, 1, 2))
        return (p[0] ^ r, jnp.where(i < 2, 1, 0), 0)

    pack = pl.BlockSpec((None, half, w), at)
    message = jax.ShapeDtypeStruct((rows, w), BF)
    return pl.pallas_call(
        add_kernel,
        grid_spec=pltpu.PrefetchScalarGridSpec(
            num_scalar_prefetch=1,
            grid=(4,),
            in_specs=[pack, pack],
            out_specs=[
                pl.BlockSpec((half, w), lambda i, p: (jnp.minimum(i, 1), 0)),
                pl.BlockSpec((half, w), lambda i, p: (jnp.maximum(i - 2, 0), 0)),
            ],
        ),
        out_shape=(message, message),
        compiler_params=pltpu.CompilerParams(vmem_limit_bytes=56 * 2**20),
        cost_estimate=cost(400_000_000),
        name="first_messages",
    )(place, keep, got)


def vector_kernel(rows_ref, lane_at, row_at, out):
    count, lanes = rows_ref.shape
    width = out.shape[1]
    lane = lax.broadcasted_iota(jnp.int32, (lanes, width), 0)
    row = lax.broadcasted_iota(jnp.int32, (count, width), 0)
    for k in range(out.shape[0]):
        choose = jnp.where(lane == lane_at[k : k + 1, :], 1.0, 0.0).astype(BF)
        spread = dg(rows_ref[...], choose, NN)
        kept = jnp.where(row == row_at[k : k + 1, :], spread, 0.0)
        out[k : k + 1, :] = jnp.sum(kept, axis=0, keepdims=True)


def vector_rows(spread, rows, ff_rows, which, width):
    n = np.arange(width)
    lane_at, row_at = np.full((8, width), -1), np.full((8, width), -1)
    for i, k in enumerate(which):
        size, at = (rows, n) if k < 8 else (ff_rows, n + (k - 8) * width)
        lane_at[i] = (k if k < 8 else 8) * rows + at % size
        row_at[i] = at // size
    return pl.pallas_call(
        vector_kernel,
        out_shape=jax.ShapeDtypeStruct((8, width), F32),
        in_specs=[VM] * 3,
        out_specs=VM,
        compiler_params=pltpu.CompilerParams(vmem_limit_bytes=16 * 2**20),
        cost_estimate=cost(400_000_000),
        name="vectors",
    )(spread, jnp.asarray(lane_at, jnp.int32), jnp.asarray(row_at, jnp.int32))


def qkv_kernel(place, w0, w1, w2, w3a, w3b, own, far, vecs, *refs):
    normed, q_ref, k_ref, v_ref, w, sems = refs[-6:]
    q, c = place[0], place[1]
    blk = w.shape[0] // 4
    half = w.shape[1] // 3
    copies = []

    def add(src, rows, r, offset, part):
        start = pl.multiple_of((q ^ r) * blk + offset, 16)
        size = rows.stop - rows.start
        copies.append(
            pltpu.make_async_copy(
                src.at[rows],
                w.at[pl.ds(start, size), part * half : part * half + half],
                sems.at[len(copies)],
            )
        )

    for r, src in enumerate((w0, w1, w2)):
        for part in range(3):
            add(src, slice(part * blk, part * blk + blk), r, 0, part)
    cut = blk // 2
    add(w3a, slice(0, blk), 3, 0, 0)
    add(w3a, slice(blk, blk + cut), 3, 0, 1)
    add(w3b, slice(0, cut), 3, cut, 1)
    add(w3b, slice(cut, cut + blk), 3, 0, 2)
    for copy in copies:
        copy.start()
    for copy in copies:
        copy.wait()
    count = q_ref.shape[0] // 2
    per = count // TILE // 2
    q_bias = jnp.where(c == 0, vecs[0:1, :half], vecs[0:1, half:])
    v_bias = jnp.where(c == 0, vecs[1:2, :half], vecs[1:2, half:])

    for k, ref in enumerate((own, far)):
        base = (c if k == 0 else 1 - c) * count

        def tile(m, _, ref=ref, base=base):
            x = ref[m // per, pl.ds(pl.multiple_of((m % per) * TILE, TILE), TILE), :].astype(F32)
            xhat, _inv = norm_tile(x)
            y = (xhat * vecs[2:3, :] + vecs[3:4, :]).astype(BF)
            s = pl.ds(pl.multiple_of(base + m * TILE, TILE), TILE)
            normed[s, :] = y
            mixed = dg(y, w[...], NN)
            q_ref[s, :] = (mixed[:, :half] + q_bias).astype(BF) * BF(0.125)
            k_ref[s, :] = mixed[:, half : 2 * half].astype(BF)
            v_ref[s, :] = (mixed[:, 2 * half :] + v_bias).astype(BF)
            return 0

        lax.fori_loop(0, 2 * per, tile, 0)


def qkv_apply(place, weights, own, far, vecs, deps):
    width = own.shape[2]
    half = width // 2
    n = 4 * (own.shape[1] - SEG_ROWS)
    part = jax.ShapeDtypeStruct((n, half), BF)
    return pl.pallas_call(
        qkv_kernel,
        out_shape=(
            jax.ShapeDtypeStruct((n, width), BF),
            part,
            part,
            part,
            jax.ShapeDtypeStruct((width, 3 * half), BF),
        ),
        in_specs=[SM] + [ANY] * 5 + [VM] * 3 + [ANY] * len(deps),
        out_specs=[VM] * 5,
        scratch_shapes=[pltpu.SemaphoreType.DMA((13,))],
        compiler_params=pltpu.CompilerParams(vmem_limit_bytes=32 * 2**20),
        cost_estimate=cost(400_000_000),
        name="qkv",
    )(place, *weights, own, far, vecs, *deps)


GELU_A = 0.7978845608028654
GELU_B = 0.7978845608028654 * 0.044715


PIECES = 10


def load_parts(place, pieces, att_refs, w_con, w_exp, w_proj, att, sems):
    q, c = place[0], place[1]
    blk = w_proj.shape[1] // 4
    n_con = w_con.shape[1] // 4
    top = n_con + blk
    for core in range(2):

        @pl.when(c == core)
        def _(core=core):
            pltpu.make_async_copy(att_refs[core], att.at[core], sems.at[1]).start()
            pltpu.make_async_copy(att_refs[2], att.at[1 - core], sems.at[1]).start()

    def each(action):
        for r in range(4):
            rows = pl.ds(pl.multiple_of((q ^ r) * blk, blk), blk)
            con_rows = pl.ds(pl.multiple_of((q ^ r) * n_con, n_con), n_con)
            for k in range(2):
                a_ref = pieces[5 * k + r]
                b_ref, b_at = (a_ref, top) if r < 3 else (pieces[5 * k + 4], 0)
                action(q ^ r, c if k == 0 else 1 - c, a_ref, b_ref, b_at, rows, con_rows)

    def proj(src_q, side, a_ref, b_ref, b_at, rows, con_rows):
        pltpu.make_async_copy(a_ref.at[n_con:top], w_proj.at[side, rows], sems.at[0]).start()

    def expand(b, src_q, side, a_ref, b_ref, b_at, rows, con_rows):
        src = b_ref.at[b_at + b * blk : b_at + b * blk + blk]
        pltpu.make_async_copy(src, w_exp.at[b, side, rows], sems.at[2 + b]).start()

    def contract(src_q, side, a_ref, b_ref, b_at, rows, con_rows):
        dst = w_con.at[side, con_rows]
        pltpu.make_async_copy(a_ref.at[0:n_con], dst, sems.at[6 + src_q]).start()

    each(proj)
    each(functools.partial(expand, 0))
    each(contract)
    for b in range(1, w_exp.shape[0]):
        each(functools.partial(expand, b))


def pair(ref, *at):
    return jnp.concatenate([ref[(*at[:-1], 0, at[-1])], ref[(*at[:-1], 1, at[-1])]], axis=1)


def wait_for(ref, sem):
    pltpu.make_async_copy(ref, ref, sem).wait()


def ffn_fwd_kernel(place, *refs):
    pieces, att_refs, rest = refs[:PIECES], refs[PIECES : PIECES + 3], refs[PIECES + 3 :]
    tok, vecs = rest[:2]
    *outs, mid_out, n2_out, w_con, w_exp, w_proj, att, acc, mid, n2, res, sems, osem = refs[-14:]
    load_parts(place, pieces, att_refs, w_con, w_exp, w_proj, att, sems)
    wide = w_proj.shape[1]
    tiles = mid.shape[0] // TILE
    per = tiles // 2
    wait_for(w_proj, sems.at[0])
    wait_for(att, sems.at[1])

    def first(m, _):
        s = pl.ds(pl.multiple_of(m * TILE, TILE), TILE)
        x = tok[m // per, pl.ds(pl.multiple_of((m % per) * TILE, TILE), TILE), :]
        v = x.astype(F32) + (dg(pair(att, s), pair(w_proj, slice(None)), NN) + vecs[0:1, :])
        mid[s, :] = v
        xhat, _inv = norm_tile(v)
        n2[s, :] = (xhat * vecs[1:2, :] + vecs[2:3, :]).astype(BF)
        pltpu.make_async_copy(mid.at[s], mid_out.at[s], osem.at[0]).start()
        pltpu.make_async_copy(n2.at[s], n2_out.at[s], osem.at[1]).start()
        return 0

    lax.fori_loop(0, tiles, first, 0)
    for b in range(4):
        wait_for(w_exp.at[b], sems.at[2 + b])
        wait_for(w_con.at[:, b * wide : b * wide + wide], sems.at[6 + b])

    def second(m, _):
        s = pl.ds(pl.multiple_of(m * TILE, TILE), TILE)
        x = n2[s, :]
        for b in range(w_exp.shape[0]):
            h = dg(x, pair(w_exp, b, slice(None)), NN) + vecs[4 + b : 5 + b, :]
            th = jnp.tanh(h * (GELU_A + GELU_B * (h * h)))
            act = (h * (0.5 + 0.5 * th)).astype(BF)
            part = dg(act, pair(w_con, slice(b * wide, b * wide + wide)), NN)
            if b == 0:
                acc[...] = part
            else:
                acc[...] += part
        res[s, :] = (mid[s, :] + (acc[...] + vecs[3:4, :])).astype(BF)
        rows = pl.ds(pl.multiple_of((m % per) * TILE, TILE), TILE)
        for p in range(2):

            @pl.when((m // per) ^ (place[0] % 2) == p)
            def _(p=p):
                pltpu.make_async_copy(res.at[s], outs[p].at[rows], osem.at[2]).start()

        return 0

    lax.fori_loop(0, tiles, second, 0)
    wait_for(mid, osem.at[0])
    wait_for(n2, osem.at[1])
    wait_for(res, osem.at[2])


def ffn_bwd_kernel(place, *refs):
    pieces, att_refs, rest = refs[:PIECES], refs[PIECES : PIECES + 3], refs[PIECES + 3 :]
    g_send, g_got0, g_got1, mid_ref, n2, vecs = rest[:6]
    (
        keep, send, mgrad, ag_own, ag_send, sums,
        w_con, w_exp, w_proj, att, g, mid, act, hg, n2g, dc, de, agr, sems, osems,
    ) = refs[-20:]
    c = place[1]
    load_parts(place, pieces, att_refs, w_con, w_exp, w_proj, att, sems)
    wide = w_proj.shape[1]
    half = wide // 2
    blk = wide // 4
    blocks = w_exp.shape[0]
    tiles = n2.shape[0] // TILE
    sums[...] = jnp.zeros_like(sums)
    odd = place[0] % 2
    count = g_got0.shape[0]

    def fetch(ref, block):
        dst = g.at[pl.ds(pl.multiple_of(block * count, count), count)]
        pltpu.make_async_copy(ref, dst, sems.at[10]).start()

    pl.when(c == place[0] // 2)(functools.partial(fetch, g_send, odd))
    pl.when(c != place[0] // 2)(functools.partial(fetch, g_got0, odd))
    fetch(g_got1, 1 - odd)
    pltpu.make_async_copy(mid_ref, mid, sems.at[11]).start()
    wait_for(g, sems.at[10])

    def store(k, b):
        side = c if k % 2 == 0 else 1 - c
        if k < 2:
            src, dst = dc.at[side], (keep, send)[k].at[b, 0:wide]
        else:
            rows = pl.ds(pl.multiple_of(wide + blk + b * blk, blk), blk)
            src, dst = de.at[side], (keep, send)[k - 2].at[:, rows]
        return pltpu.make_async_copy(src, dst, osems.at[k])

    def put(ref, t, value):
        value = value.astype(BF).reshape(ref.shape[1:-1] + (256,))
        at = t * 256
        if at < half:
            ref[0, ..., at : min(at + 256, half)] = value[..., : half - at]
        if at + 256 > half:
            ref[1, ..., max(at - half, 0) : at + 256 - half] = value[..., max(half - at, 0) :]

    def block(b, _):
        con_rows = pl.ds(pl.multiple_of(b * wide, wide), wide)
        wait_for(w_exp.at[b], sems.at[2 + b])
        wait_for(w_con.at[:, con_rows], sems.at[6 + b])
        bias = vecs[pl.ds(4 + b, 1), :]

        def tile(m, _):
            s = pl.ds(pl.multiple_of(m * TILE, TILE), TILE)
            w_e = pair(w_exp, b, slice(None))
            h = dg(n2[s, :], w_e, NN) + bias
            h2 = h * h
            t1 = 0.5 + 0.5 * jnp.tanh(h * (GELU_A + GELU_B * h2))
            ac = h * t1
            act[s, :] = ac.astype(BF)
            slope = t1 + ac * (1.0 - t1) * (2 * GELU_A + 6 * GELU_B * h2)
            hid = (dg(g[s, :], pair(w_con, con_rows), NT) * slope).astype(BF)
            hg[s, :] = hid
            sums[pl.ds(8 + b, 1), :] += jnp.sum(hid.astype(F32), axis=0, keepdims=True)
            part = dg(hid, w_e, NT)
            n2g[s, :] = jnp.where(b == 0, part, n2g[s, :] + part)
            return 0

        lax.fori_loop(0, tiles, tile, 0)

        @pl.when(b > 0)
        def _():
            for k in range(4):
                store(k, b - 1).wait()

        for t in range(3):
            cols = slice(t * 256, t * 256 + 256)
            put(dc, t, dg(act[...], g[:, cols], TN))
        for k in range(2):
            store(k, b).start()
        for t in range(3):
            cols = slice(t * 256, t * 256 + 256)
            put(de, t, dg(n2[...], hg[:, cols], TN))
        for k in range(2, 4):
            store(k, b).start()
        return 0

    lax.fori_loop(0, blocks, block, 0)
    wait_for(w_proj, sems.at[0])
    wait_for(att, sems.at[1])
    wait_for(mid, sems.at[11])

    def last(m, _):
        s = pl.ds(pl.multiple_of(m * TILE, TILE), TILE)
        xhat, inv = norm_tile(mid[s, :])
        e = n2g[s, :]
        g32 = g[s, :].astype(F32)
        ce = e * vecs[1:2, :]
        mg = g32 + inv * (
            ce
            - jnp.mean(ce, axis=-1, keepdims=True)
            - xhat * jnp.mean(ce * xhat, axis=-1, keepdims=True)
        )
        mid[s, :] = mg
        pltpu.make_async_copy(mid.at[s], mgrad.at[s], osems.at[4]).start()
        branch = mg.astype(BF)
        hg[s, :] = branch
        sums[0:1, :] += jnp.sum(branch.astype(F32), axis=0, keepdims=True)
        sums[1:2, :] += jnp.sum(e * xhat, axis=0, keepdims=True)
        sums[2:3, :] += jnp.sum(e, axis=0, keepdims=True)
        sums[3:4, :] += jnp.sum(g32, axis=0, keepdims=True)
        grad = dg(branch, pair(w_proj, slice(None)), NT).astype(BF)
        agr[0, s, :] = grad[:, :half]
        agr[1, s, :] = grad[:, half:]
        return 0

    lax.fori_loop(0, tiles, last, 0)
    for k in range(4):
        store(k, blocks - 1).wait()
    ends = [
        pltpu.make_async_copy(agr.at[c], ag_own, osems.at[0]),
        pltpu.make_async_copy(agr.at[1 - c], ag_send, osems.at[1]),
        pltpu.make_async_copy(de.at[c], keep.at[:, wide : wide + blk], osems.at[2]),
        pltpu.make_async_copy(de.at[1 - c], send.at[:, wide : wide + blk], osems.at[3]),
    ]
    for copy in ends[:2]:
        copy.start()
    for t in range(3):
        cols = slice(t * 256, t * 256 + 256)
        put(de, t, dg(pair(att, slice(None)), hg[:, cols], TN))
    for copy in ends[2:]:
        copy.start()
    for copy in ends:
        copy.wait()
    wait_for(mid, osems.at[4])


def ffn_fwd(place, pieces, atts, tok, vecs, deps):
    n, w = atts[2].shape[0], tok.shape[2]
    ff = 4 * pieces[4].shape[0]
    return pl.pallas_call(
        ffn_fwd_kernel,
        out_shape=(
            jax.ShapeDtypeStruct((n // 2, w), BF),
            jax.ShapeDtypeStruct((n // 2, w), BF),
            jax.ShapeDtypeStruct((n, w), F32),
            jax.ShapeDtypeStruct((n, w), BF),
        ),
        in_specs=[SM] + [ANY] * (PIECES + 3) + [VM] * 2 + [ANY] * len(deps),
        out_specs=[ANY] * 4,
        scratch_shapes=[
            pltpu.VMEM((2, ff, w // 2), BF),
            pltpu.VMEM((ff // w, 2, w, w // 2), BF),
            pltpu.VMEM((2, w, w // 2), BF),
            pltpu.VMEM((2, n, w // 2), BF),
            pltpu.VMEM((TILE, w), F32),
            pltpu.VMEM((n, w), F32),
            pltpu.VMEM((n, w), BF),
            pltpu.VMEM((n, w), BF),
            pltpu.SemaphoreType.DMA((10,)),
            pltpu.SemaphoreType.DMA((3,)),
        ],
        compiler_params=pltpu.CompilerParams(vmem_limit_bytes=60 * 2**20),
        cost_estimate=cost(12_000_000_000),
        name="ffn_fwd",
    )(place, *pieces, *atts, tok, vecs, *deps)


def ffn_bwd(place, pieces, atts, cots, mid, n2, vecs, deps):
    n, w = n2.shape
    half = w // 2
    ff = 4 * pieces[4].shape[0]
    pack = jax.ShapeDtypeStruct((4,) + pieces[0].shape, BF)
    cut = jax.ShapeDtypeStruct((n, half), BF)
    return pl.pallas_call(
        ffn_bwd_kernel,
        out_shape=(
            pack, pack,
            jax.ShapeDtypeStruct((n, w), F32),
            cut, cut,
            jax.ShapeDtypeStruct((16, w), F32),
        ),
        in_specs=[SM] + [ANY] * (PIECES + 3 + 4) + [VM] * 2 + [ANY] * len(deps),
        out_specs=[ANY] * 5 + [VM],
        scratch_shapes=[
            pltpu.VMEM((2, ff, w // 2), BF),
            pltpu.VMEM((ff // w, 2, w, w // 2), BF),
            pltpu.VMEM((2, w, w // 2), BF),
            pltpu.VMEM((2, n, w // 2), BF),
            pltpu.VMEM((n, w), BF),
            pltpu.VMEM((n, w), F32),
            pltpu.VMEM((n, w), BF),
            pltpu.VMEM((n, w), BF),
            pltpu.VMEM((n, w), F32),
            pltpu.VMEM((2, w, half), BF),
            pltpu.VMEM((2, 4, w // 4, half), BF),
            pltpu.VMEM((2, n, half), BF),
            pltpu.SemaphoreType.DMA((12,)),
            pltpu.SemaphoreType.DMA((5,)),
        ],
        compiler_params=pltpu.CompilerParams(vmem_limit_bytes=60 * 2**20),
        cost_estimate=cost(32_000_000_000),
        name="ffn_bwd",
    )(place, *pieces, *atts, *cots, mid, n2, vecs, *deps)


def pick(array, index, axis=0):
    return lax.dynamic_index_in_dim(array, index, axis, keepdims=False)


def ordered(flag, first, second, axis):
    return jnp.stack(
        [jnp.where(flag == 1, second, first), jnp.where(flag == 1, first, second)], axis
    )


def tie(values, *others):
    return lax.optimization_barrier((values, others))[0]


class Net:
    def __init__(self):
        self.nq = lax.axis_size("seq")
        self.nf = lax.axis_size("fsdp")
        self.q = lax.axis_index("seq")
        f = lax.axis_index("fsdp")
        self.z = f // 2
        self.c = f % 2
        self.bits = (self.nf // 2).bit_length() - 1

    def permute(self, value, target):
        pairs = []
        for q in range(self.nq):
            for f in range(self.nf):
                tq, tf = target(q, f)
                pairs.append((q * self.nf + f, tq * self.nf + tf))
        return lax.ppermute(value, ALL, pairs)

    def flip_q(self, value, mask):
        return self.permute(value, lambda q, f: (q ^ mask, f))

    def flip_f(self, value, mask):
        return self.permute(value, lambda q, f: (q, f ^ mask))

    def swap(self, value):
        return self.flip_f(value, 1)

    def _token_target(self, p):
        return lambda q, f: (2 * (f % 2) + (p ^ (q % 2)), (f // 2) * 2 + q // 2)

    def _route(self, value, target):
        pairs = []
        for q in range(self.nq):
            for f in range(self.nf):
                tq, tf = target(q, f)
                if (tq, tf) != (q, f):
                    pairs.append((q * self.nf + f, tq * self.nf + tf))
        return lax.ppermute(value, ALL, pairs)

    def token_sends(self, parts):
        return [jnp.where(self.q % 2 == p, parts[0], parts[1]) for p in range(2)]

    def to_chip(self, sends):
        return [self._route(sends[p], self._token_target(p)) for p in range(2)]

    def from_chip(self, sends):
        got = []
        for p in range(2):
            forward = self._token_target(p)
            back = {}
            for q in range(self.nq):
                for f in range(self.nf):
                    back[forward(q, f)] = (q, f)
            got.append(self._route(sends[p], lambda q, f, b=back: b[(q, f)]))
        return got

    def settle(self, sends, got):
        first = jnp.where(self.c == self.q // 2, sends[0], got[0])
        return ordered(self.q % 2, first, got[1], 0)

    def gather_z(self, block):
        return [block] + [self.flip_f(block, 2 * m) for m in range(1, self.nf // 2)]

    def by_z(self, blocks):
        for bit in range(self.bits):
            flag = (self.z >> bit) & 1 == 1
            blocks = [jnp.where(flag, blocks[i ^ (1 << bit)], x) for i, x in enumerate(blocks)]
        return jnp.stack(blocks)

    def scatter_z(self, blocks, gate=()):
        shape = blocks.shape[1:]
        for bit in range(self.bits):
            parts = blocks.reshape((-1, 2) + shape)
            mine = (self.z >> bit) & 1
            got = self.flip_f(pick(parts, 1 - mine, 1).astype(BF), 2 << bit)
            if bit == 0:
                got = tie(got, gate)
            blocks = pick(parts, mine, 1).astype(F32) + got.astype(F32)
        return blocks[0]

    def absolute(self, r0, r1, r2, r3):
        odd, high = self.q % 2 == 1, self.q // 2 == 1
        x0, x1 = jnp.where(odd, r1, r0), jnp.where(odd, r0, r1)
        x2, x3 = jnp.where(odd, r3, r2), jnp.where(odd, r2, r3)
        return jnp.stack(
            [
                jnp.where(high, x2, x0),
                jnp.where(high, x3, x1),
                jnp.where(high, x0, x2),
                jnp.where(high, x1, x3),
            ]
        )

    def scatter_one(self, term, cut):
        return [
            jnp.concatenate([term(3)[cut:], term(1)[cut:]]).astype(BF),
            jnp.concatenate([term(3)[:cut], term(2)[:cut]]).astype(BF),
        ]

    def scatter_two(self, term, cut, sends, gate):
        got = tie([self.flip_q(sends[0], 1), self.flip_q(sends[1], 2)], gate)
        rest = sends[0].shape[0] // 2
        more = [
            (term(1)[:cut] + got[1][:cut].astype(F32)).astype(BF),
            (term(2)[cut:] + got[0][:rest].astype(F32)).astype(BF),
        ]
        return got, more

    def scatter_three(self, term, cut, got, more):
        last = [self.flip_q(more[0], 1), self.flip_q(more[1], 2)]
        rest = got[0].shape[0] // 2
        return (
            term(0)[:cut] + got[1][cut:].astype(F32) + last[0].astype(F32),
            term(0)[cut:] + got[0][rest:].astype(F32) + last[1].astype(F32),
        )


def body(
    tokens,
    segments,
    qkv_weight,
    query_bias,
    value_bias,
    proj_weight,
    proj_bias,
    attn_gain,
    attn_shift,
    ffn_gain,
    ffn_shift,
    expand_weight,
    expand_bias,
    contract_weight,
    contract_bias,
    cotangent,
):
    net = Net()
    c, z = net.c, net.z
    micro, local, width = tokens.shape
    rows = qkv_weight.shape[0]
    ff = expand_weight.shape[1]
    ff_rows = contract_weight.shape[0]
    ratio = ff // width
    half = width // 2
    nq, nz = net.nq, net.nf // 2
    blk = rows * net.nf
    n = 2 * micro * local
    mine = micro * local

    place = jnp.stack([net.q, c]).astype(jnp.int32)

    seg_rows = jnp.zeros((micro, SEG_ROWS, width), BF).at[:, 0, :local].set(segments.astype(BF))
    tok_send = jnp.concatenate([tokens, seg_rows], axis=1)
    tok_sends = net.token_sends([tok_send[0], tok_send[1]])
    tok_got = net.to_chip(tok_sends)
    tok = net.settle(tok_sends, tok_got)
    tok_far = net.swap(tok)
    seg = ordered(c, tok[:, local, :local], tok_far[:, local, :local], 0).reshape(n)
    seg = seg.astype(jnp.int32)
    docs = jnp.arange(32, dtype=jnp.int32)
    before = jnp.sum((seg[None, :] < docs[:, None]).astype(jnp.int32), axis=1)
    start = jnp.sum(jnp.where(seg[None, :] == docs[:, None], before[:, None], 0), axis=0)
    lo = start[::B] // B
    start = start.reshape(n // B, B)

    qkv_w, con_w, proj_w, exp_w, vector_args = tie(
        (
            qkv_weight,
            contract_weight,
            proj_weight,
            expand_weight,
            (
                query_bias,
                value_bias,
                proj_bias,
                attn_gain,
                attn_shift,
                ffn_gain,
                ffn_shift,
                contract_bias,
                expand_bias,
            ),
        ),
        tok_sends,
    )
    small_len = sum(x.shape[0] for x in vector_args)
    small, at = 0.0, 0
    for x in vector_args:
        small = small + jnp.pad(x.astype(F32), (at, half - at - x.shape[0]))
        at += x.shape[0]
    small = jnp.pad(small.astype(BF)[None], ((0, 7), (0, 0)))

    def columns(matrix, t, s):
        return matrix[:, t * width + s * half : t * width + (s + 1) * half]

    packs = [
        jnp.concatenate(
            [columns(qkv_w, t, s) for t in range(3)]
            + [small, columns(con_w, 0, s), columns(proj_w, 0, s)]
            + [columns(exp_w, t, s) for t in range(ratio)]
        )
        for s in range(2)
    ]
    pack = ordered(
        c,
        jnp.where(c == 0, packs[0], packs[1]),
        net.swap(jnp.where(c == 0, packs[1], packs[0])),
        0,
    )
    n_q = 3 * rows + 8
    pack_qs = net.gather_z(pack[:, :n_q])
    pack_q = net.by_z(tie(pack_qs, tok_got)).reshape(net.nf, n_q, half)
    part_q = jnp.concatenate(
        [pack_q[:, t * rows : (t + 1) * rows].reshape(blk, half) for t in range(3)]
        + [pack_q[:, 3 * rows]]
    )
    cut = 3 * blk // 2
    q1, q2 = net.flip_q(part_q, 1), net.flip_q(part_q, 2)
    q3_sends = q1[:cut], q2[cut:]
    q3a, q3b = net.flip_q(q3_sends[0], 2), net.flip_q(q3_sends[1], 1)
    n_con, n_proj = ratio * blk, blk
    top = n_con + n_proj
    pack_fs = net.gather_z(tie(pack[:, n_q:], pack_qs[1]))
    pack_f = net.by_z(tie(pack_fs, q3_sends))
    pack_f = pack_f.reshape(net.nf, -1, half)
    part_f = jnp.concatenate(
        [pack_f[:, :ff_rows].reshape(-1, half), pack_f[:, ff_rows : ff_rows + rows].reshape(-1, half)]
        + [
            pack_f[:, ff_rows + t * rows : ff_rows + (t + 1) * rows].reshape(-1, half)
            for t in range(1, ratio + 1)
        ]
    )
    part_f = tie(part_f, q3a, q3b)
    f1, f2 = net.flip_q(part_f, 1), net.flip_q(part_f, 2)
    f3_sends = f1[:top], f2[top:]

    spread = net.absolute(part_q[3 * blk :], q1[3 * blk :], q2[3 * blk :], q3b[3 * blk - cut :])
    spread = spread.reshape(nq * net.nf, half)
    norm_vecs = vector_rows(spread, rows, ff_rows, (0, 1, 3, 4), width)
    vecs = vector_rows(spread, rows, ff_rows, (2, 5, 6, 7, 8, 9, 10, 11), width)

    normed_all, query, key, value, w_qkv = qkv_apply(
        place,
        (part_q, q1, q2, q3a, q3b),
        tok,
        tok_far,
        norm_vecs,
        [part_f],
    )
    att0, lse0 = attn_fwd(lo, start, query, key, value, 0, [])
    att1, lse1 = attn_fwd(lo, start, query, key, value, 1, [*f3_sends, lse0])
    att_got = net.swap(jnp.where(c == 0, att1, att0))
    f3a, f3b = net.flip_q(f3_sends[0], 2), net.flip_q(f3_sends[1], 1)
    cot_sends = net.token_sends(tie((cotangent[0], cotangent[1]), f3a, f3b))
    pieces = [part_f, f1, f2, f3a, f3b]
    pieces = pieces + [net.swap(x) for x in pieces]
    atts = (att0, att1, att_got)

    *out_sends, middle, normed_two = ffn_fwd(place, pieces, atts, tok, vecs, cot_sends)
    out_got = net.from_chip(out_sends)

    cots = (cot_sends[0], *net.to_chip(cot_sends))
    keep, send, middle_grad, ag_own, ag_send, sums = ffn_bwd(
        place, pieces, atts, cots, middle, normed_two, vecs, out_sends
    )
    ag_send, send, out_got = tie((ag_send, send, out_got))
    result = net.settle(out_sends, out_got)
    ag_got = net.swap(ag_send)

    got = net.swap(send)
    packs = (keep, got)
    f_sends = first_messages(place, keep, got)
    d_mixed = attn_bwd(
        place, lo, start, query, key, value, atts[:2], (lse0, lse1), ag_own, ag_got, f_sends
    )
    f_x, f_y = tie((net.flip_q(f_sends[0], 1), net.flip_q(f_sends[1], 2)), d_mixed)
    cut_f = keep.shape[1] // 2

    def term(r, half_row):
        rows_of = slice(half_row * cut_f, half_row * cut_f + cut_f)
        return sum(pick(x, net.q ^ r)[rows_of].astype(F32) for x in packs)

    f_more = (
        (term(1, 0) + f_y[:cut_f].astype(F32)).astype(BF),
        (term(2, 1) + f_x[:cut_f].astype(F32)).astype(BF),
    )
    e_own, e_send, qkv_grad, d_sum = qkv_bwd(place, d_mixed, normed_all, w_qkv, f_more)

    e_got = net.swap(e_send)
    f_last = net.flip_q(f_more[0], 1), net.flip_q(f_more[1], 2)
    f_sum = jnp.concatenate(
        [
            term(0, 0) + f_y[cut_f:].astype(F32) + f_last[0].astype(F32),
            term(0, 1) + f_x[cut_f:].astype(F32) + f_last[1].astype(F32),
        ]
    )
    per_f = jnp.concatenate(
        [
            f_sum[:n_con].reshape(net.nf, ff_rows, half),
            f_sum[n_con:top].reshape(net.nf, rows, half),
        ]
        + [
            f_sum[top + t * blk : top + (t + 1) * blk].reshape(net.nf, rows, half)
            for t in range(ratio)
        ],
        axis=1,
    )
    e_own, per_f = tie((e_own, per_f))
    tok_grad, vec = last_norm(
        place, e_own, e_got, tok, middle_grad, norm_vecs, sums, d_sum, 3 * half
    )
    tg_sends = net.token_sends([tok_grad[0], tok_grad[1]])
    def q_term(r):
        return jnp.concatenate([pick(qkv_grad, net.q ^ r).astype(F32), pick(vec, net.q ^ r)])

    q_cut = (blk + 16) // 2
    q_sends = tie(net.scatter_one(q_term, q_cut), tg_sends)

    q_got, q_more = net.scatter_two(q_term, q_cut, q_sends, tg_sends)
    tg_sends = tie(tg_sends, q_more)
    token_grad = net.settle(tg_sends, net.from_chip(tg_sends))
    q_sum = jnp.concatenate(net.scatter_three(q_term, q_cut, q_got, q_more))
    q_rows, vec = q_sum[:blk].reshape(nz, 2 * rows, 3 * half), q_sum[blk:]

    def split(bit):
        parts = q_rows.reshape(-1, 2, 2 * rows, 3 * half)
        side = (z >> bit) & 1
        away = pick(parts, 1 - side, 1).reshape(-1, 3 * half)
        return pick(parts, side, 1), jnp.concatenate([away, vec]).astype(BF)

    q_kept, q_away = split(0)
    per_core = net.scatter_z(per_f.reshape(nz, 2, -1, half), q_away)
    final = ordered(c, pick(per_core, c), net.swap(pick(per_core, 1 - c)), 0)
    con_out = jnp.concatenate([final[0, :ff_rows], final[1, :ff_rows]], axis=1)
    proj_out = jnp.concatenate(
        [final[0, ff_rows : ff_rows + rows], final[1, ff_rows : ff_rows + rows]], axis=1
    )
    exp_out = jnp.concatenate(
        [
            final[s, ff_rows + rows + t * rows : ff_rows + rows + (t + 1) * rows]
            for t in range(ratio)
            for s in range(2)
        ],
        axis=1,
    )
    for bit in range(net.bits):
        if bit:
            q_kept, q_away = split(bit)
        moved = net.flip_f(q_away, 2 << bit).astype(F32)
        count = moved.shape[0] - vec.shape[0]
        q_rows = q_kept + moved[:count].reshape(q_kept.shape)
        vec = vec + moved[count:]
    q_core = q_rows.reshape(2, rows, 3 * half)
    moved = net.swap(jnp.concatenate([pick(q_core, 1 - c), vec]))
    vec = vec[:, :blk] + moved[rows:, :blk]
    final = ordered(c, pick(q_core, c), moved[:rows], 0)
    qkv_out = jnp.concatenate(
        [final[s, :, t * half : (t + 1) * half] for t in range(3) for s in range(2)], axis=1
    )
    f = 2 * z + c
    outs = lax.dynamic_slice(vec, (0, f * rows), (8, rows))
    exp_off_out = lax.dynamic_slice(vec[8 : 8 + ratio].reshape(-1), (f * ff_rows,), (ff_rows,))
    return (
        result,
        token_grad,
        qkv_out,
        outs[0],
        outs[1],
        proj_out,
        outs[2],
        outs[3],
        outs[4],
        outs[5],
        outs[6],
        exp_out,
        exp_off_out,
        con_out,
        outs[7],
    )


def solution(mesh):
    act = P("fsdp", "seq", None)
    mat = P(ALL, None)
    vec = P(ALL)
    return jax.shard_map(
        body,
        mesh=mesh,
        in_specs=(
            act, P("fsdp", "seq"), mat, vec, vec, mat, vec, vec, vec, vec, vec, mat, vec, mat, vec, act,
        ),
        out_specs=(act, act, mat, vec, vec, mat, vec, vec, vec, vec, vec, mat, vec, mat, vec),
        check_vma=False,
    )
```

```python
import functools

import jax
import jax.numpy as jnp
import numpy as np
from jax import lax
from jax.experimental import pallas as pl
from jax.experimental.pallas import tpu as pltpu
from jax.sharding import PartitionSpec as P

HD = 64
NORM_EPS = 1e-05
NEG = -1e30
B = 256
MOST_DOC = 1024
ALL = ("seq", "fsdp")
BF = jnp.bfloat16
F32 = jnp.float32
NT = (((1,), (1,)), ((), ()))
NN = (((1,), (0,)), ((), ()))
TN = (((0,), (0,)), ((), ()))
TILE = 512
SEG_ROWS = 16
COST = 1.0
ANY = pl.BlockSpec(memory_space=pl.ANY)
VM = pl.BlockSpec(memory_space=pltpu.VMEM)
SM = pl.BlockSpec(memory_space=pltpu.SMEM)


def dg(a, b, dims):
    return lax.dot_general(a, b, dims, preferred_element_type=F32)


def cost(flops):
    return pl.CostEstimate(flops=int(flops * COST), bytes_accessed=1_000_000, transcendentals=0)


def norm_tile(v):
    mean = jnp.mean(v, axis=-1, keepdims=True)
    centered = v - mean
    var = jnp.mean(centered * centered, axis=-1, keepdims=True)
    inv = lax.rsqrt(var + NORM_EPS)
    return centered * inv, inv


def fwd_kernel(lo_ref, start_ref, q_ref, k_ref, v_ref, *refs, heads, base):
    o_ref, lse_ref, qm, vt, sbuf, mx8, acc, sum8 = refs[-8:]
    end = base + o_ref.shape[0] // B
    lane = lax.broadcasted_iota(jnp.int32, (B, 128), 1)

    def transpose_block(j, _):
        s = pl.ds(pl.multiple_of(j * B, B), B)
        for p in range(heads // 2):
            vt[128 * p : 128 * p + 128, s] = v_ref[s, 128 * p : 128 * p + 128].T
        return 0

    lax.fori_loop(lo_ref[base], end, transpose_block, 0)

    def qblock(i, _):
        qs = pl.multiple_of(i * B, B)
        rows_out = pl.ds(pl.multiple_of((i - base) * B, B), B)
        for p in range(heads // 2):
            qq = q_ref[pl.ds(qs, B), 128 * p : 128 * p + 128]
            qm[2 * p] = jnp.where(lane < 64, qq, jnp.zeros_like(qq))
            qm[2 * p + 1] = jnp.where(lane >= 64, qq, jnp.zeros_like(qq))
        st_row = start_ref[pl.ds(i, 1), :]

        low = lo_ref[i]
        rest = jnp.maximum(i - low - 1, 0)

        def each(body):
            pl.when(low < i)(lambda: body(i - 1, 2, True))
            pl.when(low == i)(lambda: body(i, 1, True))

            def step(t, c):
                body(low + 2 * t, 2, False)
                return c

            lax.fori_loop(0, rest // 2, step, 0)
            pl.when(rest % 2 == 1)(lambda: body(i - 2, 1, False))

        def scores(j, count, first):
            ks = pl.multiple_of(j * B, B)
            held = pl.ds(pl.multiple_of((j - low) * B, B), count * B)
            kpos = lax.broadcasted_iota(jnp.int32, (count * B, B), 0) + ks
            mask = kpos >= st_row
            if first:
                mask = mask & (kpos - qs <= lax.broadcasted_iota(jnp.int32, (count * B, B), 1))
            for h in range(heads):
                p = h // 2
                k_blk = k_ref[pl.ds(ks, count * B), 128 * p : 128 * p + 128]
                st = jnp.where(mask, dg(k_blk, qm[h], NT), NEG)
                sbuf[h, held, :] = st
                m8 = jnp.max(st.reshape(count * B // 8, 8, B), axis=0)
                mx8[h] = m8 if first else jnp.maximum(mx8[h], m8)

        each(scores)
        ms = [jnp.max(mx8[h], axis=0, keepdims=True) for h in range(heads)]

        def weigh(j, count, first):
            ks = pl.multiple_of(j * B, B)
            held = pl.ds(pl.multiple_of((j - low) * B, B), count * B)
            for h in range(heads):
                p = jnp.exp(sbuf[h, held, :] - ms[h])
                l8 = jnp.sum(p.reshape(count * B // 8, 8, B), axis=0)
                ot = dg(vt[64 * h : 64 * h + 64, pl.ds(ks, count * B)], p.astype(BF), NN)
                acc[h] = ot if first else acc[h] + ot
                sum8[h] = l8 if first else sum8[h] + l8

        each(weigh)
        for p in range(heads // 2):
            rows = []
            for h in (2 * p, 2 * p + 1):
                total = jnp.sum(sum8[h], axis=0, keepdims=True)
                rows.append(acc[h] * (1.0 / total))
                lse_ref[h : h + 1, rows_out] = ms[h] + jnp.log(total)
            pair = jnp.concatenate(rows, axis=0)
            o_ref[rows_out, 128 * p : 128 * p + 128] = pair.T.astype(BF)
        return 0

    lax.fori_loop(base, end, qblock, 0)


def attn_fwd(lo, start, q, k, v, part, deps):
    n, w = q.shape
    heads = w // HD
    maxb = min(n // B, (MOST_DOC + B - 2) // B + 1)
    return pl.pallas_call(
        functools.partial(fwd_kernel, heads=heads, base=part * (n // 2 // B)),
        out_shape=(
            jax.ShapeDtypeStruct((n // 2, w), BF),
            jax.ShapeDtypeStruct((8, n // 2), F32),
        ),
        in_specs=[SM] + [VM] * 4 + [ANY] * len(deps),
        out_specs=[VM] * 2,
        scratch_shapes=[
            pltpu.VMEM((heads, B, 128), BF),
            pltpu.VMEM((w, n), BF),
            pltpu.VMEM((heads, maxb * B, B), F32),
            pltpu.VMEM((heads, 8, B), F32),
            pltpu.VMEM((heads, HD, B), F32),
            pltpu.VMEM((heads, 8, B), F32),
        ],
        compiler_params=pltpu.CompilerParams(vmem_limit_bytes=32 * 2**20),
        cost_estimate=cost(10_000_000_000),
        name="attn_fwd",
    )(lo, start, q, k, v, *deps)


def bwd_kernel(
    place, lo_ref, start_ref, q_ref, k_ref, v_ref, o0_ref, o1_ref, lse0_ref, lse1_ref, own_ref, got_ref, *refs, heads,
):
    out_ref, qm, dm, dqa, dka, dva, dd, kt = refs[-8:]
    n = q_ref.shape[0] // B
    wide = heads * HD
    c = place[1]
    lane = lax.broadcasted_iota(jnp.int32, (B, 128), 1)
    dka[...] = jnp.zeros_like(dka)
    dva[...] = jnp.zeros_like(dva)

    def transpose_block(j, _):
        s = pl.ds(pl.multiple_of(j * B, B), B)
        for p in range(heads // 2):
            kt[128 * p : 128 * p + 128, s] = k_ref[s, 128 * p : 128 * p + 128].T
        return 0

    lax.fori_loop(0, n, transpose_block, 0)

    def qblock(i, _):
        qs = pl.multiple_of(i * B, B)
        for p in range(heads // 2):
            cs = slice(128 * p, 128 * p + 128)
            qq = q_ref[pl.ds(qs, B), cs]
            gs = pl.ds(pl.multiple_of((i % (n // 2)) * B, B), B)
            gg = jnp.where(i // (n // 2) == c, own_ref[gs, cs], got_ref[gs, cs])
            oo = jnp.where(i < n // 2, o0_ref[gs, cs], o1_ref[gs, cs])
            prod = (oo.astype(F32) * gg.astype(F32)).T
            dd[2 * p : 2 * p + 1, :] = jnp.sum(prod[:64], axis=0, keepdims=True)
            dd[2 * p + 1 : 2 * p + 2, :] = jnp.sum(prod[64:], axis=0, keepdims=True)
            z = jnp.zeros_like(qq)
            qm[2 * p] = jnp.where(lane < 64, qq, z)
            qm[2 * p + 1] = jnp.where(lane >= 64, qq, z)
            dm[2 * p] = jnp.where(lane < 64, gg, z)
            dm[2 * p + 1] = jnp.where(lane >= 64, gg, z)
        st_row = start_ref[pl.ds(i, 1), :]
        gs = pl.ds(pl.multiple_of((i % (n // 2)) * B, B), B)

        def block(j, count, first):
            ks = pl.multiple_of(j * B, B)
            rows = pl.ds(ks, count * B)
            kpos = lax.broadcasted_iota(jnp.int32, (count * B, B), 0) + ks
            mask = kpos >= st_row
            if first:
                mask = mask & (kpos - qs <= lax.broadcasted_iota(jnp.int32, (count * B, B), 1))
            for p in range(heads // 2):
                cs = slice(128 * p, 128 * p + 128)
                k_blk = k_ref[rows, cs]
                v_blk = v_ref[rows, cs]
                dvs, dks, dqs = [], [], []
                for h in (2 * p, 2 * p + 1):
                    st = dg(k_blk, qm[h], NT)
                    lse = jnp.where(i < n // 2, lse0_ref[h : h + 1, gs], lse1_ref[h : h + 1, gs])
                    pt = jnp.exp(jnp.where(mask, st, NEG) - lse)
                    dp = dg(v_blk, dm[h], NT)
                    ds = pt * (dp - dd[h : h + 1, :])
                    pb = pt.astype(BF)
                    db = ds.astype(BF)
                    dvs.append(dg(pb, dm[h], NN))
                    dks.append(dg(db, qm[h], NN))
                    dqs.append(dg(kt[64 * h : 64 * h + 64, rows], db, NN))
                dva[rows, cs] += dvs[0] + dvs[1]
                dka[rows, cs] += dks[0] + dks[1]
                dq = jnp.concatenate(dqs, axis=0)
                if first:
                    dqa[cs, :] = dq
                else:
                    dqa[cs, :] += dq

        low = lo_ref[i]
        rest = jnp.maximum(i - low - 1, 0)
        pl.when(low < i)(lambda: block(i - 1, 2, True))
        pl.when(low == i)(lambda: block(i, 1, True))

        def step(t, c):
            block(low + 2 * t, 2, False)
            return c

        lax.fori_loop(0, rest // 2, step, 0)
        pl.when(rest % 2 == 1)(lambda: block(i - 2, 1, False))
        for p in range(heads // 2):
            cs = slice(128 * p, 128 * p + 128)
            out_ref[pl.ds(qs, B), cs] = (dqa[cs, :] * 0.125).T.astype(BF)
        return 0

    lax.fori_loop(0, n, qblock, 0)

    def finish(i, _):
        s = pl.ds(pl.multiple_of(i * B, B), B)
        out_ref[s, wide : 2 * wide] = dka[s, :].astype(BF)
        out_ref[s, 2 * wide :] = dva[s, :].astype(BF)
        return 0

    lax.fori_loop(0, n, finish, 0)


def attn_bwd(place, lo, start, q, k, v, atts, lses, own, got, deps):
    n, w = q.shape
    heads = w // HD
    return pl.pallas_call(
        functools.partial(bwd_kernel, heads=heads),
        out_shape=jax.ShapeDtypeStruct((n, 3 * w), BF),
        in_specs=[SM] * 2 + [VM] * 10 + [ANY] * len(deps),
        out_specs=VM,
        scratch_shapes=[
            pltpu.VMEM((heads, B, 128), BF),
            pltpu.VMEM((heads, B, 128), BF),
            pltpu.VMEM((w, B), F32),
            pltpu.VMEM((n, w), F32),
            pltpu.VMEM((n, w), F32),
            pltpu.VMEM((8, B), F32),
            pltpu.VMEM((w, n), BF),
        ],
        compiler_params=pltpu.CompilerParams(vmem_limit_bytes=56 * 2**20),
        cost_estimate=cost(42_000_000_000),
        name="attn_bwd",
    )(place, lo, start, q, k, v, *atts, *lses, own, got, *deps)


def qkv_bwd_kernel(place, mixed, normed, w_ref, *refs):
    e_own, e_send, qg, sums = refs[-4:]
    c = place[1]
    count = e_own.shape[0]
    wide = sums.shape[1]
    step = min(512, count)
    sums[...] = jnp.zeros_like(sums)

    def push(m, _):
        s = pl.ds(pl.multiple_of(m * step, step), step)
        far = pl.ds(pl.multiple_of((1 - c) * count + m * step, step), step)
        own = pl.ds(pl.multiple_of(c * count + m * step, step), step)
        for rows in (far, own):
            sums[0:1, :] += jnp.sum(mixed[rows, :wide].astype(F32), axis=0, keepdims=True)
            sums[1:2, :] += jnp.sum(mixed[rows, 2 * wide :].astype(F32), axis=0, keepdims=True)
        e_send[s, :] = dg(mixed[far, :], w_ref[...], NT).astype(BF)
        e_own[s, :] = dg(mixed[own, :], w_ref[...], NT)
        return 0

    lax.fori_loop(0, count // step, push, 0)
    for at in range(0, 3 * wide, 256):
        cols = slice(at, min(at + 256, 3 * wide))
        grad = dg(normed[...], mixed[:, cols], TN).astype(BF)
        qg[:, :, cols] = grad.reshape(qg.shape[0], qg.shape[1], -1)


def qkv_bwd(place, mixed, normed, w_qkv, deps):
    n, d = normed.shape
    w = mixed.shape[1] // 3
    return pl.pallas_call(
        qkv_bwd_kernel,
        out_shape=(
            jax.ShapeDtypeStruct((n // 2, d), F32),
            jax.ShapeDtypeStruct((n // 2, d), BF),
            jax.ShapeDtypeStruct((4, d // 4, 3 * w), BF),
            jax.ShapeDtypeStruct((8, w), F32),
        ),
        in_specs=[SM] + [VM] * 3 + [ANY] * len(deps),
        out_specs=[VM] * 4,
        compiler_params=pltpu.CompilerParams(vmem_limit_bytes=40 * 2**20),
        cost_estimate=cost(1_000_000_000),
        name="qkv_bwd",
    )(place, mixed, normed, w_qkv, *deps)


def last_kernel(place, e_own, e_got, x_ref, mg_ref, vecs, f_sums, d_sums, out, vec, sums):
    step = pl.program_id(0)

    @pl.when(step == 0)
    def _():
        sums[...] = jnp.zeros_like(sums)
        vec[...] = jnp.zeros_like(vec)

    e = e_own[...] + e_got[...].astype(F32)
    xhat, inv = norm_tile(x_ref[0].astype(F32))
    ce = e * vecs[2:3, :]
    grad = mg_ref[...] + inv * (
        ce
        - jnp.mean(ce, axis=-1, keepdims=True)
        - xhat * jnp.mean(ce * xhat, axis=-1, keepdims=True)
    )
    out[0] = grad.astype(BF)
    sums[3:4, :] += jnp.sum(e * xhat, axis=0, keepdims=True)
    sums[4:5, :] += jnp.sum(e, axis=0, keepdims=True)

    @pl.when(step == pl.num_programs(0) - 1)
    def _():
        half = d_sums.shape[1]
        for core in range(2):

            @pl.when(place[1] == core)
            def _(core=core):
                sums[0:2, core * half : core * half + half] = d_sums[0:2, :]

        sums[2:3, :] = f_sums[0:1, :]
        sums[5:8, :] = f_sums[1:4, :]
        parts = vec.shape[0]
        blk = sums.shape[1] // parts
        for p in range(parts):
            vec[p, 0:8, 0:blk] = sums[:, p * blk : p * blk + blk]
            for t in range(parts):
                vec[p, 8 + t : 9 + t, 0:blk] = f_sums[8 + p : 9 + p, t * blk : t * blk + blk]


def last_norm(place, e_own, e_got, tok, mg, vecs, f_sums, d_sums, lanes):
    n, w = e_own.shape
    count = n // 2
    step = 256
    per = count // step
    flat = pl.BlockSpec((step, w), lambda i: (i, 0))
    block = pl.BlockSpec((1, step, w), lambda i: (i // per, i % per, 0))
    return pl.pallas_call(
        last_kernel,
        grid=(n // step,),
        out_shape=(
            jax.ShapeDtypeStruct((2, count, w), BF),
            jax.ShapeDtypeStruct((4, 16, lanes), F32),
        ),
        in_specs=[SM, flat, flat, block, flat]
        + [pl.BlockSpec(x.shape, lambda i: (0, 0)) for x in (vecs, f_sums, d_sums)],
        out_specs=[block, pl.BlockSpec((4, 16, lanes), lambda i: (0, 0, 0))],
        scratch_shapes=[pltpu.VMEM((8, w), F32)],
        compiler_params=pltpu.CompilerParams(vmem_limit_bytes=16 * 2**20),
        cost_estimate=cost(400_000_000),
        name="last_norm",
    )(place, e_own, e_got, tok, mg, vecs, f_sums, d_sums)


def message_kernel(place, keep, got, out_x, out_y, kept, gave, sems):
    half = kept.shape[1]
    loads, stores = [], []
    for t, (r, row) in enumerate(((3, 1), (1, 1), (3, 0), (2, 0))):
        src = place[0] ^ r
        rows = slice(row * half, row * half + half)
        loads.append(
            (
                pltpu.make_async_copy(keep.at[src, rows], kept.at[t], sems.at[t]),
                pltpu.make_async_copy(got.at[src, rows], gave.at[t], sems.at[4 + t]),
            )
        )
        for copy in loads[-1]:
            copy.start()
    for t in range(4):
        for copy in loads[t]:
            copy.wait()
        kept[t] = (kept[t].astype(F32) + gave[t].astype(F32)).astype(BF)
        dst = (out_x, out_y)[t // 2].at[(t % 2) * half : (t % 2) * half + half]
        stores.append(pltpu.make_async_copy(kept.at[t], dst, sems.at[8 + t]))
        stores[-1].start()
    for copy in stores:
        copy.wait()


def first_messages(place, keep, got):
    _, rows, w = keep.shape
    message = jax.ShapeDtypeStruct((rows, w), BF)
    return pl.pallas_call(
        message_kernel,
        in_specs=[SM, ANY, ANY],
        out_specs=[ANY, ANY],
        out_shape=(message, message),
        scratch_shapes=[pltpu.VMEM((4, rows // 2, w), BF)] * 2 + [pltpu.SemaphoreType.DMA((12,))],
        compiler_params=pltpu.CompilerParams(vmem_limit_bytes=56 * 2**20),
        cost_estimate=cost(400_000_000),
        name="first_messages",
    )(place, keep, got)


def vector_kernel(rows_ref, lane_at, row_at, out):
    count, lanes = rows_ref.shape
    width = out.shape[1]
    lane = lax.broadcasted_iota(jnp.int32, (lanes, width), 0)
    row = lax.broadcasted_iota(jnp.int32, (count, width), 0)
    for k in range(out.shape[0]):
        choose = jnp.where(lane == lane_at[k : k + 1, :], 1.0, 0.0).astype(BF)
        spread = dg(rows_ref[...], choose, NN)
        kept = jnp.where(row == row_at[k : k + 1, :], spread, 0.0)
        out[k : k + 1, :] = jnp.sum(kept, axis=0, keepdims=True)


def vector_rows(spread, rows, ff_rows, which, width):
    n = np.arange(width)
    lane_at, row_at = np.full((8, width), -1), np.full((8, width), -1)
    for i, k in enumerate(which):
        size, at = (rows, n) if k < 8 else (ff_rows, n + (k - 8) * width)
        lane_at[i] = (k if k < 8 else 8) * rows + at % size
        row_at[i] = at // size
    return pl.pallas_call(
        vector_kernel,
        out_shape=jax.ShapeDtypeStruct((8, width), F32),
        in_specs=[VM] * 3,
        out_specs=VM,
        compiler_params=pltpu.CompilerParams(vmem_limit_bytes=16 * 2**20),
        cost_estimate=cost(400_000_000),
        name="vectors",
    )(spread, jnp.asarray(lane_at, jnp.int32), jnp.asarray(row_at, jnp.int32))


def qkv_kernel(place, w0, w1, w2, w3a, w3b, own, far, vecs, *refs):
    normed, q_ref, k_ref, v_ref, w, sems = refs[-6:]
    q, c = place[0], place[1]
    blk = w.shape[0] // 4
    half = w.shape[1] // 3
    copies = []

    def add(src, rows, r, offset, part):
        start = pl.multiple_of((q ^ r) * blk + offset, 16)
        size = rows.stop - rows.start
        copies.append(
            pltpu.make_async_copy(
                src.at[rows],
                w.at[pl.ds(start, size), part * half : part * half + half],
                sems.at[len(copies)],
            )
        )

    for r, src in enumerate((w0, w1, w2)):
        for part in range(3):
            add(src, slice(part * blk, part * blk + blk), r, 0, part)
    cut = blk // 2
    add(w3a, slice(0, blk), 3, 0, 0)
    add(w3a, slice(blk, blk + cut), 3, 0, 1)
    add(w3b, slice(0, cut), 3, cut, 1)
    add(w3b, slice(cut, cut + blk), 3, 0, 2)
    for copy in copies:
        copy.start()
    for copy in copies:
        copy.wait()
    count = q_ref.shape[0] // 2
    per = count // TILE // 2
    q_bias = jnp.where(c == 0, vecs[0:1, :half], vecs[0:1, half:])
    v_bias = jnp.where(c == 0, vecs[1:2, :half], vecs[1:2, half:])

    for k, ref in enumerate((own, far)):
        base = (c if k == 0 else 1 - c) * count

        def tile(m, _, ref=ref, base=base):
            x = ref[m // per, pl.ds(pl.multiple_of((m % per) * TILE, TILE), TILE), :].astype(F32)
            xhat, _inv = norm_tile(x)
            y = (xhat * vecs[2:3, :] + vecs[3:4, :]).astype(BF)
            s = pl.ds(pl.multiple_of(base + m * TILE, TILE), TILE)
            normed[s, :] = y
            mixed = dg(y, w[...], NN)
            q_ref[s, :] = (mixed[:, :half] + q_bias).astype(BF) * BF(0.125)
            k_ref[s, :] = mixed[:, half : 2 * half].astype(BF)
            v_ref[s, :] = (mixed[:, 2 * half :] + v_bias).astype(BF)
            return 0

        lax.fori_loop(0, 2 * per, tile, 0)


def qkv_apply(place, weights, own, far, vecs, deps):
    width = own.shape[2]
    half = width // 2
    n = 4 * (own.shape[1] - SEG_ROWS)
    part = jax.ShapeDtypeStruct((n, half), BF)
    return pl.pallas_call(
        qkv_kernel,
        out_shape=(
            jax.ShapeDtypeStruct((n, width), BF),
            part,
            part,
            part,
            jax.ShapeDtypeStruct((width, 3 * half), BF),
        ),
        in_specs=[SM] + [ANY] * 5 + [VM] * 3 + [ANY] * len(deps),
        out_specs=[VM] * 5,
        scratch_shapes=[pltpu.SemaphoreType.DMA((13,))],
        compiler_params=pltpu.CompilerParams(vmem_limit_bytes=32 * 2**20),
        cost_estimate=cost(400_000_000),
        name="qkv",
    )(place, *weights, own, far, vecs, *deps)


GELU_A = 0.7978845608028654
GELU_B = 0.7978845608028654 * 0.044715


PIECES = 10


def load_parts(place, pieces, att_refs, w_con, w_exp, w_proj, att, sems):
    q, c = place[0], place[1]
    blk = w_proj.shape[1] // 4
    n_con = w_con.shape[1] // 4
    top = n_con + blk
    for core in range(2):

        @pl.when(c == core)
        def _(core=core):
            pltpu.make_async_copy(att_refs[core], att.at[core], sems.at[1]).start()
            pltpu.make_async_copy(att_refs[2], att.at[1 - core], sems.at[1]).start()

    def each(action):
        for r in range(4):
            rows = pl.ds(pl.multiple_of((q ^ r) * blk, blk), blk)
            con_rows = pl.ds(pl.multiple_of((q ^ r) * n_con, n_con), n_con)
            for k in range(2):
                a_ref = pieces[5 * k + r]
                b_ref, b_at = (a_ref, top) if r < 3 else (pieces[5 * k + 4], 0)
                action(q ^ r, c if k == 0 else 1 - c, a_ref, b_ref, b_at, rows, con_rows)

    def proj(src_q, side, a_ref, b_ref, b_at, rows, con_rows):
        pltpu.make_async_copy(a_ref.at[n_con:top], w_proj.at[side, rows], sems.at[0]).start()

    def expand(b, src_q, side, a_ref, b_ref, b_at, rows, con_rows):
        src = b_ref.at[b_at + b * blk : b_at + b * blk + blk]
        pltpu.make_async_copy(src, w_exp.at[b, side, rows], sems.at[2 + b]).start()

    def contract(src_q, side, a_ref, b_ref, b_at, rows, con_rows):
        dst = w_con.at[side, con_rows]
        pltpu.make_async_copy(a_ref.at[0:n_con], dst, sems.at[6 + src_q]).start()

    each(proj)
    each(functools.partial(expand, 0))
    each(contract)
    for b in range(1, w_exp.shape[0]):
        each(functools.partial(expand, b))


def pair(ref, *at):
    return jnp.concatenate([ref[(*at[:-1], 0, at[-1])], ref[(*at[:-1], 1, at[-1])]], axis=1)


def wait_for(ref, sem):
    pltpu.make_async_copy(ref, ref, sem).wait()


def ffn_fwd_kernel(place, *refs):
    pieces, att_refs, rest = refs[:PIECES], refs[PIECES : PIECES + 3], refs[PIECES + 3 :]
    tok, vecs = rest[:2]
    *outs, mid_out, n2_out, w_con, w_exp, w_proj, att, acc, mid, n2, res, sems, osem = refs[-14:]
    load_parts(place, pieces, att_refs, w_con, w_exp, w_proj, att, sems)
    wide = w_proj.shape[1]
    tiles = mid.shape[0] // TILE
    per = tiles // 2
    wait_for(w_proj, sems.at[0])
    wait_for(att, sems.at[1])

    def first(m, _):
        s = pl.ds(pl.multiple_of(m * TILE, TILE), TILE)
        x = tok[m // per, pl.ds(pl.multiple_of((m % per) * TILE, TILE), TILE), :]
        v = x.astype(F32) + (dg(pair(att, s), pair(w_proj, slice(None)), NN) + vecs[0:1, :])
        mid[s, :] = v
        xhat, _inv = norm_tile(v)
        n2[s, :] = (xhat * vecs[1:2, :] + vecs[2:3, :]).astype(BF)
        pltpu.make_async_copy(mid.at[s], mid_out.at[s], osem.at[0]).start()
        pltpu.make_async_copy(n2.at[s], n2_out.at[s], osem.at[1]).start()
        return 0

    lax.fori_loop(0, tiles, first, 0)
    for b in range(4):
        wait_for(w_exp.at[b], sems.at[2 + b])
        wait_for(w_con.at[:, b * wide : b * wide + wide], sems.at[6 + b])

    def second(m, _):
        s = pl.ds(pl.multiple_of(m * TILE, TILE), TILE)
        x = n2[s, :]
        for b in range(w_exp.shape[0]):
            h = dg(x, pair(w_exp, b, slice(None)), NN) + vecs[4 + b : 5 + b, :]
            th = jnp.tanh(h * (GELU_A + GELU_B * (h * h)))
            act = (h * (0.5 + 0.5 * th)).astype(BF)
            part = dg(act, pair(w_con, slice(b * wide, b * wide + wide)), NN)
            if b == 0:
                acc[...] = part
            else:
                acc[...] += part
        res[s, :] = (mid[s, :] + (acc[...] + vecs[3:4, :])).astype(BF)
        rows = pl.ds(pl.multiple_of((m % per) * TILE, TILE), TILE)
        for p in range(2):

            @pl.when((m // per) ^ (place[0] % 2) == p)
            def _(p=p):
                pltpu.make_async_copy(res.at[s], outs[p].at[rows], osem.at[2]).start()

        return 0

    lax.fori_loop(0, tiles, second, 0)
    wait_for(mid, osem.at[0])
    wait_for(n2, osem.at[1])
    wait_for(res, osem.at[2])


def ffn_bwd_kernel(place, *refs):
    pieces, att_refs, rest = refs[:PIECES], refs[PIECES : PIECES + 3], refs[PIECES + 3 :]
    g_send, g_got0, g_got1, mid_ref, n2, vecs = rest[:6]
    (
        keep, send, mgrad, ag_own, ag_send, sums,
        w_con, w_exp, w_proj, att, g, mid, act, hg, n2g, dc, de, agr, sems, osems,
    ) = refs[-20:]
    c = place[1]
    load_parts(place, pieces, att_refs, w_con, w_exp, w_proj, att, sems)
    wide = w_proj.shape[1]
    half = wide // 2
    blk = wide // 4
    blocks = w_exp.shape[0]
    tiles = n2.shape[0] // TILE
    sums[...] = jnp.zeros_like(sums)
    odd = place[0] % 2
    count = g_got0.shape[0]

    def fetch(ref, block):
        dst = g.at[pl.ds(pl.multiple_of(block * count, count), count)]
        pltpu.make_async_copy(ref, dst, sems.at[10]).start()

    pl.when(c == place[0] // 2)(functools.partial(fetch, g_send, odd))
    pl.when(c != place[0] // 2)(functools.partial(fetch, g_got0, odd))
    fetch(g_got1, 1 - odd)
    pltpu.make_async_copy(mid_ref, mid, sems.at[11]).start()
    wait_for(g, sems.at[10])

    def store(k, b):
        side = c if k % 2 == 0 else 1 - c
        if k < 2:
            src, dst = dc.at[side], (keep, send)[k].at[b, 0:wide]
        else:
            rows = pl.ds(pl.multiple_of(wide + blk + b * blk, blk), blk)
            src, dst = de.at[side], (keep, send)[k - 2].at[:, rows]
        return pltpu.make_async_copy(src, dst, osems.at[k])

    def put(ref, t, value):
        value = value.astype(BF).reshape(ref.shape[1:-1] + (256,))
        at = t * 256
        if at < half:
            ref[0, ..., at : min(at + 256, half)] = value[..., : half - at]
        if at + 256 > half:
            ref[1, ..., max(at - half, 0) : at + 256 - half] = value[..., max(half - at, 0) :]

    def block(b, _):
        con_rows = pl.ds(pl.multiple_of(b * wide, wide), wide)
        wait_for(w_exp.at[b], sems.at[2 + b])
        wait_for(w_con.at[:, con_rows], sems.at[6 + b])
        bias = vecs[pl.ds(4 + b, 1), :]

        def tile(m, _):
            s = pl.ds(pl.multiple_of(m * TILE, TILE), TILE)
            w_e = pair(w_exp, b, slice(None))
            h = dg(n2[s, :], w_e, NN) + bias
            h2 = h * h
            t1 = 0.5 + 0.5 * jnp.tanh(h * (GELU_A + GELU_B * h2))
            ac = h * t1
            act[s, :] = ac.astype(BF)
            slope = t1 + ac * (1.0 - t1) * (2 * GELU_A + 6 * GELU_B * h2)
            hid = (dg(g[s, :], pair(w_con, con_rows), NT) * slope).astype(BF)
            hg[s, :] = hid
            sums[pl.ds(8 + b, 1), :] += jnp.sum(hid.astype(F32), axis=0, keepdims=True)
            part = dg(hid, w_e, NT)
            n2g[s, :] = jnp.where(b == 0, part, n2g[s, :] + part)
            return 0

        lax.fori_loop(0, tiles, tile, 0)

        @pl.when(b > 0)
        def _():
            for k in range(4):
                store(k, b - 1).wait()

        for t in range(3):
            cols = slice(t * 256, t * 256 + 256)
            put(dc, t, dg(act[...], g[:, cols], TN))
        for k in range(2):
            store(k, b).start()
        for t in range(3):
            cols = slice(t * 256, t * 256 + 256)
            put(de, t, dg(n2[...], hg[:, cols], TN))
        for k in range(2, 4):
            store(k, b).start()
        return 0

    lax.fori_loop(0, blocks, block, 0)
    wait_for(w_proj, sems.at[0])
    wait_for(att, sems.at[1])
    wait_for(mid, sems.at[11])

    def last(m, _):
        s = pl.ds(pl.multiple_of(m * TILE, TILE), TILE)
        xhat, inv = norm_tile(mid[s, :])
        e = n2g[s, :]
        g32 = g[s, :].astype(F32)
        ce = e * vecs[1:2, :]
        mg = g32 + inv * (
            ce
            - jnp.mean(ce, axis=-1, keepdims=True)
            - xhat * jnp.mean(ce * xhat, axis=-1, keepdims=True)
        )
        mid[s, :] = mg
        pltpu.make_async_copy(mid.at[s], mgrad.at[s], osems.at[4]).start()
        branch = mg.astype(BF)
        hg[s, :] = branch
        sums[0:1, :] += jnp.sum(branch.astype(F32), axis=0, keepdims=True)
        sums[1:2, :] += jnp.sum(e * xhat, axis=0, keepdims=True)
        sums[2:3, :] += jnp.sum(e, axis=0, keepdims=True)
        sums[3:4, :] += jnp.sum(g32, axis=0, keepdims=True)
        grad = dg(branch, pair(w_proj, slice(None)), NT).astype(BF)
        agr[0, s, :] = grad[:, :half]
        agr[1, s, :] = grad[:, half:]
        return 0

    lax.fori_loop(0, tiles, last, 0)
    for k in range(4):
        store(k, blocks - 1).wait()
    ends = [
        pltpu.make_async_copy(agr.at[c], ag_own, osems.at[0]),
        pltpu.make_async_copy(agr.at[1 - c], ag_send, osems.at[1]),
        pltpu.make_async_copy(de.at[c], keep.at[:, wide : wide + blk], osems.at[2]),
        pltpu.make_async_copy(de.at[1 - c], send.at[:, wide : wide + blk], osems.at[3]),
    ]
    for copy in ends[:2]:
        copy.start()
    for t in range(3):
        cols = slice(t * 256, t * 256 + 256)
        put(de, t, dg(pair(att, slice(None)), hg[:, cols], TN))
    for copy in ends[2:]:
        copy.start()
    for copy in ends:
        copy.wait()
    wait_for(mid, osems.at[4])


def ffn_fwd(place, pieces, atts, tok, vecs, deps):
    n, w = atts[2].shape[0], tok.shape[2]
    ff = 4 * pieces[4].shape[0]
    return pl.pallas_call(
        ffn_fwd_kernel,
        out_shape=(
            jax.ShapeDtypeStruct((n // 2, w), BF),
            jax.ShapeDtypeStruct((n // 2, w), BF),
            jax.ShapeDtypeStruct((n, w), F32),
            jax.ShapeDtypeStruct((n, w), BF),
        ),
        in_specs=[SM] + [ANY] * (PIECES + 3) + [VM] * 2 + [ANY] * len(deps),
        out_specs=[ANY] * 4,
        scratch_shapes=[
            pltpu.VMEM((2, ff, w // 2), BF),
            pltpu.VMEM((ff // w, 2, w, w // 2), BF),
            pltpu.VMEM((2, w, w // 2), BF),
            pltpu.VMEM((2, n, w // 2), BF),
            pltpu.VMEM((TILE, w), F32),
            pltpu.VMEM((n, w), F32),
            pltpu.VMEM((n, w), BF),
            pltpu.VMEM((n, w), BF),
            pltpu.SemaphoreType.DMA((10,)),
            pltpu.SemaphoreType.DMA((3,)),
        ],
        compiler_params=pltpu.CompilerParams(vmem_limit_bytes=60 * 2**20),
        cost_estimate=cost(12_000_000_000),
        name="ffn_fwd",
    )(place, *pieces, *atts, tok, vecs, *deps)


def ffn_bwd(place, pieces, atts, cots, mid, n2, vecs, deps):
    n, w = n2.shape
    half = w // 2
    ff = 4 * pieces[4].shape[0]
    pack = jax.ShapeDtypeStruct((4,) + pieces[0].shape, BF)
    cut = jax.ShapeDtypeStruct((n, half), BF)
    return pl.pallas_call(
        ffn_bwd_kernel,
        out_shape=(
            pack, pack,
            jax.ShapeDtypeStruct((n, w), F32),
            cut, cut,
            jax.ShapeDtypeStruct((16, w), F32),
        ),
        in_specs=[SM] + [ANY] * (PIECES + 3 + 4) + [VM] * 2 + [ANY] * len(deps),
        out_specs=[ANY] * 5 + [VM],
        scratch_shapes=[
            pltpu.VMEM((2, ff, w // 2), BF),
            pltpu.VMEM((ff // w, 2, w, w // 2), BF),
            pltpu.VMEM((2, w, w // 2), BF),
            pltpu.VMEM((2, n, w // 2), BF),
            pltpu.VMEM((n, w), BF),
            pltpu.VMEM((n, w), F32),
            pltpu.VMEM((n, w), BF),
            pltpu.VMEM((n, w), BF),
            pltpu.VMEM((n, w), F32),
            pltpu.VMEM((2, w, half), BF),
            pltpu.VMEM((2, 4, w // 4, half), BF),
            pltpu.VMEM((2, n, half), BF),
            pltpu.SemaphoreType.DMA((12,)),
            pltpu.SemaphoreType.DMA((5,)),
        ],
        compiler_params=pltpu.CompilerParams(vmem_limit_bytes=60 * 2**20),
        cost_estimate=cost(32_000_000_000),
        name="ffn_bwd",
    )(place, *pieces, *atts, *cots, mid, n2, vecs, *deps)


def pick(array, index, axis=0):
    return lax.dynamic_index_in_dim(array, index, axis, keepdims=False)


def ordered(flag, first, second, axis):
    return jnp.stack(
        [jnp.where(flag == 1, second, first), jnp.where(flag == 1, first, second)], axis
    )


def tie(values, *others):
    return lax.optimization_barrier((values, others))[0]


class Net:
    def __init__(self):
        self.nq = lax.axis_size("seq")
        self.nf = lax.axis_size("fsdp")
        self.q = lax.axis_index("seq")
        f = lax.axis_index("fsdp")
        self.z = f // 2
        self.c = f % 2
        self.bits = (self.nf // 2).bit_length() - 1

    def permute(self, value, target):
        pairs = []
        for q in range(self.nq):
            for f in range(self.nf):
                tq, tf = target(q, f)
                pairs.append((q * self.nf + f, tq * self.nf + tf))
        return lax.ppermute(value, ALL, pairs)

    def flip_q(self, value, mask):
        return self.permute(value, lambda q, f: (q ^ mask, f))

    def flip_f(self, value, mask):
        return self.permute(value, lambda q, f: (q, f ^ mask))

    def swap(self, value):
        return self.flip_f(value, 1)

    def _token_target(self, p):
        return lambda q, f: (2 * (f % 2) + (p ^ (q % 2)), (f // 2) * 2 + q // 2)

    def _route(self, value, target):
        pairs = []
        for q in range(self.nq):
            for f in range(self.nf):
                tq, tf = target(q, f)
                if (tq, tf) != (q, f):
                    pairs.append((q * self.nf + f, tq * self.nf + tf))
        return lax.ppermute(value, ALL, pairs)

    def token_sends(self, parts):
        return [jnp.where(self.q % 2 == p, parts[0], parts[1]) for p in range(2)]

    def to_chip(self, sends):
        return [self._route(sends[p], self._token_target(p)) for p in range(2)]

    def from_chip(self, sends):
        got = []
        for p in range(2):
            forward = self._token_target(p)
            back = {}
            for q in range(self.nq):
                for f in range(self.nf):
                    back[forward(q, f)] = (q, f)
            got.append(self._route(sends[p], lambda q, f, b=back: b[(q, f)]))
        return got

    def settle(self, sends, got):
        first = jnp.where(self.c == self.q // 2, sends[0], got[0])
        return ordered(self.q % 2, first, got[1], 0)

    def gather_z(self, block):
        return [block] + [self.flip_f(block, 2 * m) for m in range(1, self.nf // 2)]

    def by_z(self, blocks):
        for bit in range(self.bits):
            flag = (self.z >> bit) & 1 == 1
            blocks = [jnp.where(flag, blocks[i ^ (1 << bit)], x) for i, x in enumerate(blocks)]
        return jnp.stack(blocks)

    def scatter_z(self, blocks, gate=()):
        shape = blocks.shape[1:]
        for bit in range(self.bits):
            parts = blocks.reshape((-1, 2) + shape)
            mine = (self.z >> bit) & 1
            got = self.flip_f(pick(parts, 1 - mine, 1).astype(BF), 2 << bit)
            if bit == 0:
                got = tie(got, gate)
            blocks = pick(parts, mine, 1).astype(F32) + got.astype(F32)
        return blocks[0]

    def absolute(self, r0, r1, r2, r3):
        odd, high = self.q % 2 == 1, self.q // 2 == 1
        x0, x1 = jnp.where(odd, r1, r0), jnp.where(odd, r0, r1)
        x2, x3 = jnp.where(odd, r3, r2), jnp.where(odd, r2, r3)
        return jnp.stack(
            [
                jnp.where(high, x2, x0),
                jnp.where(high, x3, x1),
                jnp.where(high, x0, x2),
                jnp.where(high, x1, x3),
            ]
        )

    def scatter_one(self, term, cut):
        return [
            jnp.concatenate([term(3)[cut:], term(1)[cut:]]).astype(BF),
            jnp.concatenate([term(3)[:cut], term(2)[:cut]]).astype(BF),
        ]

    def scatter_two(self, term, cut, sends, gate):
        got = tie([self.flip_q(sends[0], 1), self.flip_q(sends[1], 2)], gate)
        rest = sends[0].shape[0] // 2
        more = [
            (term(1)[:cut] + got[1][:cut].astype(F32)).astype(BF),
            (term(2)[cut:] + got[0][:rest].astype(F32)).astype(BF),
        ]
        return got, more

    def scatter_three(self, term, cut, got, more):
        last = [self.flip_q(more[0], 1), self.flip_q(more[1], 2)]
        rest = got[0].shape[0] // 2
        return (
            term(0)[:cut] + got[1][cut:].astype(F32) + last[0].astype(F32),
            term(0)[cut:] + got[0][rest:].astype(F32) + last[1].astype(F32),
        )


def body(
    tokens,
    segments,
    qkv_weight,
    query_bias,
    value_bias,
    proj_weight,
    proj_bias,
    attn_gain,
    attn_shift,
    ffn_gain,
    ffn_shift,
    expand_weight,
    expand_bias,
    contract_weight,
    contract_bias,
    cotangent,
):
    net = Net()
    c, z = net.c, net.z
    micro, local, width = tokens.shape
    rows = qkv_weight.shape[0]
    ff = expand_weight.shape[1]
    ff_rows = contract_weight.shape[0]
    ratio = ff // width
    half = width // 2
    nq, nz = net.nq, net.nf // 2
    blk = rows * net.nf
    n = 2 * micro * local
    mine = micro * local

    place = jnp.stack([net.q, c]).astype(jnp.int32)

    seg_rows = jnp.zeros((micro, SEG_ROWS, width), BF).at[:, 0, :local].set(segments.astype(BF))
    tok_send = jnp.concatenate([tokens, seg_rows], axis=1)
    tok_sends = net.token_sends([tok_send[0], tok_send[1]])
    tok_got = net.to_chip(tok_sends)
    tok = net.settle(tok_sends, tok_got)
    tok_far = net.swap(tok)
    seg = ordered(c, tok[:, local, :local], tok_far[:, local, :local], 0).reshape(n)
    seg = seg.astype(jnp.int32)
    docs = jnp.arange(32, dtype=jnp.int32)
    before = jnp.sum((seg[None, :] < docs[:, None]).astype(jnp.int32), axis=1)
    start = jnp.sum(jnp.where(seg[None, :] == docs[:, None], before[:, None], 0), axis=0)
    lo = start[::B] // B
    start = start.reshape(n // B, B)

    qkv_w, con_w, proj_w, exp_w, vector_args = tie(
        (
            qkv_weight,
            contract_weight,
            proj_weight,
            expand_weight,
            (
                query_bias,
                value_bias,
                proj_bias,
                attn_gain,
                attn_shift,
                ffn_gain,
                ffn_shift,
                contract_bias,
                expand_bias,
            ),
        ),
        tok_sends,
    )
    small_len = sum(x.shape[0] for x in vector_args)
    small, at = 0.0, 0
    for x in vector_args:
        small = small + jnp.pad(x.astype(F32), (at, half - at - x.shape[0]))
        at += x.shape[0]
    small = jnp.pad(small.astype(BF)[None], ((0, 7), (0, 0)))

    def columns(matrix, t, s):
        return matrix[:, t * width + s * half : t * width + (s + 1) * half]

    packs = [
        jnp.concatenate(
            [columns(qkv_w, t, s) for t in range(3)]
            + [small, columns(con_w, 0, s), columns(proj_w, 0, s)]
            + [columns(exp_w, t, s) for t in range(ratio)]
        )
        for s in range(2)
    ]
    pack = ordered(
        c,
        jnp.where(c == 0, packs[0], packs[1]),
        net.swap(jnp.where(c == 0, packs[1], packs[0])),
        0,
    )
    n_q = 3 * rows + 8
    pack_qs = net.gather_z(pack[:, :n_q])
    pack_q = net.by_z(tie(pack_qs, tok_got)).reshape(net.nf, n_q, half)
    part_q = jnp.concatenate(
        [pack_q[:, t * rows : (t + 1) * rows].reshape(blk, half) for t in range(3)]
        + [pack_q[:, 3 * rows]]
    )
    cut = 3 * blk // 2
    q1, q2 = net.flip_q(part_q, 1), net.flip_q(part_q, 2)
    q3_sends = q1[:cut], q2[cut:]
    q3a, q3b = net.flip_q(q3_sends[0], 2), net.flip_q(q3_sends[1], 1)
    n_con, n_proj = ratio * blk, blk
    top = n_con + n_proj
    pack_fs = net.gather_z(tie(pack[:, n_q:], pack_qs[1]))
    pack_f = net.by_z(tie(pack_fs, q3_sends))
    pack_f = pack_f.reshape(net.nf, -1, half)
    part_f = jnp.concatenate(
        [pack_f[:, :ff_rows].reshape(-1, half), pack_f[:, ff_rows : ff_rows + rows].reshape(-1, half)]
        + [
            pack_f[:, ff_rows + t * rows : ff_rows + (t + 1) * rows].reshape(-1, half)
            for t in range(1, ratio + 1)
        ]
    )
    part_f = tie(part_f, q3a, q3b)
    f1, f2 = net.flip_q(part_f, 1), net.flip_q(part_f, 2)
    f3_sends = f1[:top], f2[top:]

    spread = net.absolute(part_q[3 * blk :], q1[3 * blk :], q2[3 * blk :], q3b[3 * blk - cut :])
    spread = spread.reshape(nq * net.nf, half)
    norm_vecs = vector_rows(spread, rows, ff_rows, (0, 1, 3, 4), width)
    vecs = vector_rows(spread, rows, ff_rows, (2, 5, 6, 7, 8, 9, 10, 11), width)

    normed_all, query, key, value, w_qkv = qkv_apply(
        place,
        (part_q, q1, q2, q3a, q3b),
        tok,
        tok_far,
        norm_vecs,
        [part_f],
    )
    att0, lse0 = attn_fwd(lo, start, query, key, value, 0, [])
    att1, lse1 = attn_fwd(lo, start, query, key, value, 1, [*f3_sends, lse0])
    att_got = net.swap(jnp.where(c == 0, att1, att0))
    f3a, f3b = net.flip_q(f3_sends[0], 2), net.flip_q(f3_sends[1], 1)
    cot_sends = net.token_sends(tie((cotangent[0], cotangent[1]), f3a, f3b))
    pieces = [part_f, f1, f2, f3a, f3b]
    pieces = pieces + [net.swap(x) for x in pieces]
    atts = (att0, att1, att_got)

    *out_sends, middle, normed_two = ffn_fwd(place, pieces, atts, tok, vecs, cot_sends)
    out_got = net.from_chip(out_sends)

    cots = (cot_sends[0], *net.to_chip(cot_sends))
    keep, send, middle_grad, ag_own, ag_send, sums = ffn_bwd(
        place, pieces, atts, cots, middle, normed_two, vecs, out_sends
    )
    ag_send, send, out_got = tie((ag_send, send, out_got))
    result = net.settle(out_sends, out_got)
    ag_got = net.swap(ag_send)

    got = net.swap(send)
    packs = (keep, got)
    f_sends = first_messages(place, keep, got)
    d_mixed = attn_bwd(
        place, lo, start, query, key, value, atts[:2], (lse0, lse1), ag_own, ag_got, f_sends
    )
    f_x, f_y = tie((net.flip_q(f_sends[0], 1), net.flip_q(f_sends[1], 2)), d_mixed)
    cut_f = keep.shape[1] // 2

    def term(r, half_row):
        rows_of = slice(half_row * cut_f, half_row * cut_f + cut_f)
        return sum(pick(x, net.q ^ r)[rows_of].astype(F32) for x in packs)

    f_more = (
        (term(1, 0) + f_y[:cut_f].astype(F32)).astype(BF),
        (term(2, 1) + f_x[:cut_f].astype(F32)).astype(BF),
    )
    e_own, e_send, qkv_grad, d_sum = qkv_bwd(place, d_mixed, normed_all, w_qkv, f_more)

    e_got = net.swap(e_send)
    f_last = net.flip_q(f_more[0], 1), net.flip_q(f_more[1], 2)
    f_sum = jnp.concatenate(
        [
            term(0, 0) + f_y[cut_f:].astype(F32) + f_last[0].astype(F32),
            term(0, 1) + f_x[cut_f:].astype(F32) + f_last[1].astype(F32),
        ]
    )
    per_f = jnp.concatenate(
        [
            f_sum[:n_con].reshape(net.nf, ff_rows, half),
            f_sum[n_con:top].reshape(net.nf, rows, half),
        ]
        + [
            f_sum[top + t * blk : top + (t + 1) * blk].reshape(net.nf, rows, half)
            for t in range(ratio)
        ],
        axis=1,
    )
    e_own, per_f = tie((e_own, per_f))
    tok_grad, vec = last_norm(
        place, e_own, e_got, tok, middle_grad, norm_vecs, sums, d_sum, 3 * half
    )
    tg_sends = net.token_sends([tok_grad[0], tok_grad[1]])
    def q_term(r):
        return jnp.concatenate([pick(qkv_grad, net.q ^ r).astype(F32), pick(vec, net.q ^ r)])

    q_cut = (blk + 16) // 2
    q_sends = tie(net.scatter_one(q_term, q_cut), tg_sends)

    q_got, q_more = net.scatter_two(q_term, q_cut, q_sends, tg_sends)
    tg_sends = tie(tg_sends, q_more)
    token_grad = net.settle(tg_sends, net.from_chip(tg_sends))
    q_sum = jnp.concatenate(net.scatter_three(q_term, q_cut, q_got, q_more))
    q_rows, vec = q_sum[:blk].reshape(nz, 2 * rows, 3 * half), q_sum[blk:]

    def split(bit):
        parts = q_rows.reshape(-1, 2, 2 * rows, 3 * half)
        side = (z >> bit) & 1
        away = pick(parts, 1 - side, 1).reshape(-1, 3 * half)
        return pick(parts, side, 1), jnp.concatenate([away, vec]).astype(BF)

    q_kept, q_away = split(0)
    per_core = net.scatter_z(per_f.reshape(nz, 2, -1, half), q_away)
    final = ordered(c, pick(per_core, c), net.swap(pick(per_core, 1 - c)), 0)
    con_out = jnp.concatenate([final[0, :ff_rows], final[1, :ff_rows]], axis=1)
    proj_out = jnp.concatenate(
        [final[0, ff_rows : ff_rows + rows], final[1, ff_rows : ff_rows + rows]], axis=1
    )
    exp_out = jnp.concatenate(
        [
            final[s, ff_rows + rows + t * rows : ff_rows + rows + (t + 1) * rows]
            for t in range(ratio)
            for s in range(2)
        ],
        axis=1,
    )
    for bit in range(net.bits):
        if bit:
            q_kept, q_away = split(bit)
        moved = net.flip_f(q_away, 2 << bit).astype(F32)
        count = moved.shape[0] - vec.shape[0]
        q_rows = q_kept + moved[:count].reshape(q_kept.shape)
        vec = vec + moved[count:]
    q_core = q_rows.reshape(2, rows, 3 * half)
    moved = net.swap(jnp.concatenate([pick(q_core, 1 - c), vec]))
    vec = vec[:, :blk] + moved[rows:, :blk]
    final = ordered(c, pick(q_core, c), moved[:rows], 0)
    qkv_out = jnp.concatenate(
        [final[s, :, t * half : (t + 1) * half] for t in range(3) for s in range(2)], axis=1
    )
    f = 2 * z + c
    outs = lax.dynamic_slice(vec, (0, f * rows), (8, rows))
    exp_off_out = lax.dynamic_slice(vec[8 : 8 + ratio].reshape(-1), (f * ff_rows,), (ff_rows,))
    return (
        result,
        token_grad,
        qkv_out,
        outs[0],
        outs[1],
        proj_out,
        outs[2],
        outs[3],
        outs[4],
        outs[5],
        outs[6],
        exp_out,
        exp_off_out,
        con_out,
        outs[7],
    )


def solution(mesh):
    act = P("fsdp", "seq", None)
    mat = P(ALL, None)
    vec = P(ALL)
    return jax.shard_map(
        body,
        mesh=mesh,
        in_specs=(
            act, P("fsdp", "seq"), mat, vec, vec, mat, vec, vec, vec, vec, vec, mat, vec, mat, vec, act,
        ),
        out_specs=(act, act, mat, vec, vec, mat, vec, vec, vec, vec, vec, mat, vec, mat, vec),
        check_vma=False,
    )
```
